128 devices in a mesh: dp: 8 (over x, core), tensor: 16 (over y, z).
Axes of the slice: x: 4, y: 4, z: 4, core: 2. Of those that a mesh axis runs over, the one named last changes fastest.
Arguments:
- tokens: bfloat16 [1536, 6144], P('dp', 'tensor'), may hold values from -6 to 6
- cotangent: bfloat16 [1536, 6144], P('dp', 'tensor'), may hold values from -6 to 6
- w1_blocks: bfloat16 [192, 15, 128, 128], P('tensor', None, 'dp'), may hold values from -0.125 to 0.125
- w1_rows: int32 [192, 15], replicated, may hold values from 0 to 47, all different within a row
- w1_scale: float32 [192, 15], replicated, may hold values from 0.5 to 2
- w2_blocks: bfloat16 [288, 15, 128, 128], P('tensor', None, 'dp'), may hold values from -0.0625 to 0.0625
- w2_cols: int32 [288, 15], replicated, may hold values from 0 to 47, all different within a row
- w2_scale: float32 [288, 15], replicated, may hold values from 0.5 to 2
- owner: int32 [192], replicated, may hold values from 0 to 15, as said below
Outputs:
- mixed: bfloat16 [1536, 6144], P('dp', 'tensor')
- input_grad: bfloat16 [1536, 6144], P('dp', 'tensor')
- grad_w1: bfloat16 [192, 15, 128, 128], P('tensor', None, 'dp')
- grad_w2: bfloat16 [288, 15, 128, 128], P('tensor', None, 'dp')
The draws below stay inside these ranges and needn't reach their ends.
Inputs may be any that keep to these rules, and one draw needn't show every extreme that they name: `owner`: hidden block g is computed from first-projection rows held on tensor index g // 12. Every tensor index owns at most 18 hidden blocks, and at most 2 of the hidden blocks of one tensor index are owned by one index; some index owns exactly 18 and some pair reaches 2 in every draw. `w1_rows`: each row names 15 different feature blocks. `w2_cols`: each row names 15 different feature blocks.
All inputs are finite; a program needn't handle non-finite values.
Results may differ from the reference program's by a relative error of at most 0.02.
Values may be sent and summed in bfloat16 or wider, within the bound.
A program may use at most 192 MiB of HBM per device.

```python
import math
import jax
import jax.numpy as jnp
from jax import lax

D = 6144
BLK = 128
K1 = 15
K2 = 15
TOK_DEV = 192
DB = 48
HB = 192
HB_DEV = 12
CAP = 18
SLOTS = 288
TOKENS = 1536
N_DP = 8
N_TENSOR = 16


def draw_owner(key, part):
    key = jax.random.fold_in(key, 11)
    first, second, third, fourth = jax.random.split(key, 4)
    half = N_TENSOR // 2
    moved = jax.random.randint(first, (half,), 0, CAP - HB_DEV + 1, dtype=jnp.int32)
    moved = moved.at[0].set(CAP - HB_DEV)
    loads = jnp.concatenate([HB_DEV + moved, HB_DEV - moved])
    bounds = jnp.cumsum(loads)
    position = jnp.arange(HB, dtype=jnp.int32)
    dest_pos = jnp.sum((position[:, None] >= bounds[None, :]).astype(jnp.int32), axis=1)
    src_pos = position % N_TENSOR
    within = position // N_TENSOR
    dest_perm = jax.random.permutation(second, N_TENSOR).astype(jnp.int32)
    src_perm = jax.random.permutation(third, N_TENSOR).astype(jnp.int32)
    scores = jax.random.randint(fourth, (N_TENSOR, HB_DEV), 0, 1 << 20, dtype=jnp.int32) * HB_DEV + jnp.arange(HB_DEV, dtype=jnp.int32)[None, :]
    local_perm = jnp.argsort(scores, axis=1).astype(jnp.int32)
    block = src_perm[src_pos] * HB_DEV + local_perm[src_pos, within]
    return jnp.zeros((HB,), jnp.int32).at[block].set(dest_perm[dest_pos])


def block_levels(own_key, extent, cuts, smallest, high):
    gain, own = 1.0, jax.random.fold_in(own_key, 6)
    for axis_at, blocks in cuts:
        steps = jnp.exp(jax.random.uniform(jax.random.fold_in(own, axis_at), (blocks,), jnp.float32, smallest / len(cuts), high / len(cuts)))
        gain = gain * jnp.repeat(steps, extent[axis_at] // blocks).reshape([-1 if axis == axis_at else 1 for axis in range(len(extent))])
    return gain


def choose_distinct(stream_key, rows, number_of, top, lift):
    ranking = jax.random.permutation(jax.random.fold_in(stream_key, 1), number_of)
    favour = ranking
    for power in range(3):
        favour = favour * favour // number_of
    favour = favour * lift // number_of
    lots = jax.random.randint(jax.random.fold_in(stream_key, 2), (rows, number_of), 0, 4096) + favour
    holders = jax.random.permutation(jax.random.fold_in(stream_key, 3), rows)[jnp.arange(number_of) % rows]
    lots = jnp.where(jnp.arange(rows)[:, None] == holders[None, :], 1 << 14, lots)
    score = lots * number_of + jnp.arange(number_of)
    return lax.top_k(score.astype(jnp.int32), top)[1].astype(jnp.int32)


def normal_values(stream_key, extent, deviation, reach, pieces=(), kind=jnp.bfloat16):
    drawn = deviation * jax.random.normal(stream_key, extent, jnp.float32)
    if pieces:
        drawn = drawn * block_levels(stream_key, extent, pieces, -0.22, 0.18)
    return jnp.clip(drawn, -reach, reach).astype(kind)


def setup_inputs(seed: int = 0) -> dict:
    seeds = jax.random.split(jax.random.key(seed), 10)
    tokens = normal_values(seeds[0], (TOKENS, D), 1.0, 6.0, ((0, 8), (1, 16)))
    cotangent = normal_values(seeds[1], (TOKENS, D), 1.0, 6.0, ((0, 8), (1, 16)))
    w1_blocks = normal_values(seeds[2], (HB, K1, BLK, BLK), (K1 * BLK) ** -0.5, 0.125, ((0, 16), (2, 8)))
    w1_rows = choose_distinct(seeds[3], HB, DB, K1, 0)
    w1_scale = jnp.clip(jnp.exp(jax.random.uniform(seeds[4], (HB, K1), jnp.float32, math.log(0.5), math.log(2.0))), 0.5, 2.0)
    w2_blocks = normal_values(seeds[5], (SLOTS, K2, BLK, BLK), (HB * K2 * BLK // DB) ** -0.5, 0.0625, ((0, 16), (2, 8)))
    w2_cols = choose_distinct(seeds[6], SLOTS, DB, K2, 0)
    w2_scale = jnp.clip(jnp.exp(jax.random.uniform(seeds[7], (SLOTS, K2), jnp.float32, math.log(0.5), math.log(2.0))), 0.5, 2.0)
    owner = draw_owner(jax.random.fold_in(seeds[9], 71), 0)
    return {"tokens": tokens, "cotangent": cotangent, "w1_blocks": w1_blocks, "w1_rows": w1_rows, "w1_scale": w1_scale, "w2_blocks": w2_blocks, "w2_cols": w2_cols, "w2_scale": w2_scale, "owner": owner}


GELU_C = 0.7978845608028654
GELU_A = 0.044715


def gelu_value(h):
    inner = GELU_C * (h + GELU_A * h * h * h)
    return 0.5 * h * (1.0 + jnp.tanh(inner))


def gelu_slope(h):
    inner = GELU_C * (h + GELU_A * h * h * h)
    tanh_val = jnp.tanh(inner)
    return 0.5 * (1.0 + tanh_val) + 0.5 * h * (1.0 - tanh_val * tanh_val) * GELU_C * (1.0 + 3.0 * GELU_A * h * h)


def route_tables(owner, per_dev):
    count = owner.shape[0]
    index = jnp.arange(count, dtype=jnp.int32)
    source = index // per_dev
    earlier = index[None, :] < index[:, None]
    same_dest = owner[None, :] == owner[:, None]
    same_src = source[None, :] == source[:, None]
    slot = jnp.sum((earlier & same_dest).astype(jnp.int32), axis=1).astype(jnp.int32)
    pair = jnp.sum((earlier & same_dest & same_src).astype(jnp.int32), axis=1).astype(jnp.int32)
    return source, slot, pair


def dequantize(values, scale):
    return (values.astype(jnp.float32) * scale[:, :, None, None]).astype(jnp.bfloat16)


def rounded_sum(terms):
    kept = lax.optimization_barrier(terms.astype(jnp.bfloat16)).astype(jnp.float32)
    return jnp.sum(kept, axis=0)


def reference(tokens, cotangent, w1_blocks, w1_rows, w1_scale, w2_blocks, w2_cols, w2_scale, owner):
    source, slot, pair = route_tables(owner, HB_DEV)
    where_two = (owner * CAP + slot).astype(jnp.int32)
    eff_one = dequantize(w1_blocks, w1_scale)
    eff_two = dequantize(w2_blocks, w2_scale)[where_two]
    cols_two = w2_cols[where_two]
    scale_two = w2_scale[where_two]
    x_cube = tokens.reshape(TOKENS, DB, BLK)
    dy_cube = cotangent.reshape(TOKENS, DB, BLK)
    start = (jnp.zeros((TOKENS, DB, BLK), jnp.float32), jnp.zeros((TOKENS, DB, BLK), jnp.float32), jnp.zeros((TOKENS, DB, BLK), jnp.float32))
    steps_in = (jnp.arange(HB, dtype=jnp.int32), w1_rows, eff_one, cols_two, eff_two, w1_scale, scale_two)

    def step(carry, inputs):
        y_acc, dx_total, dx_part = carry
        index, rows, weff_one, cols, weff_two, scale_one, scale_tw = inputs
        x_sel = x_cube[:, rows]
        pre = jnp.dot(x_sel.reshape(TOKENS, K1 * BLK), weff_one.reshape(K1 * BLK, BLK), preferred_element_type=jnp.float32)
        act = gelu_value(pre).astype(jnp.bfloat16)
        z_two = jnp.einsum("ti,bio->tbo", act.astype(jnp.float32), weff_two.astype(jnp.float32), precision=lax.Precision.HIGHEST)
        y_acc = y_acc.at[:, cols].add(z_two)
        dy_sel = dy_cube[:, cols]
        flipped = jnp.transpose(weff_two, (0, 2, 1)).reshape(K2 * BLK, BLK)
        d_act = jnp.dot(dy_sel.reshape(TOKENS, K2 * BLK), flipped, preferred_element_type=jnp.float32).astype(jnp.bfloat16)
        d_pre = (d_act.astype(jnp.float32) * gelu_slope(pre)).astype(jnp.bfloat16)
        terms_two = jnp.einsum("pti,ptbo->pbio", act.reshape(N_DP, TOK_DEV, BLK).astype(jnp.float32), dy_sel.reshape(N_DP, TOK_DEV, K2, BLK).astype(jnp.float32), precision=lax.Precision.HIGHEST)
        grad_two = (rounded_sum(terms_two) * scale_tw[:, None, None]).astype(jnp.bfloat16)
        terms_one = jnp.einsum("ptbi,pto->pbio", x_sel.reshape(N_DP, TOK_DEV, K1, BLK).astype(jnp.float32), d_pre.reshape(N_DP, TOK_DEV, BLK).astype(jnp.float32), precision=lax.Precision.HIGHEST)
        grad_one = (rounded_sum(terms_one) * scale_one[:, None, None]).astype(jnp.bfloat16)
        dx_blocks = jnp.einsum("to,bio->tbi", d_pre.astype(jnp.float32), weff_one.astype(jnp.float32), precision=lax.Precision.HIGHEST)
        dx_part = dx_part.at[:, rows].add(dx_blocks)
        last = (index % HB_DEV) == HB_DEV - 1
        kept = lax.optimization_barrier(dx_part.astype(jnp.bfloat16)).astype(jnp.float32)
        dx_total = dx_total + jnp.where(last, kept, jnp.zeros_like(kept))
        dx_part = jnp.where(last, jnp.zeros_like(dx_part), dx_part)
        return (y_acc, dx_total, dx_part), (grad_one, grad_two)

    (y_acc, dx_total, dx_part), (grads_one, grads_two) = lax.scan(step, start, steps_in)
    mixed = y_acc.reshape(TOKENS, D).astype(jnp.bfloat16)
    input_grad = dx_total.reshape(TOKENS, D).astype(jnp.bfloat16)
    grad_w2 = jnp.zeros((SLOTS, K2, BLK, BLK), jnp.bfloat16).at[where_two].set(grads_two)
    return mixed, input_grad, grads_one, grad_w2
```

```python
import jax
import jax.numpy as jnp
from jax import lax
from jax.experimental import pallas as pl
from jax.experimental.pallas import tpu as pltpu
from jax.sharding import PartitionSpec as P

GELU_C = 0.7978845608028654
GELU_A = 0.044715
MESH = pl.DeviceIdType.MESH
BF = jnp.bfloat16
F32 = jnp.float32
NB = 12
NK = 15
CAP = 18
HALF = NB // 2


def where_am_i():
    p = lax.axis_index("dp")
    t = lax.axis_index("tensor")
    return p, t, p // 2, p % 2, t // 4, t % 4


def enter(p, t, x, c, y, z):
    barrier = pltpu.get_barrier_semaphore()
    for d in range(1, 16):
        peer = ((y + d // 4) % 4) * 4 + (z + d % 4) % 4
        pl.semaphore_signal(barrier, inc=1, device_id=(p, peer), device_id_type=MESH)
    for q in (2 * ((x + 1) % 4) + c, 2 * ((x + 3) % 4) + c, 2 * x + 1 - c):
        pl.semaphore_signal(barrier, inc=1, device_id=(q, t), device_id_type=MESH)
    return barrier


def gather_kernel(
    tok_ref,
    cot_ref,
    w1_ref,
    w2_ref,
    s1_ref,
    s2_ref,
    own_slot_ref,
    home_lane_ref,
    xall,
    dyall,
    w1all,
    w2all,
    tok3,
    cot3,
    e1s,
    e2s,
    lanes,
    rbuf,
    a_send,
    a_recv,
    w_send,
    w_recv,
    x_send,
    x_recv,
    l_sem,
):
    p, t, x, c, y, z = where_am_i()
    barrier = enter(p, t, x, c, y, z)
    rp, lp, op, sp = 2 * ((x + 1) % 4) + c, 2 * ((x + 3) % 4) + c, 2 * ((x + 2) % 4) + c, 2 * x + 1 - c

    def copy_lane(i, _):
        s = own_slot_ref[i]
        lanes[i] = w2_ref[s]
        return 0

    lax.fori_loop(0, 32, copy_lane, 0)

    def scale_one(g, _):
        for k in range(NK):
            e1s[g, k] = (w1_ref[g, k].astype(F32) * s1_ref[g, k]).astype(BF)
        return 0

    lax.fori_loop(0, NB, scale_one, 0)
    for b in range(3):
        tok3[b] = tok_ref[:, b * 128 : (b + 1) * 128]
        cot3[b] = cot_ref[:, b * 128 : (b + 1) * 128]

    def lane_copy(d):
        peer = ((y + d // 4) % 4) * 4 + (z + d % 4) % 4
        return pltpu.make_async_remote_copy(
            lanes.at[pl.ds(2 * peer, 2)],
            rbuf.at[pl.ds(2 * t, 2)],
            a_send.at[d],
            a_recv.at[d],
            device_id=(p, peer),
            device_id_type=MESH,
        )

    def weight_copy(w, i):
        e, a = ((e1s, w1all), (e2s, w2all))[w]
        first, second = pl.ds(0, HALF), pl.ds(HALF, HALF)
        src, dst, dev = (
            (e.at[first], a.at[p, first], rp),
            (e.at[second], a.at[p, second], rp),
            (e.at[second], a.at[p, second], lp),
            (e.at[first], a.at[p, first], lp),
            (e, a.at[p], sp),
            (a.at[lp, first], a.at[lp, first], rp),
            (a.at[rp, second], a.at[rp, second], lp),
            (a.at[lp], a.at[lp], sp),
            (a.at[rp], a.at[rp], sp),
            (a.at[op], a.at[op], sp),
        )[i]
        return pltpu.make_async_remote_copy(
            src, dst, w_send.at[w, i], w_recv.at[w, i], device_id=(dev, t), device_id_type=MESH
        )

    def feature_copy(w, first, second):
        own, full = ((tok3, xall), (cot3, dyall))[w]
        if second == 0:
            src = own
            holder = t
            ay, az = (first, 0) if w == 0 else (0, first)
        else:
            by, bz = (first, 0) if w == 0 else (0, first)
            holder = ((y + 4 - by) % 4) * 4 + (z + 4 - bz) % 4
            src = own if first == 0 else full.at[holder]
            ay, az = (0, second) if w == 0 else (second, 0)
        peer = ((y + ay) % 4) * 4 + (z + az) % 4
        return pltpu.make_async_remote_copy(
            src,
            full.at[holder],
            x_send.at[w, first, second],
            x_recv.at[w, first, second],
            device_id=(p, peer),
            device_id_type=MESH,
        )

    pl.semaphore_wait(barrier, 18)
    for d in range(1, 16):
        lane_copy(d).start()
    for i in range(5):
        weight_copy(0, i).start()
    local = [
        pltpu.make_async_copy(tok3, xall.at[t], l_sem.at[0]),
        pltpu.make_async_copy(cot3, dyall.at[t], l_sem.at[1]),
        pltpu.make_async_copy(e1s, w1all.at[p], l_sem.at[2]),
    ]
    for cp in local:
        cp.start()
    for first in range(1, 4):
        for w in range(2):
            feature_copy(w, first, 0).start()

    def weights_on(w):
        weight_copy(w, 0).wait_recv()
        weight_copy(w, 5).start()
        weight_copy(w, 2).wait_recv()
        weight_copy(w, 6).start()
        weight_copy(w, 1).wait_recv()
        weight_copy(w, 7).start()
        weight_copy(w, 3).wait_recv()
        weight_copy(w, 8).start()

    for second in range(1, 4):
        for w in range(2):
            feature_copy(w, 0, second).start()
    weights_on(0)
    for d in range(1, 16):
        lane_copy(d).wait_recv()
    rbuf[pl.ds(2 * t, 2)] = lanes[pl.ds(2 * t, 2)]

    def scale_two(g, _):
        i = home_lane_ref[g]
        for k in range(NK):
            e2s[g, k] = (rbuf[i, k].astype(F32) * s2_ref[g, k]).astype(BF)
        return 0

    lax.fori_loop(0, NB, scale_two, 0)
    for i in range(5):
        weight_copy(1, i).start()
    keep = pltpu.make_async_copy(e2s, w2all.at[p], l_sem.at[3])
    keep.start()
    local.append(keep)
    for first in range(1, 4):
        for w in range(2):
            feature_copy(w, first, 0).wait_recv()
            for second in range(1, 4):
                feature_copy(w, first, second).start()
    weight_copy(0, 5).wait_recv()
    weight_copy(0, 6).wait_recv()
    weight_copy(0, 9).start()
    weights_on(1)
    weight_copy(1, 5).wait_recv()
    weight_copy(1, 6).wait_recv()
    weight_copy(1, 9).start()
    for first in range(4):
        for second in range(1, 4):
            for w in range(2):
                feature_copy(w, first, second).wait_recv()
    for w in range(2):
        for i in (4, 7, 8, 9):
            weight_copy(w, i).wait_recv()
    for cp in local:
        cp.wait()
    for d in range(1, 16):
        lane_copy(d).wait_send()
    for w in range(2):
        for i in range(10):
            weight_copy(w, i).wait_send()
        for first in range(4):
            for second in range(4):
                if first or second:
                    feature_copy(w, first, second).wait_send()


def compute_kernel(
    rows, cols, x_ref, dy_ref, w1_ref, w2_ref, m_ref, d_ref, g1_ref, g2_ref, acc_m, acc_d, xt
):
    g = pl.program_id(0)

    @pl.when(g == 0)
    def _():
        acc_m[...] = jnp.zeros_like(acc_m)
        acc_d[...] = jnp.zeros_like(acc_d)

        def flip(j, _):
            xt[j] = x_ref[j].T
            return 0

        lax.fori_loop(0, 48, flip, 0)

    nt = (((1,), (1,)), ((), ()))
    r = [rows[g, k] for k in range(NK)]
    q = [cols[g, k] for k in range(NK)]
    w1c = jnp.concatenate([w1_ref[:, 0, k].reshape(128, 128) for k in range(NK)], axis=0)
    w2c = jnp.concatenate([w2_ref[:, 0, k].reshape(128, 128) for k in range(NK)], axis=1)
    xs = jnp.concatenate([x_ref[r[k]] for k in range(NK)], axis=1)
    dys = jnp.concatenate([dy_ref[q[k]] for k in range(NK)], axis=1)
    pre = jnp.dot(xs, w1c, preferred_element_type=F32)
    dact = lax.dot_general(dys, w2c, nt, preferred_element_type=F32).astype(BF)
    th = jnp.tanh(GELU_C * (pre + GELU_A * pre * pre * pre))
    act = (0.5 * pre * (1.0 + th)).astype(BF)
    slope = 0.5 * (1.0 + th) + 0.5 * pre * (1.0 - th * th) * GELU_C * (
        1.0 + 3.0 * GELU_A * pre * pre
    )
    dpre = (dact.astype(F32) * slope).astype(BF)
    mix = jnp.dot(act, w2c, preferred_element_type=F32)
    for k in range(NK):
        acc_m[q[k]] += mix[:, k * 128 : (k + 1) * 128]
    dx = lax.dot_general(dpre, w1c, nt, preferred_element_type=F32)
    for k in range(NK):
        acc_d[r[k]] += dx[:, k * 128 : (k + 1) * 128]
    gw2 = jnp.dot(act.T, dys, preferred_element_type=F32).astype(BF)
    for k in range(NK):
        g2_ref[:, 0, k] = gw2[:, k * 128 : (k + 1) * 128].reshape(8, 16, 128)
        g1_ref[:, 0, k] = (
            jnp.dot(xt[r[k]], dpre, preferred_element_type=F32).astype(BF).reshape(8, 16, 128)
        )

    @pl.when(g == pl.num_programs(0) - 1)
    def _():
        def out(j, _):
            m_ref[j] = acc_m[j].astype(BF)
            d_ref[j] = acc_d[j].astype(BF)
            return 0

        lax.fori_loop(0, 48, out, 0)


def reduce_kernel(
    m_ref,
    d_ref,
    g1_ref,
    g2_ref,
    s1_ref,
    s2_ref,
    home_local_ref,
    slot_lane_ref,
    slot_live_ref,
    mixed,
    dxo,
    o1,
    o2,
    own,
    sib,
    fwd,
    fin,
    red2,
    lanes,
    rbuf,
    f_own,
    f_buf,
    f_sum,
    f_fin,
    w_send,
    w_recv,
    f_send,
    f_recv,
    a_send,
    a_recv,
    l_sem,
):
    p, t, x, c, y, z = where_am_i()
    barrier = enter(p, t, x, c, y, z)
    xr, xl, xo = (x + 1) % 4, (x + 3) % 4, (x + 2) % 4
    rp, lp, sp = 2 * xr + c, 2 * xl + c, 2 * x + 1 - c
    grads = (g2_ref, g1_ref)
    feats = (m_ref, d_ref)
    first, second = pl.ds(0, HALF), pl.ds(HALF, HALF)

    def grad_copy(w, i):
        src, dst, dev = (
            (own.at[w, xo, first], fwd.at[w, 0], rp),
            (own.at[w, xo, second], fwd.at[w, 1], lp),
            (own.at[w, xr, second], fin.at[w, 0, second], rp),
            (own.at[w, xl, first], fin.at[w, 1, first], lp),
            (own.at[w, xr, first], fin.at[w, 0, first], rp),
            (own.at[w, xl, second], fin.at[w, 1, second], lp),
            (grads[w].at[:, 1 - c], sib.at[w], sp),
        )[i]
        return pltpu.make_async_remote_copy(
            src, dst, w_send.at[w, i], w_recv.at[w, i], device_id=(dev, t), device_id_type=MESH
        )

    def feat_copy(w, step, d):
        along_y = (w == 0) == (step == 0)
        peer_y, peer_z = ((y + d) % 4, z) if along_y else (y, (z + d) % 4)
        if step == 0:
            src = feats[w].at[peer_y] if along_y else feats[w].at[:, peer_z]
            dst = f_buf.at[w, d - 1]
        else:
            src = f_sum.at[w, peer_y if along_y else peer_z]
            dst = f_fin.at[w, d - 1]
        return pltpu.make_async_remote_copy(
            src,
            dst,
            f_send.at[w, step, d],
            f_recv.at[w, step, d],
            device_id=(p, peer_y * 4 + peer_z),
            device_id_type=MESH,
        )

    def lane_copy(d):
        peer = ((y + d // 4) % 4) * 4 + (z + d % 4) % 4
        return pltpu.make_async_remote_copy(
            lanes.at[pl.ds(2 * peer, 2)],
            rbuf.at[pl.ds(2 * t, 2)],
            a_send.at[d],
            a_recv.at[d],
            device_id=(p, peer),
            device_id_type=MESH,
        )

    local = [pltpu.make_async_copy(grads[w].at[:, c], own.at[w], l_sem.at[w]) for w in range(2)]
    local.append(pltpu.make_async_copy(m_ref.at[y], f_own.at[0], l_sem.at[2]))
    local.append(pltpu.make_async_copy(d_ref.at[:, z], f_own.at[1], l_sem.at[3]))
    for cp in local:
        cp.start()
    pl.semaphore_wait(barrier, 18)
    grad_copy(0, 6).start()
    for d in range(1, 4):
        for w in range(2):
            feat_copy(w, 0, d).start()
    grad_copy(1, 6).start()

    def pair_sum(w, chunk, lo, n):
        def body(g, _):
            own[w, chunk, g] = (own[w, chunk, g].astype(F32) + sib[w, chunk, g].astype(F32)).astype(
                BF
            )
            return 0

        lax.fori_loop(lo, lo + n, body, 0)

    def pair_stage(w):
        local[w].wait()
        grad_copy(w, 6).wait_recv()
        pair_sum(w, xo, 0, NB)
        grad_copy(w, 0).start()
        grad_copy(w, 1).start()
        pair_sum(w, xr, HALF, HALF)
        grad_copy(w, 2).start()
        pair_sum(w, xl, 0, HALF)
        grad_copy(w, 3).start()
        pair_sum(w, xr, 0, HALF)
        pair_sum(w, xl, HALF, HALF)
        pair_sum(w, x, 0, NB)

    def pass_stage(w):
        grad_copy(w, 0).wait_recv()

        def right(g, _):
            own[w, xr, g] = (own[w, xr, g].astype(F32) + fwd[w, 0, g].astype(F32)).astype(BF)
            return 0

        lax.fori_loop(0, HALF, right, 0)
        grad_copy(w, 4).start()
        grad_copy(w, 1).wait_recv()

        def left(g, _):
            own[w, xl, g + HALF] = (
                own[w, xl, g + HALF].astype(F32) + fwd[w, 1, g].astype(F32)
            ).astype(BF)
            return 0

        lax.fori_loop(0, HALF, left, 0)
        grad_copy(w, 5).start()

    def last_stage(w, out, scale):
        for i in (2, 3, 4, 5):
            grad_copy(w, i).wait_recv()

        def body(g, _):
            for k in range(NK):
                total = own[w, x, g, k].astype(F32) + fin[w, 0, g, k].astype(F32)
                total = total + fin[w, 1, g, k].astype(F32)
                out[g, k] = (total * scale[g, k]).astype(BF)
            return 0

        lax.fori_loop(0, NB, body, 0)

    pair_stage(0)
    for w in range(2):
        local[2 + w].wait()
        for d in range(1, 4):
            feat_copy(w, 0, d).wait_recv()

        def add_four(i, _):
            a, b = i // 3, i % 3
            total = f_own[w, a, b].astype(F32)
            for d in range(3):
                total = total + f_buf[w, d, a, b].astype(F32)
            f_sum[w, a, b] = total.astype(BF)
            return 0

        lax.fori_loop(0, 12, add_four, 0)
        for d in range(1, 4):
            feat_copy(w, 1, d).start()
    pass_stage(0)
    pair_stage(1)
    for w, out in ((0, mixed), (1, dxo)):
        for d in range(1, 4):
            feat_copy(w, 1, d).wait_recv()
        here = z if w == 0 else y
        for b in range(3):
            total = f_sum[w, here, b].astype(F32)
            for d in range(3):
                total = total + f_fin[w, d, b].astype(F32)
            out[:, b * 128 : (b + 1) * 128] = total.astype(BF)
    last_stage(0, red2, s2_ref)

    def copy_lane(i, _):
        s = home_local_ref[i]
        lanes[i] = red2[s]
        return 0

    lax.fori_loop(0, 32, copy_lane, 0)
    for d in range(1, 16):
        lane_copy(d).start()
    rbuf[pl.ds(2 * t, 2)] = lanes[pl.ds(2 * t, 2)]
    pass_stage(1)
    for d in range(1, 16):
        lane_copy(d).wait_recv()

    def slot_out(s, _):
        i = slot_lane_ref[s]
        o2[s] = jnp.where(slot_live_ref[s] > 0, rbuf[i], jnp.zeros_like(rbuf[i]))
        return 0

    lax.fori_loop(0, CAP, slot_out, 0)
    last_stage(1, o1, s1_ref)
    for w in range(2):
        for i in range(7):
            grad_copy(w, i).wait_send()
        for step in range(2):
            for d in range(1, 4):
                feat_copy(w, step, d).wait_send()
    for d in range(1, 16):
        lane_copy(d).wait_send()


def route_tables(owner, rank):
    index = jnp.arange(192, dtype=jnp.int32)
    source = index // NB
    earlier = index[None, :] < index[:, None]
    same_dest = owner[None, :] == owner[:, None]
    same_src = source[None, :] == source[:, None]
    slot = jnp.sum((earlier & same_dest).astype(jnp.int32), axis=1)
    pair = jnp.sum((earlier & same_dest & same_src).astype(jnp.int32), axis=1)
    mine_first = rank * NB
    mine_owner = lax.dynamic_slice(owner, (mine_first,), (NB,))
    mine_pair = lax.dynamic_slice(pair, (mine_first,), (NB,))
    mine_slot = lax.dynamic_slice(slot, (mine_first,), (NB,))
    home_lane = mine_owner * 2 + mine_pair
    home_q = mine_owner * CAP + mine_slot
    lane = jnp.arange(32, dtype=jnp.int32)
    mine_lane = jnp.where(owner == rank, source * 2 + pair, -1)
    own_slot = jnp.sum(jnp.where(lane[:, None] == mine_lane[None, :], slot[None, :], 0), axis=1)
    home_local = jnp.sum(
        jnp.where(
            lane[:, None] == home_lane[None, :], jnp.arange(NB, dtype=jnp.int32)[None, :], 0
        ),
        axis=1,
    )
    mine_at = jnp.where(owner == rank, slot, -1)
    hit = jnp.arange(CAP, dtype=jnp.int32)[:, None] == mine_at[None, :]
    slot_lane = jnp.sum(jnp.where(hit, (source * 2 + pair)[None, :], 0), axis=1)
    slot_live = jnp.any(hit, axis=1).astype(jnp.int32)
    return home_lane, home_q, own_slot, home_local, slot_lane, slot_live


VM = pl.BlockSpec(memory_space=pltpu.VMEM)
SM = pl.BlockSpec(memory_space=pltpu.SMEM)
ANY = pl.BlockSpec(memory_space=pl.ANY)
SHARD = (NB, NK, 16, 128)
LANES = (32, NK, 16, 128)


def local(tokens, cotangent, w1_blocks, w1_rows, w1_scale, w2_blocks, w2_cols, w2_scale, owner):
    rank = lax.axis_index("tensor")
    home_lane, home_q, own_slot, home_local, slot_lane, slot_live = route_tables(owner, rank)
    rows = lax.dynamic_slice(w1_rows, (rank * NB, 0), (NB, NK))
    scale_one = lax.dynamic_slice(w1_scale, (rank * NB, 0), (NB, NK))
    cols = w2_cols[home_q]
    scale_two = w2_scale[home_q]
    dma = pltpu.SemaphoreType.DMA
    xall, dyall, w1all, w2all = pl.pallas_call(
        gather_kernel,
        out_shape=[
            jax.ShapeDtypeStruct((16, 3, 192, 128), BF),
            jax.ShapeDtypeStruct((16, 3, 192, 128), BF),
            jax.ShapeDtypeStruct((8,) + SHARD, BF),
            jax.ShapeDtypeStruct((8,) + SHARD, BF),
        ],
        in_specs=[VM, VM, VM, VM, SM, SM, SM, SM],
        out_specs=[ANY] * 4,
        scratch_shapes=[
            pltpu.VMEM((3, 192, 128), BF),
            pltpu.VMEM((3, 192, 128), BF),
            pltpu.VMEM(SHARD, BF),
            pltpu.VMEM(SHARD, BF),
            pltpu.VMEM(LANES, BF),
            pltpu.VMEM(LANES, BF),
            dma((16,)),
            dma((16,)),
            dma((2, 10)),
            dma((2, 10)),
            dma((2, 4, 4)),
            dma((2, 4, 4)),
            dma((4,)),
        ],
        compiler_params=pltpu.CompilerParams(
            collective_id=0, has_side_effects=True, vmem_limit_bytes=40 << 20
        ),
    )(tokens, cotangent, w1_blocks, w2_blocks, scale_one, scale_two, own_slot, home_lane)
    whole = pl.BlockSpec((48, 192, 128), lambda g, *_: (0, 0, 0))
    blocks = pl.BlockSpec((8, 1, NK, 16, 128), lambda g, *_: (0, g, 0, 0, 0))
    m_part, d_part, g1, g2 = pl.pallas_call(
        compute_kernel,
        grid_spec=pltpu.PrefetchScalarGridSpec(
            num_scalar_prefetch=2,
            grid=(NB,),
            in_specs=[whole, whole, blocks, blocks],
            out_specs=[whole, whole, blocks, blocks],
            scratch_shapes=[
                pltpu.VMEM((48, 192, 128), F32),
                pltpu.VMEM((48, 192, 128), F32),
                pltpu.VMEM((48, 128, 192), BF),
            ],
        ),
        out_shape=[
            jax.ShapeDtypeStruct((48, 192, 128), BF),
            jax.ShapeDtypeStruct((48, 192, 128), BF),
            jax.ShapeDtypeStruct((8,) + SHARD, BF),
            jax.ShapeDtypeStruct((8,) + SHARD, BF),
        ],
        compiler_params=pltpu.CompilerParams(
            dimension_semantics=("arbitrary",), vmem_limit_bytes=56 << 20
        ),
    )(rows, cols, xall.reshape(48, 192, 128), dyall.reshape(48, 192, 128), w1all, w2all)
    feat = (4, 4, 3, 192, 128)
    grad = (4, 2) + SHARD
    mixed, dx, o1, o2 = pl.pallas_call(
        reduce_kernel,
        out_shape=[
            jax.ShapeDtypeStruct((192, 384), BF),
            jax.ShapeDtypeStruct((192, 384), BF),
            jax.ShapeDtypeStruct(SHARD, BF),
            jax.ShapeDtypeStruct((CAP, NK, 16, 128), BF),
        ],
        in_specs=[ANY] * 4 + [SM] * 5,
        out_specs=[VM] * 4,
        scratch_shapes=[
            pltpu.VMEM((2, 4) + SHARD, BF),
            pltpu.VMEM((2, 4) + SHARD, BF),
            pltpu.VMEM((2, 2, HALF, NK, 16, 128), BF),
            pltpu.VMEM((2, 2) + SHARD, BF),
            pltpu.VMEM(SHARD, BF),
            pltpu.VMEM(LANES, BF),
            pltpu.VMEM(LANES, BF),
            pltpu.VMEM((2, 4, 3, 192, 128), BF),
            pltpu.VMEM((2, 3, 4, 3, 192, 128), BF),
            pltpu.VMEM((2, 4, 3, 192, 128), BF),
            pltpu.VMEM((2, 3, 3, 192, 128), BF),
            dma((2, 7)),
            dma((2, 7)),
            dma((2, 2, 4)),
            dma((2, 2, 4)),
            dma((16,)),
            dma((16,)),
            dma((4,)),
        ],
        compiler_params=pltpu.CompilerParams(
            collective_id=1, has_side_effects=True, vmem_limit_bytes=48 << 20
        ),
    )(
        m_part.reshape(feat),
        d_part.reshape(feat),
        g1.reshape(grad),
        g2.reshape(grad),
        scale_one,
        scale_two,
        home_local,
        slot_lane,
        slot_live,
    )
    return mixed, dx, o1, o2


def solution(mesh):
    in_specs = (
        P("dp", "tensor"),
        P("dp", "tensor"),
        P("tensor", None, "dp", None),
        P(),
        P(),
        P("tensor", None, "dp", None),
        P(),
        P(),
        P(),
    )
    out_specs = (
        P("dp", "tensor"),
        P("dp", "tensor"),
        P("tensor", None, "dp", None),
        P("tensor", None, "dp", None),
    )
    return jax.shard_map(local, mesh=mesh, in_specs=in_specs, out_specs=out_specs, check_vma=False)
```

```python
import jax
import jax.numpy as jnp
from jax import lax
from jax.experimental import pallas as pl
from jax.experimental.pallas import tpu as pltpu
from jax.sharding import PartitionSpec as P

GELU_C = 0.7978845608028654
GELU_A = 0.044715
MESH = pl.DeviceIdType.MESH
BF = jnp.bfloat16
F32 = jnp.float32
NB = 12
NK = 15
CAP = 18
HALF = NB // 2


def where_am_i():
    p = lax.axis_index("dp")
    t = lax.axis_index("tensor")
    return p, t, p // 2, p % 2, t // 4, t % 4


def enter(p, t, x, c, y, z):
    barrier = pltpu.get_barrier_semaphore()
    for d in range(1, 16):
        peer = ((y + d // 4) % 4) * 4 + (z + d % 4) % 4
        pl.semaphore_signal(barrier, inc=1, device_id=(p, peer), device_id_type=MESH)
    for q in (2 * ((x + 1) % 4) + c, 2 * ((x + 3) % 4) + c, 2 * x + 1 - c):
        pl.semaphore_signal(barrier, inc=1, device_id=(q, t), device_id_type=MESH)
    return barrier


def layer_kernel(
    tok_ref,
    cot_ref,
    w1_ref,
    w2_ref,
    s1_ref,
    s2_ref,
    rows,
    cols,
    kv1,
    kv2,
    own_slot_ref,
    home_lane_ref,
    home_local_ref,
    slot_lane_ref,
    slot_live_ref,
    mixed,
    dxo,
    o1,
    o2,
    w1in,
    w2in,
    xall,
    dyall,
    w1all,
    w2all,
    lanes,
    rbuf,
    rback,
    xt,
    slope,
    act_all,
    dpre_all,
    g1s,
    g2s,
    sib,
    fwd,
    fin,
    m_part,
    d_part,
    f_buf,
    f_fin,
    a_send,
    a_recv,
    b_send,
    b_recv,
    w_send,
    w_recv,
    x_send,
    x_recv,
    g_send,
    g_recv,
    f_send,
    f_recv,
    l_sem,
    free_sem,
):
    p, t, x, c, y, z = where_am_i()
    barrier = enter(p, t, x, c, y, z)
    xr, xl, xo = (x + 1) % 4, (x + 3) % 4, (x + 2) % 4
    rp, lp, op, sp = 2 * xr + c, 2 * xl + c, 2 * xo + c, 2 * x + 1 - c
    halves = (pl.ds(0, HALF), pl.ds(HALF, HALF))
    first, second = halves
    whole = pl.ds(0, NB)
    feats = (xall, dyall)
    weights = (w1all, w2all)
    grads = (g2s, g1s)
    parts = (m_part, d_part)
    nt = (((1,), (1,)), ((), ()))

    def lane_copy(back, d):
        peer = ((y + d // 4) % 4) * 4 + (z + d % 4) % 4
        return pltpu.make_async_remote_copy(
            lanes.at[pl.ds(2 * peer, 2)],
            (rback if back else rbuf).at[pl.ds(2 * t, 2)],
            (b_send if back else a_send).at[d],
            (b_recv if back else a_recv).at[d],
            device_id=(p, peer),
            device_id_type=MESH,
        )

    def weight_copy(w, i):
        who, part, dev = (
            (p, first, rp),
            (p, second, rp),
            (p, second, lp),
            (p, first, lp),
            (p, whole, sp),
            (lp, first, rp),
            (rp, second, lp),
            (lp, whole, sp),
            (rp, whole, sp),
            (op, whole, sp),
        )[i]
        ref = weights[w].at[who, part, pl.ds(0, NK)]
        return pltpu.make_async_remote_copy(
            ref, ref, w_send.at[w, i], w_recv.at[w, i], device_id=(dev, t), device_id_type=MESH
        )

    def feature_copy(w, one, two):
        if two == 0:
            holder = t
            ay, az = (one, 0) if w == 0 else (0, one)
        else:
            by, bz = (one, 0) if w == 0 else (0, one)
            holder = ((y + 4 - by) % 4) * 4 + (z + 4 - bz) % 4
            ay, az = (0, two) if w == 0 else (two, 0)
        peer = ((y + ay) % 4) * 4 + (z + az) % 4
        ref = feats[w].at[pl.ds(3 * holder, 3)]
        return pltpu.make_async_remote_copy(
            ref,
            ref,
            x_send.at[w, one, two],
            x_recv.at[w, one, two],
            device_id=(p, peer),
            device_id_type=MESH,
        )

    def grad_copy(w, i):
        own = grads[w]
        src, dst, dev = (
            (own.at[xo, c, first], fwd.at[w, 0], rp),
            (own.at[xo, c, second], fwd.at[w, 1], lp),
            (own.at[xr, c, second], fin.at[w, 0, second], rp),
            (own.at[xl, c, first], fin.at[w, 1, first], lp),
            (own.at[xr, c, first], fin.at[w, 0, first], rp),
            (own.at[xl, c, second], fin.at[w, 1, second], lp),
            (own.at[:, 1 - c, first], sib.at[:, first], sp),
            (own.at[:, 1 - c, second], sib.at[:, second], sp),
        )[i]
        return pltpu.make_async_remote_copy(
            src, dst, g_send.at[w, i], g_recv.at[w, i], device_id=(dev, t), device_id_type=MESH
        )

    def part_copy(w, step, d):
        along_y = (w == 0) == (step == 0)
        peer_y, peer_z = ((y + d) % 4, z) if along_y else (y, (z + d) % 4)
        if step == 0:
            src = parts[w].at[peer_y] if along_y else parts[w].at[:, peer_z]
            dst = f_buf.at[w, d - 1]
        else:
            src = parts[w].at[peer_y, peer_z]
            dst = f_fin.at[w, d - 1]
        return pltpu.make_async_remote_copy(
            src,
            dst,
            f_send.at[w, step, d],
            f_recv.at[w, step, d],
            device_id=(p, peer_y * 4 + peer_z),
            device_id_type=MESH,
        )

    loads = [
        pltpu.make_async_copy(w2_ref, w2in, l_sem.at[0]),
        pltpu.make_async_copy(w1_ref, w1in, l_sem.at[1]),
    ]
    for w, ref in enumerate((tok_ref, cot_ref)):
        for b in range(3):
            loads.append(
                pltpu.make_async_copy(
                    ref.at[:, pl.ds(b * 128, 128)],
                    feats[w].at[3 * t + b],
                    l_sem.at[2 + 3 * w + b],
                )
            )
    for cp in loads:
        cp.start()
    loads[0].wait()

    def lanes_out(i, _):
        s = own_slot_ref[i]
        lanes[i] = w2in[s]
        return 0

    lax.fori_loop(0, 32, lanes_out, 0)
    pl.semaphore_wait(barrier, 18)
    for d in range(1, 16):
        lane_copy(False, d).start()
    loads[1].wait()

    def scale_one(g, _):
        for k in range(NK):
            w1all[p, g, k] = (w1in[g, k].astype(F32) * s1_ref[g, k]).astype(BF)
        return 0

    lax.fori_loop(0, NB, scale_one, 0)
    for i in range(5):
        weight_copy(0, i).start()
    for cp in loads[2:]:
        cp.wait()
    for one in range(1, 4):
        for w in range(2):
            feature_copy(w, one, 0).start()
    for two in range(1, 4):
        for w in range(2):
            feature_copy(w, 0, two).start()
    w1all[:, :, NK] = jnp.zeros((8, NB, 16, 128), BF)
    w2all[:, :, NK] = jnp.zeros((8, NB, 16, 128), BF)

    def weights_on(w):
        weight_copy(w, 0).wait_recv()
        weight_copy(w, 5).start()
        weight_copy(w, 2).wait_recv()
        weight_copy(w, 6).start()
        weight_copy(w, 1).wait_recv()
        weight_copy(w, 7).start()
        weight_copy(w, 3).wait_recv()
        weight_copy(w, 8).start()

    def weights_last(w):
        weight_copy(w, 5).wait_recv()
        weight_copy(w, 6).wait_recv()
        weight_copy(w, 9).start()

    weights_on(0)
    for d in range(1, 16):
        lane_copy(False, d).wait_recv()
    rbuf[pl.ds(2 * t, 2)] = lanes[pl.ds(2 * t, 2)]

    def scale_two(g, _):
        i = home_lane_ref[g]
        for k in range(NK):
            w2all[p, g, k] = (rbuf[i, k].astype(F32) * s2_ref[g, k]).astype(BF)
        return 0

    lax.fori_loop(0, NB, scale_two, 0)
    for i in range(5):
        weight_copy(1, i).start()
    for one in range(1, 4):
        for w in range(2):
            feature_copy(w, one, 0).wait_recv()
            for two in range(1, 4):
                feature_copy(w, one, two).start()
    weights_last(0)
    for one in range(4):
        for two in range(1, 4):
            for w in range(2):
                feature_copy(w, one, two).wait_recv()
    for i in (4, 7, 8, 9):
        weight_copy(0, i).wait_recv()

    def project(g, _):
        w1c = jnp.concatenate([w1all[:, g, k].reshape(128, 128) for k in range(NK)], axis=0)
        xs = jnp.concatenate([xall[rows[g, k]] for k in range(NK)], axis=1)
        pre = jnp.dot(xs, w1c, preferred_element_type=F32)
        th = jnp.tanh(GELU_C * (pre + GELU_A * pre * pre * pre))
        act = (0.5 * pre * (1.0 + th)).astype(BF)
        slope[g] = 0.5 * (1.0 + th) + 0.5 * pre * (1.0 - th * th) * GELU_C * (
            1.0 + 3.0 * GELU_A * pre * pre
        )
        act_all[:, pl.ds(pl.multiple_of(g * 128, 128), 128)] = act
        dys = jnp.concatenate([dyall[cols[g, k]] for k in range(NK)], axis=1)
        gw2 = jnp.dot(act.T, dys, preferred_element_type=F32).astype(BF)
        for k in range(NK):
            g2s[:, :, g, k] = gw2[:, k * 128 : (k + 1) * 128].reshape(4, 2, 16, 128)
        return 0

    lax.fori_loop(0, HALF, project, 0)
    grad_copy(0, 6).start()
    weights_on(1)
    lax.fori_loop(HALF, NB, project, 0)
    grad_copy(0, 7).start()

    def pair_sum(w, chunk, h):
        own = grads[w]

        def body(g, _):
            own[chunk, c, g] = (own[chunk, c, g].astype(F32) + sib[chunk, g].astype(F32)).astype(BF)
            return 0

        lax.fori_loop(h * HALF, (h + 1) * HALF, body, 0)

    def pair_stage(w):
        grad_copy(w, 6).wait_recv()
        pair_sum(w, xo, 0)
        grad_copy(w, 0).start()
        pair_sum(w, xl, 0)
        grad_copy(w, 3).start()
        grad_copy(w, 7).wait_recv()
        pair_sum(w, xo, 1)
        grad_copy(w, 1).start()
        pair_sum(w, xr, 1)
        grad_copy(w, 2).start()
        pair_sum(w, xr, 0)
        pair_sum(w, xl, 1)
        pair_sum(w, x, 0)
        pair_sum(w, x, 1)

    def pass_stage(w):
        own = grads[w]
        grad_copy(w, 0).wait_recv()

        def right(g, _):
            own[xr, c, g] = (own[xr, c, g].astype(F32) + fwd[w, 0, g].astype(F32)).astype(BF)
            return 0

        lax.fori_loop(0, HALF, right, 0)
        grad_copy(w, 4).start()
        grad_copy(w, 1).wait_recv()

        def left(g, _):
            own[xl, c, g + HALF] = (
                own[xl, c, g + HALF].astype(F32) + fwd[w, 1, g].astype(F32)
            ).astype(BF)
            return 0

        lax.fori_loop(0, HALF, left, 0)
        grad_copy(w, 5).start()

    def last_stage(w, out, scale):
        own = grads[w]
        for i in (2, 3, 4, 5):
            grad_copy(w, i).wait_recv()

        def body(g, _):
            for k in range(NK):
                total = own[x, c, g, k].astype(F32) + fin[w, 0, g, k].astype(F32)
                total = total + fin[w, 1, g, k].astype(F32)
                out(g, k, (total * scale[g, k]).astype(BF))
            return 0

        lax.fori_loop(0, NB, body, 0)

    weights_last(1)
    pair_stage(0)
    pl.semaphore_signal(free_sem, inc=1, device_id=(sp, t), device_id_type=MESH)

    def flip(j, _):
        xt[j] = xall[j].T
        return 0

    lax.fori_loop(0, 48, flip, 0)
    for i in (4, 7, 8, 9):
        weight_copy(1, i).wait_recv()

    def hidden(g, _):
        w2c = jnp.concatenate([w2all[:, g, k].reshape(128, 128) for k in range(NK)], axis=1)
        dys = jnp.concatenate([dyall[cols[g, k]] for k in range(NK)], axis=1)
        dact = lax.dot_general(dys, w2c, nt, preferred_element_type=F32).astype(BF)
        dpre = (dact.astype(F32) * slope[g]).astype(BF)
        dpre_all[:, pl.ds(pl.multiple_of(g * 128, 128), 128)] = dpre
        for k in range(NK):
            gw1 = jnp.dot(xt[rows[g, k]], dpre, preferred_element_type=F32).astype(BF)
            g1s[:, :, g, k] = gw1.reshape(4, 2, 16, 128)
        return 0

    lax.fori_loop(0, HALF, hidden, 0)
    pl.semaphore_wait(free_sem, 1)
    grad_copy(1, 6).start()
    lax.fori_loop(HALF, NB, hidden, 0)
    grad_copy(1, 7).start()
    pass_stage(0)

    def mix(row):
        def body(i, _):
            j = 12 * row + 2 * i
            panel = jnp.concatenate(
                [
                    jnp.concatenate(
                        [w2all[:, g, kv2[j + b, g]].reshape(128, 128) for g in range(NB)], axis=0
                    )
                    for b in range(2)
                ],
                axis=1,
            )
            res = jnp.dot(act_all[...], panel, preferred_element_type=F32).astype(BF)
            for b in range(2):
                at = 2 * i + b
                m_part[row, at // 3, at % 3] = res[:, b * 128 : (b + 1) * 128]
            return 0

        lax.fori_loop(0, 6, body, 0)

    def back(col):
        def body(i, _):
            at = (2 * i, 2 * i + 1)
            panel = jnp.concatenate(
                [
                    jnp.concatenate(
                        [
                            w1all[:, g, kv1[12 * (a // 3) + 3 * col + a % 3, g]].reshape(128, 128)
                            for g in range(NB)
                        ],
                        axis=1,
                    )
                    for a in at
                ],
                axis=0,
            )
            res = lax.dot_general(dpre_all[...], panel, nt, preferred_element_type=F32).astype(BF)
            for b, a in enumerate(at):
                d_part[a // 3, col, a % 3] = res[:, b * 128 : (b + 1) * 128]
            return 0

        lax.fori_loop(0, 6, body, 0)

    for d in range(1, 4):
        mix((y + d) % 4)
        part_copy(0, 0, d).start()
        back((z + d) % 4)
        part_copy(1, 0, d).start()
        if d == 1:
            pair_stage(1)
    mix(y)
    back(z)

    def keep_two(g, k, value):
        g2s[x, c, g, k] = value

    last_stage(0, keep_two, s2_ref)
    for d in range(1, 16):
        lane_copy(False, d).wait_send()

    def lanes_back(i, _):
        s = home_local_ref[i]
        lanes[i] = g2s[x, c, s]
        return 0

    lax.fori_loop(0, 32, lanes_back, 0)
    for d in range(1, 16):
        lane_copy(True, d).start()
    rback[pl.ds(2 * t, 2)] = lanes[pl.ds(2 * t, 2)]
    for w in range(2):
        for d in range(1, 4):
            part_copy(w, 0, d).wait_recv()
        part = parts[w]

        def add_four(i, _):
            a, b = i // 3, i % 3
            here = (y, a) if w == 0 else (a, z)
            total = part[here[0], here[1], b].astype(F32)
            for d in range(3):
                total = total + f_buf[w, d, a, b].astype(F32)
            part[here[0], here[1], b] = total.astype(BF)
            return 0

        lax.fori_loop(0, 12, add_four, 0)
        for d in range(1, 4):
            part_copy(w, 1, d).start()
    pass_stage(1)
    for w, out in ((0, mixed), (1, dxo)):
        for d in range(1, 4):
            part_copy(w, 1, d).wait_recv()
        for b in range(3):
            total = parts[w][y, z, b].astype(F32)
            for d in range(3):
                total = total + f_fin[w, d, b].astype(F32)
            out[:, b * 128 : (b + 1) * 128] = total.astype(BF)
    for d in range(1, 16):
        lane_copy(True, d).wait_recv()

    def slot_out(s, _):
        i = slot_lane_ref[s]
        o2[s] = jnp.where(slot_live_ref[s] > 0, rback[i], jnp.zeros_like(rback[i]))
        return 0

    lax.fori_loop(0, CAP, slot_out, 0)

    def keep_one(g, k, value):
        o1[g, k] = value

    last_stage(1, keep_one, s1_ref)
    for d in range(1, 16):
        lane_copy(True, d).wait_send()
    for w in range(2):
        for i in range(10):
            weight_copy(w, i).wait_send()
        for one in range(4):
            for two in range(4):
                if one or two:
                    feature_copy(w, one, two).wait_send()
        for i in range(8):
            grad_copy(w, i).wait_send()
        for step in range(2):
            for d in range(1, 4):
                part_copy(w, step, d).wait_send()


def route_tables(owner, rank):
    index = jnp.arange(192, dtype=jnp.int32)
    source = index // NB
    earlier = index[None, :] < index[:, None]
    same_dest = owner[None, :] == owner[:, None]
    same_src = source[None, :] == source[:, None]
    slot = jnp.sum((earlier & same_dest).astype(jnp.int32), axis=1)
    pair = jnp.sum((earlier & same_dest & same_src).astype(jnp.int32), axis=1)
    mine_first = rank * NB
    mine_owner = lax.dynamic_slice(owner, (mine_first,), (NB,))
    mine_pair = lax.dynamic_slice(pair, (mine_first,), (NB,))
    mine_slot = lax.dynamic_slice(slot, (mine_first,), (NB,))
    home_lane = mine_owner * 2 + mine_pair
    home_q = mine_owner * CAP + mine_slot
    lane = jnp.arange(32, dtype=jnp.int32)
    mine_lane = jnp.where(owner == rank, source * 2 + pair, -1)
    own_slot = jnp.sum(jnp.where(lane[:, None] == mine_lane[None, :], slot[None, :], 0), axis=1)
    home_local = jnp.sum(
        jnp.where(
            lane[:, None] == home_lane[None, :], jnp.arange(NB, dtype=jnp.int32)[None, :], 0
        ),
        axis=1,
    )
    mine_at = jnp.where(owner == rank, slot, -1)
    hit = jnp.arange(CAP, dtype=jnp.int32)[:, None] == mine_at[None, :]
    slot_lane = jnp.sum(jnp.where(hit, (source * 2 + pair)[None, :], 0), axis=1)
    slot_live = jnp.any(hit, axis=1).astype(jnp.int32)
    return home_lane, home_q, own_slot, home_local, slot_lane, slot_live


VM = pl.BlockSpec(memory_space=pltpu.VMEM)
SM = pl.BlockSpec(memory_space=pltpu.SMEM)
ANY = pl.BlockSpec(memory_space=pl.ANY)
SHARD = (NB, NK, 16, 128)
LANES = (32, NK, 16, 128)


def inverse(index):
    k = jnp.arange(NK, dtype=jnp.int32)
    hit = index[None, :, :] == jnp.arange(48, dtype=jnp.int32)[:, None, None]
    return NK + jnp.sum(jnp.where(hit, k[None, None, :] - NK, 0), axis=2)


def local(tokens, cotangent, w1_blocks, w1_rows, w1_scale, w2_blocks, w2_cols, w2_scale, owner):
    rank = lax.axis_index("tensor")
    home_lane, home_q, own_slot, home_local, slot_lane, slot_live = route_tables(owner, rank)
    rows = lax.dynamic_slice(w1_rows, (rank * NB, 0), (NB, NK))
    scale_one = lax.dynamic_slice(w1_scale, (rank * NB, 0), (NB, NK))
    cols = w2_cols[home_q]
    scale_two = w2_scale[home_q]
    dma = pltpu.SemaphoreType.DMA
    part = (4, 4, 3, 192, 128)
    return pl.pallas_call(
        layer_kernel,
        out_shape=[
            jax.ShapeDtypeStruct((192, 384), BF),
            jax.ShapeDtypeStruct((192, 384), BF),
            jax.ShapeDtypeStruct(SHARD, BF),
            jax.ShapeDtypeStruct((CAP, NK, 16, 128), BF),
        ],
        in_specs=[ANY] * 4 + [SM] * 11,
        out_specs=[VM] * 4,
        scratch_shapes=[
            pltpu.VMEM(SHARD, BF),
            pltpu.VMEM((CAP, NK, 16, 128), BF),
            pltpu.VMEM((48, 192, 128), BF),
            pltpu.VMEM((48, 192, 128), BF),
            pltpu.VMEM((8, NB, NK + 1, 16, 128), BF),
            pltpu.VMEM((8, NB, NK + 1, 16, 128), BF),
            pltpu.VMEM(LANES, BF),
            pltpu.VMEM(LANES, BF),
            pltpu.VMEM(LANES, BF),
            pltpu.VMEM((48, 128, 192), BF),
            pltpu.VMEM((NB, 192, 128), F32),
            pltpu.VMEM((192, NB * 128), BF),
            pltpu.VMEM((192, NB * 128), BF),
            pltpu.VMEM((4, 2) + SHARD, BF),
            pltpu.VMEM((4, 2) + SHARD, BF),
            pltpu.VMEM((4,) + SHARD, BF),
            pltpu.VMEM((2, 2, HALF, NK, 16, 128), BF),
            pltpu.VMEM((2, 2) + SHARD, BF),
            pltpu.VMEM(part, BF),
            pltpu.VMEM(part, BF),
            pltpu.VMEM((2, 3, 4, 3, 192, 128), BF),
            pltpu.VMEM((2, 3, 3, 192, 128), BF),
            dma((16,)),
            dma((16,)),
            dma((16,)),
            dma((16,)),
            dma((2, 10)),
            dma((2, 10)),
            dma((2, 4, 4)),
            dma((2, 4, 4)),
            dma((2, 8)),
            dma((2, 8)),
            dma((2, 2, 4)),
            dma((2, 2, 4)),
            dma((8,)),
            pltpu.SemaphoreType.REGULAR,
        ],
        compiler_params=pltpu.CompilerParams(
            collective_id=0, has_side_effects=True, vmem_limit_bytes=63 << 20
        ),
    )(
        tokens,
        cotangent,
        w1_blocks,
        w2_blocks,
        scale_one,
        scale_two,
        rows,
        cols,
        inverse(rows),
        inverse(cols),
        own_slot,
        home_lane,
        home_local,
        slot_lane,
        slot_live,
    )


def solution(mesh):
    in_specs = (
        P("dp", "tensor"),
        P("dp", "tensor"),
        P("tensor", None, "dp", None),
        P(),
        P(),
        P("tensor", None, "dp", None),
        P(),
        P(),
        P(),
    )
    out_specs = (
        P("dp", "tensor"),
        P("dp", "tensor"),
        P("tensor", None, "dp", None),
        P("tensor", None, "dp", None),
    )
    return jax.shard_map(local, mesh=mesh, in_specs=in_specs, out_specs=out_specs, check_vma=False)
```

```python
import jax
import jax.numpy as jnp
from jax import lax
from jax.experimental import pallas as pl
from jax.experimental.pallas import tpu as pltpu
from jax.sharding import PartitionSpec as P

GELU_C = 0.7978845608028654
GELU_A = 0.044715
MESH = pl.DeviceIdType.MESH
BF = jnp.bfloat16
F32 = jnp.float32
NB = 12
NK = 15
CAP = 18
HALF = NB // 2


def where_am_i():
    p = lax.axis_index("dp")
    t = lax.axis_index("tensor")
    return p, t, p // 2, p % 2, t // 4, t % 4


def enter(p, t, x, c, y, z):
    barrier = pltpu.get_barrier_semaphore()
    for d in range(1, 4):
        for peer in (((y + d) % 4) * 4 + z, y * 4 + (z + d) % 4):
            pl.semaphore_signal(barrier, inc=1, device_id=(p, peer), device_id_type=MESH)
    for q in (2 * ((x + 1) % 4) + c, 2 * ((x + 3) % 4) + c, 2 * x + 1 - c):
        pl.semaphore_signal(barrier, inc=1, device_id=(q, t), device_id_type=MESH)
    return barrier


def layer_kernel(
    tok_ref,
    cot_ref,
    w1_ref,
    w2_ref,
    s1_ref,
    s2_ref,
    rows,
    cols,
    kv1,
    kv2,
    own_slot_ref,
    home_lane_ref,
    home_local_ref,
    slot_lane_ref,
    slot_live_ref,
    mixed,
    dxo,
    o1,
    o2,
    w1in,
    w2in,
    xall,
    dyall,
    w1all,
    w2all,
    lanes,
    rbuf,
    rback,
    middle,
    xt,
    slope,
    act_all,
    dpre_all,
    g1s,
    g2s,
    sib,
    fwd,
    fin,
    m_part,
    d_part,
    f_buf,
    f_fin,
    a_send,
    a_recv,
    w_send,
    w_recv,
    x_send,
    x_recv,
    g_send,
    g_recv,
    f_send,
    f_recv,
    l_sem,
    free_sem,
):
    p, t, x, c, y, z = where_am_i()
    barrier = enter(p, t, x, c, y, z)
    xr, xl, xo = (x + 1) % 4, (x + 3) % 4, (x + 2) % 4
    rp, lp, op, sp = 2 * xr + c, 2 * xl + c, 2 * xo + c, 2 * x + 1 - c
    halves = (pl.ds(0, HALF), pl.ds(HALF, HALF))
    first, second = halves
    whole = pl.ds(0, NB)
    feats = (xall, dyall)
    weights = (w1all, w2all)
    grads = (g2s, g1s)
    parts = (m_part, d_part)
    landed = (rbuf, rback)
    nt = (((1,), (1,)), ((), ()))

    def lane_copy(trip, j, step, d):
        along_y = (j == 0) == (step == 0)
        peer_y, peer_z = ((y + d) % 4, z) if along_y else (y, (z + d) % 4)
        src = lanes.at[j] if step == 0 else middle.at[trip, j]
        dst = middle.at[trip, j] if step == 0 else landed[trip].at[j]
        return pltpu.make_async_remote_copy(
            src.at[peer_y] if along_y else src.at[:, peer_z],
            dst.at[y] if along_y else dst.at[:, z],
            a_send.at[trip, j, step, d],
            a_recv.at[trip, j, step, d],
            device_id=(p, peer_y * 4 + peer_z),
            device_id_type=MESH,
        )

    def lanes_go(trip):
        for d in (2, 1, 3):
            for j in range(2):
                lane_copy(trip, j, 0, d).start()
        middle[trip, 0, y] = lanes[0, y]
        middle[trip, 1, :, z] = lanes[1, :, z]

    def lanes_turn(trip):
        for j in range(2):
            for d in range(1, 4):
                lane_copy(trip, j, 0, d).wait_recv()
            for d in (2, 1, 3):
                lane_copy(trip, j, 1, d).start()
        landed[trip][0, :, z] = middle[trip, 0, :, z]
        landed[trip][1, y] = middle[trip, 1, y]

    def lanes_end(trip):
        for j in range(2):
            for d in range(1, 4):
                lane_copy(trip, j, 1, d).wait_recv()

    def lanes_sent(trip):
        for j in range(2):
            for step in range(2):
                for d in range(1, 4):
                    lane_copy(trip, j, step, d).wait_send()

    def weight_copy(w, i):
        who, part, dev = (
            (p, first, rp),
            (p, second, rp),
            (p, second, lp),
            (p, first, lp),
            (p, whole, sp),
            (lp, first, rp),
            (rp, second, lp),
            (lp, whole, sp),
            (rp, whole, sp),
            (op, whole, sp),
        )[i]
        ref = weights[w].at[who, part, pl.ds(0, NK)]
        return pltpu.make_async_remote_copy(
            ref, ref, w_send.at[w, i], w_recv.at[w, i], device_id=(dev, t), device_id_type=MESH
        )

    def feature_copy(w, group, i):
        along_y = (w == 0) == (group == 0)
        came = 0 if group == 0 else group - 1
        on = (0, 0, 1, 3)[i]
        if along_y:
            holder = ((y + 4 - on) % 4) * 4 + (z + 4 - came) % 4
        else:
            holder = ((y + 4 - came) % 4) * 4 + (z + 4 - on) % 4
        d = (1, 3, 1, 3)[i]
        peer = ((y + d) % 4) * 4 + z if along_y else y * 4 + (z + d) % 4
        ref = feats[w].at[pl.ds(3 * holder, 3)]
        if i >= 2:
            ref = ref.at[:, pl.ds(96 * (i - 2), 96)]
        return pltpu.make_async_remote_copy(
            ref,
            ref,
            x_send.at[w, group, i],
            x_recv.at[w, group, i],
            device_id=(p, peer),
            device_id_type=MESH,
        )

    def grad_copy(w, i):
        own = grads[w]
        src, dst, dev = (
            (own.at[xo, c, first], fwd.at[w, 0], rp),
            (own.at[xo, c, second], fwd.at[w, 1], lp),
            (own.at[xr, c, second], fin.at[w, 0, second], rp),
            (own.at[xl, c, first], fin.at[w, 1, first], lp),
            (own.at[xr, c, first], fin.at[w, 0, first], rp),
            (own.at[xl, c, second], fin.at[w, 1, second], lp),
            (own.at[:, 1 - c, first], sib.at[:, first], sp),
            (own.at[:, 1 - c, second], sib.at[:, second], sp),
        )[i]
        return pltpu.make_async_remote_copy(
            src, dst, g_send.at[w, i], g_recv.at[w, i], device_id=(dev, t), device_id_type=MESH
        )

    def part_copy(w, step, d):
        along_y = (w == 0) == (step == 0)
        peer_y, peer_z = ((y + d) % 4, z) if along_y else (y, (z + d) % 4)
        if step == 0:
            src = parts[w].at[peer_y] if along_y else parts[w].at[:, peer_z]
            dst = f_buf.at[w, d - 1]
        else:
            src = parts[w].at[peer_y, peer_z]
            dst = f_fin.at[w, d - 1]
        return pltpu.make_async_remote_copy(
            src,
            dst,
            f_send.at[w, step, d],
            f_recv.at[w, step, d],
            device_id=(p, peer_y * 4 + peer_z),
            device_id_type=MESH,
        )

    loads = [
        pltpu.make_async_copy(w2_ref, w2in, l_sem.at[0]),
        pltpu.make_async_copy(w1_ref, w1in, l_sem.at[1]),
    ]
    for w, ref in enumerate((tok_ref, cot_ref)):
        for b in range(3):
            loads.append(
                pltpu.make_async_copy(
                    ref.at[:, pl.ds(b * 128, 128)],
                    feats[w].at[3 * t + b],
                    l_sem.at[2 + 3 * w + b],
                )
            )
    for cp in loads:
        cp.start()
    loads[0].wait()

    def lanes_out(i, _):
        s = own_slot_ref[i]
        lanes[i // 16, (i // 4) % 4, i % 4] = w2in[s]
        return 0

    lax.fori_loop(0, 32, lanes_out, 0)
    pl.semaphore_wait(barrier, 9)
    lanes_go(0)
    loads[1].wait()

    def scale_one(g, _):
        for k in range(NK):
            w1all[p, g, k] = (w1in[g, k].astype(F32) * s1_ref[g, k]).astype(BF)
        return 0

    lax.fori_loop(0, NB, scale_one, 0)
    for i in range(5):
        weight_copy(0, i).start()
    w1all[:, :, NK] = jnp.zeros((8, NB, 16, 128), BF)
    w2all[:, :, NK] = jnp.zeros((8, NB, 16, 128), BF)
    for cp in loads[2:]:
        cp.wait()

    def weights_on(w):
        weight_copy(w, 0).wait_recv()
        weight_copy(w, 5).start()
        weight_copy(w, 2).wait_recv()
        weight_copy(w, 6).start()
        weight_copy(w, 1).wait_recv()
        weight_copy(w, 7).start()
        weight_copy(w, 3).wait_recv()
        weight_copy(w, 8).start()

    def weights_last(w):
        weight_copy(w, 5).wait_recv()
        weight_copy(w, 6).wait_recv()
        weight_copy(w, 9).start()

    lanes_turn(0)
    for group in (0, 1):
        for w in range(2):
            for i in range(2):
                feature_copy(w, group, i).start()
    weights_on(0)
    lanes_end(0)

    def scale_two(g, _):
        i = home_lane_ref[g]
        for k in range(NK):
            w2all[p, g, k] = (rbuf[i // 16, (i // 4) % 4, i % 4, k].astype(F32) * s2_ref[g, k]).astype(BF)
        return 0

    lax.fori_loop(0, NB, scale_two, 0)
    for i in range(5):
        weight_copy(1, i).start()

    def feature_on(w, group):
        for i in range(2):
            feature_copy(w, group, i).wait_recv()
            feature_copy(w, group, i + 2).start()
            if group == 0:
                for k in range(2):
                    feature_copy(w, (2, 4)[i], k).start()

    for w in range(2):
        feature_on(w, 0)
    for w in range(2):
        feature_on(w, 1)
    weights_last(0)
    for w in range(2):
        for i in (2, 3):
            feature_copy(w, 0, i).wait_recv()
        for k in range(2):
            feature_copy(w, 3, k).start()
    for group in (2, 4):
        for w in range(2):
            feature_on(w, group)
    weights_on(1)
    for w in range(2):
        feature_on(w, 3)
    for group in range(1, 5):
        for w in range(2):
            for i in (2, 3):
                feature_copy(w, group, i).wait_recv()
    for i in (4, 7, 8, 9):
        weight_copy(0, i).wait_recv()

    def project(g, _):
        w1c = jnp.concatenate([w1all[:, g, k].reshape(128, 128) for k in range(NK)], axis=0)
        xs = jnp.concatenate([xall[rows[g, k]] for k in range(NK)], axis=1)
        pre = jnp.dot(xs, w1c, preferred_element_type=F32)
        th = jnp.tanh(GELU_C * (pre + GELU_A * pre * pre * pre))
        act = (0.5 * pre * (1.0 + th)).astype(BF)
        slope[g] = 0.5 * (1.0 + th) + 0.5 * pre * (1.0 - th * th) * GELU_C * (
            1.0 + 3.0 * GELU_A * pre * pre
        )
        act_all[:, pl.ds(pl.multiple_of(g * 128, 128), 128)] = act
        dys = jnp.concatenate([dyall[cols[g, k]] for k in range(NK)], axis=1)
        gw2 = jnp.dot(act.T, dys, preferred_element_type=F32).astype(BF)
        for k in range(NK):
            g2s[:, :, g, k] = gw2[:, k * 128 : (k + 1) * 128].reshape(4, 2, 16, 128)
        return 0

    lax.fori_loop(0, HALF, project, 0)
    grad_copy(0, 6).start()
    weights_last(1)
    lax.fori_loop(HALF, NB, project, 0)
    grad_copy(0, 7).start()

    def pair_sum(w, chunk, h):
        own = grads[w]

        def body(g, _):
            own[chunk, c, g] = (own[chunk, c, g].astype(F32) + sib[chunk, g].astype(F32)).astype(BF)
            return 0

        lax.fori_loop(h * HALF, (h + 1) * HALF, body, 0)

    def pair_stage(w):
        grad_copy(w, 6).wait_recv()
        pair_sum(w, xo, 0)
        grad_copy(w, 0).start()
        pair_sum(w, xl, 0)
        grad_copy(w, 3).start()
        grad_copy(w, 7).wait_recv()
        pair_sum(w, xo, 1)
        grad_copy(w, 1).start()
        pair_sum(w, xr, 1)
        grad_copy(w, 2).start()
        pair_sum(w, xr, 0)
        pair_sum(w, xl, 1)
        pair_sum(w, x, 0)
        pair_sum(w, x, 1)

    def pass_stage(w):
        own = grads[w]
        grad_copy(w, 0).wait_recv()

        def right(g, _):
            own[xr, c, g] = (own[xr, c, g].astype(F32) + fwd[w, 0, g].astype(F32)).astype(BF)
            return 0

        lax.fori_loop(0, HALF, right, 0)
        grad_copy(w, 4).start()
        grad_copy(w, 1).wait_recv()

        def left(g, _):
            own[xl, c, g + HALF] = (
                own[xl, c, g + HALF].astype(F32) + fwd[w, 1, g].astype(F32)
            ).astype(BF)
            return 0

        lax.fori_loop(0, HALF, left, 0)
        grad_copy(w, 5).start()

    def last_stage(w, out, scale):
        own = grads[w]
        for i in (2, 3, 4, 5):
            grad_copy(w, i).wait_recv()

        def body(g, _):
            for k in range(NK):
                total = own[x, c, g, k].astype(F32) + fin[w, 0, g, k].astype(F32)
                total = total + fin[w, 1, g, k].astype(F32)
                out(g, k, (total * scale[g, k]).astype(BF))
            return 0

        lax.fori_loop(0, NB, body, 0)

    def mix(row):
        def body(i, _):
            j = 12 * row + 2 * i
            panel = jnp.concatenate(
                [
                    jnp.concatenate(
                        [w2all[:, g, kv2[j + b, g]].reshape(128, 128) for g in range(NB)], axis=0
                    )
                    for b in range(2)
                ],
                axis=1,
            )
            res = jnp.dot(act_all[...], panel, preferred_element_type=F32).astype(BF)
            for b in range(2):
                at = 2 * i + b
                m_part[row, at // 3, at % 3] = res[:, b * 128 : (b + 1) * 128]
            return 0

        lax.fori_loop(0, 6, body, 0)

    def back(col):
        def body(i, _):
            at = (2 * i, 2 * i + 1)
            panel = jnp.concatenate(
                [
                    jnp.concatenate(
                        [
                            w1all[:, g, kv1[12 * (a // 3) + 3 * col + a % 3, g]].reshape(128, 128)
                            for g in range(NB)
                        ],
                        axis=1,
                    )
                    for a in at
                ],
                axis=0,
            )
            res = lax.dot_general(dpre_all[...], panel, nt, preferred_element_type=F32).astype(BF)
            for b, a in enumerate(at):
                d_part[a // 3, col, a % 3] = res[:, b * 128 : (b + 1) * 128]
            return 0

        lax.fori_loop(0, 6, body, 0)

    pair_stage(0)
    pl.semaphore_signal(free_sem, inc=1, device_id=(sp, t), device_id_type=MESH)

    def flip(j, _):
        xt[j] = xall[j].T
        return 0

    lax.fori_loop(0, 48, flip, 0)
    for i in (4, 7, 8, 9):
        weight_copy(1, i).wait_recv()

    for d in (2, 1, 3):
        mix((y + d) % 4)
        part_copy(0, 0, d).start()

    def hidden(g, _):
        w2c = jnp.concatenate([w2all[:, g, k].reshape(128, 128) for k in range(NK)], axis=1)
        dys = jnp.concatenate([dyall[cols[g, k]] for k in range(NK)], axis=1)
        dact = lax.dot_general(dys, w2c, nt, preferred_element_type=F32).astype(BF)
        dpre = (dact.astype(F32) * slope[g]).astype(BF)
        dpre_all[:, pl.ds(pl.multiple_of(g * 128, 128), 128)] = dpre
        for k in range(NK):
            gw1 = jnp.dot(xt[rows[g, k]], dpre, preferred_element_type=F32).astype(BF)
            g1s[:, :, g, k] = gw1.reshape(4, 2, 16, 128)
        return 0

    lax.fori_loop(0, HALF, hidden, 0)
    pl.semaphore_wait(free_sem, 1)
    grad_copy(1, 6).start()
    lax.fori_loop(HALF, NB, hidden, 0)
    grad_copy(1, 7).start()
    pass_stage(0)
    pair_stage(1)
    back((z + 2) % 4)
    part_copy(1, 0, 2).start()

    def keep_two(g, k, value):
        g2s[x, c, g, k] = value

    last_stage(0, keep_two, s2_ref)
    lanes_sent(0)

    def lanes_back(i, _):
        s = home_local_ref[i]
        lanes[i // 16, (i // 4) % 4, i % 4] = g2s[x, c, s]
        return 0

    lax.fori_loop(0, 32, lanes_back, 0)
    lanes_go(1)
    for d in (1, 3):
        back((z + d) % 4)
        part_copy(1, 0, d).start()
    pass_stage(1)
    mix(y)
    lanes_turn(1)
    back(z)
    for w in range(2):
        for d in range(1, 4):
            part_copy(w, 0, d).wait_recv()
        part = parts[w]

        def add_four(i, _):
            a, b = i // 3, i % 3
            here = (y, a) if w == 0 else (a, z)
            total = part[here[0], here[1], b].astype(F32)
            for d in range(3):
                total = total + f_buf[w, d, a, b].astype(F32)
            part[here[0], here[1], b] = total.astype(BF)
            return 0

        lax.fori_loop(0, 12, add_four, 0)
        for d in range(1, 4):
            part_copy(w, 1, d).start()
    for w, out in ((0, mixed), (1, dxo)):
        for d in range(1, 4):
            part_copy(w, 1, d).wait_recv()
        for b in range(3):
            total = parts[w][y, z, b].astype(F32)
            for d in range(3):
                total = total + f_fin[w, d, b].astype(F32)
            out[:, b * 128 : (b + 1) * 128] = total.astype(BF)
    lanes_end(1)

    def slot_out(s, _):
        i = slot_lane_ref[s]
        got = rback[i // 16, (i // 4) % 4, i % 4]
        o2[s] = jnp.where(slot_live_ref[s] > 0, got, jnp.zeros_like(got))
        return 0

    lax.fori_loop(0, CAP, slot_out, 0)

    def keep_one(g, k, value):
        o1[g, k] = value

    last_stage(1, keep_one, s1_ref)
    lanes_sent(1)
    for w in range(2):
        for i in range(10):
            weight_copy(w, i).wait_send()
        for group in range(5):
            for i in range(4):
                feature_copy(w, group, i).wait_send()
        for i in range(8):
            grad_copy(w, i).wait_send()
        for step in range(2):
            for d in range(1, 4):
                part_copy(w, step, d).wait_send()


def route_tables(owner, rank):
    index = jnp.arange(192, dtype=jnp.int32)
    source = index // NB
    earlier = index[None, :] < index[:, None]
    same_dest = owner[None, :] == owner[:, None]
    same_src = source[None, :] == source[:, None]
    slot = jnp.sum((earlier & same_dest).astype(jnp.int32), axis=1)
    pair = jnp.sum((earlier & same_dest & same_src).astype(jnp.int32), axis=1)
    mine_first = rank * NB
    mine_owner = lax.dynamic_slice(owner, (mine_first,), (NB,))
    mine_pair = lax.dynamic_slice(pair, (mine_first,), (NB,))
    mine_slot = lax.dynamic_slice(slot, (mine_first,), (NB,))
    home_lane = mine_pair * 16 + mine_owner
    home_q = mine_owner * CAP + mine_slot
    lane = jnp.arange(32, dtype=jnp.int32)
    mine_lane = jnp.where(owner == rank, pair * 16 + source, -1)
    own_slot = jnp.sum(jnp.where(lane[:, None] == mine_lane[None, :], slot[None, :], 0), axis=1)
    home_local = jnp.sum(
        jnp.where(
            lane[:, None] == home_lane[None, :], jnp.arange(NB, dtype=jnp.int32)[None, :], 0
        ),
        axis=1,
    )
    mine_at = jnp.where(owner == rank, slot, -1)
    hit = jnp.arange(CAP, dtype=jnp.int32)[:, None] == mine_at[None, :]
    slot_lane = jnp.sum(jnp.where(hit, (pair * 16 + source)[None, :], 0), axis=1)
    slot_live = jnp.any(hit, axis=1).astype(jnp.int32)
    return home_lane, home_q, own_slot, home_local, slot_lane, slot_live


VM = pl.BlockSpec(memory_space=pltpu.VMEM)
SM = pl.BlockSpec(memory_space=pltpu.SMEM)
ANY = pl.BlockSpec(memory_space=pl.ANY)
SHARD = (NB, NK, 16, 128)
LANES = (2, 4, 4, NK, 16, 128)


def inverse(index):
    k = jnp.arange(NK, dtype=jnp.int32)
    hit = index[None, :, :] == jnp.arange(48, dtype=jnp.int32)[:, None, None]
    return NK + jnp.sum(jnp.where(hit, k[None, None, :] - NK, 0), axis=2)


def local(tokens, cotangent, w1_blocks, w1_rows, w1_scale, w2_blocks, w2_cols, w2_scale, owner):
    rank = lax.axis_index("tensor")
    home_lane, home_q, own_slot, home_local, slot_lane, slot_live = route_tables(owner, rank)
    rows = lax.dynamic_slice(w1_rows, (rank * NB, 0), (NB, NK))
    scale_one = lax.dynamic_slice(w1_scale, (rank * NB, 0), (NB, NK))
    cols = w2_cols[home_q]
    scale_two = w2_scale[home_q]
    dma = pltpu.SemaphoreType.DMA
    part = (4, 4, 3, 192, 128)
    return pl.pallas_call(
        layer_kernel,
        out_shape=[
            jax.ShapeDtypeStruct((192, 384), BF),
            jax.ShapeDtypeStruct((192, 384), BF),
            jax.ShapeDtypeStruct(SHARD, BF),
            jax.ShapeDtypeStruct((CAP, NK, 16, 128), BF),
        ],
        in_specs=[ANY] * 4 + [SM] * 11,
        out_specs=[VM] * 4,
        scratch_shapes=[
            pltpu.VMEM(SHARD, BF),
            pltpu.VMEM((CAP, NK, 16, 128), BF),
            pltpu.VMEM((48, 192, 128), BF),
            pltpu.VMEM((48, 192, 128), BF),
            pltpu.VMEM((8, NB, NK + 1, 16, 128), BF),
            pltpu.VMEM((8, NB, NK + 1, 16, 128), BF),
            pltpu.VMEM(LANES, BF),
            pltpu.VMEM(LANES, BF),
            pltpu.VMEM(LANES, BF),
            pltpu.VMEM((2,) + LANES, BF),
            pltpu.VMEM((48, 128, 192), BF),
            pltpu.VMEM((NB, 192, 128), F32),
            pltpu.VMEM((192, NB * 128), BF),
            pltpu.VMEM((192, NB * 128), BF),
            pltpu.VMEM((4, 2) + SHARD, BF),
            pltpu.VMEM((4, 2) + SHARD, BF),
            pltpu.VMEM((4,) + SHARD, BF),
            pltpu.VMEM((2, 2, HALF, NK, 16, 128), BF),
            pltpu.VMEM((2, 2) + SHARD, BF),
            pltpu.VMEM(part, BF),
            pltpu.VMEM(part, BF),
            pltpu.VMEM((2, 3, 4, 3, 192, 128), BF),
            pltpu.VMEM((2, 3, 3, 192, 128), BF),
            dma((2, 2, 2, 4)),
            dma((2, 2, 2, 4)),
            dma((2, 10)),
            dma((2, 10)),
            dma((2, 5, 4)),
            dma((2, 5, 4)),
            dma((2, 8)),
            dma((2, 8)),
            dma((2, 2, 4)),
            dma((2, 2, 4)),
            dma((8,)),
            pltpu.SemaphoreType.REGULAR,
        ],
        compiler_params=pltpu.CompilerParams(
            collective_id=0, has_side_effects=True, vmem_limit_bytes=(64 << 20) - (64 << 10)
        ),
    )(
        tokens,
        cotangent,
        w1_blocks,
        w2_blocks,
        scale_one,
        scale_two,
        rows,
        cols,
        inverse(rows),
        inverse(cols),
        own_slot,
        home_lane,
        home_local,
        slot_lane,
        slot_live,
    )


def solution(mesh):
    in_specs = (
        P("dp", "tensor"),
        P("dp", "tensor"),
        P("tensor", None, "dp", None),
        P(),
        P(),
        P("tensor", None, "dp", None),
        P(),
        P(),
        P(),
    )
    out_specs = (
        P("dp", "tensor"),
        P("dp", "tensor"),
        P("tensor", None, "dp", None),
        P("tensor", None, "dp", None),
    )
    return jax.shard_map(local, mesh=mesh, in_specs=in_specs, out_specs=out_specs, check_vma=False)
```

```python
import jax
import jax.numpy as jnp
from jax import lax
from jax.experimental import pallas as pl
from jax.experimental.pallas import tpu as pltpu
from jax.sharding import PartitionSpec as P

GELU_C = 0.7978845608028654
GELU_A = 0.044715
MESH = pl.DeviceIdType.MESH
BF = jnp.bfloat16
F32 = jnp.float32
NB = 12
NK = 15
CAP = 18
HALF = NB // 2


def where_am_i():
    p = lax.axis_index("dp")
    t = lax.axis_index("tensor")
    return p, t, p // 2, p % 2, t // 4, t % 4


def enter(p, t, x, c, y, z):
    barrier = pltpu.get_barrier_semaphore()
    for d in range(1, 4):
        for peer in (((y + d) % 4) * 4 + z, y * 4 + (z + d) % 4):
            pl.semaphore_signal(barrier, inc=1, device_id=(p, peer), device_id_type=MESH)
    for q in (2 * ((x + 1) % 4) + c, 2 * ((x + 3) % 4) + c, 2 * x + 1 - c):
        pl.semaphore_signal(barrier, inc=1, device_id=(q, t), device_id_type=MESH)
    return barrier


def layer_kernel(
    tok_ref,
    cot_ref,
    w1_ref,
    w2_ref,
    s1_ref,
    s2_ref,
    rows,
    cols,
    kv1,
    kv2,
    own_slot_ref,
    home_lane_ref,
    home_local_ref,
    slot_lane_ref,
    slot_live_ref,
    mixed,
    dxo,
    o1,
    o2,
    w1in,
    w2in,
    xall,
    dyall,
    w1all,
    w2all,
    lanes,
    rbuf,
    rback,
    middle,
    xt,
    slope,
    act_all,
    dpre_all,
    g1s,
    g2s,
    sib,
    fwd,
    fin,
    m_part,
    d_part,
    f_buf,
    f_fin,
    a_send,
    a_recv,
    w_send,
    w_recv,
    x_send,
    x_recv,
    g_send,
    g_recv,
    f_send,
    f_recv,
    l_sem,
    free_sem,
):
    p, t, x, c, y, z = where_am_i()
    barrier = enter(p, t, x, c, y, z)
    xr, xl, xo = (x + 1) % 4, (x + 3) % 4, (x + 2) % 4
    rp, lp, op, sp = 2 * xr + c, 2 * xl + c, 2 * xo + c, 2 * x + 1 - c
    halves = (pl.ds(0, HALF), pl.ds(HALF, HALF))
    first, second = halves
    whole = pl.ds(0, NB)
    feats = (xall, dyall)
    weights = (w1all, w2all)
    grads = (g2s, g1s)
    parts = (m_part, d_part)
    landed = (rbuf, rback)
    nt = (((1,), (1,)), ((), ()))

    def lane_copy(trip, j, step, d):
        along_y = (j == 0) == (step == 0)
        peer_y, peer_z = ((y + d) % 4, z) if along_y else (y, (z + d) % 4)
        src = lanes.at[j] if step == 0 else middle.at[trip, j]
        dst = middle.at[trip, j] if step == 0 else landed[trip].at[j]
        return pltpu.make_async_remote_copy(
            src.at[peer_y] if along_y else src.at[:, peer_z],
            dst.at[y] if along_y else dst.at[:, z],
            a_send.at[trip, j, step, d],
            a_recv.at[trip, j, step, d],
            device_id=(p, peer_y * 4 + peer_z),
            device_id_type=MESH,
        )

    def lanes_go(trip):
        for d in (2, 1, 3):
            for j in range(2):
                lane_copy(trip, j, 0, d).start()
        middle[trip, 0, y] = lanes[0, y]
        middle[trip, 1, :, z] = lanes[1, :, z]

    def lanes_turn(trip):
        for j in range(2):
            for d in range(1, 4):
                lane_copy(trip, j, 0, d).wait_recv()
            for d in (2, 1, 3):
                lane_copy(trip, j, 1, d).start()
        landed[trip][0, :, z] = middle[trip, 0, :, z]
        landed[trip][1, y] = middle[trip, 1, y]

    def lanes_end(trip):
        for j in range(2):
            for d in range(1, 4):
                lane_copy(trip, j, 1, d).wait_recv()

    def lanes_sent(trip):
        for j in range(2):
            for step in range(2):
                for d in range(1, 4):
                    lane_copy(trip, j, step, d).wait_send()

    def weight_copy(w, i):
        who, part, dev = (
            (p, first, rp),
            (p, second, rp),
            (p, second, lp),
            (p, first, lp),
            (p, whole, sp),
            (lp, first, rp),
            (rp, second, lp),
            (lp, whole, sp),
            (rp, whole, sp),
            (op, whole, sp),
        )[i]
        ref = weights[w].at[who, part, pl.ds(0, NK)]
        return pltpu.make_async_remote_copy(
            ref, ref, w_send.at[w, i], w_recv.at[w, i], device_id=(dev, t), device_id_type=MESH
        )

    def feature_copy(w, group, i):
        along_y = (w == 0) == (group == 0)
        came = 0 if group == 0 else group - 1
        on = (0, 0, 1, 3)[i]
        if along_y:
            holder = ((y + 4 - on) % 4) * 4 + (z + 4 - came) % 4
        else:
            holder = ((y + 4 - came) % 4) * 4 + (z + 4 - on) % 4
        d = (1, 3, 1, 3)[i]
        peer = ((y + d) % 4) * 4 + z if along_y else y * 4 + (z + d) % 4
        ref = feats[w].at[pl.ds(3 * holder, 3)]
        if i >= 2:
            ref = ref.at[:, pl.ds(96 * (i - 2), 96)]
        return pltpu.make_async_remote_copy(
            ref,
            ref,
            x_send.at[w, group, i],
            x_recv.at[w, group, i],
            device_id=(p, peer),
            device_id_type=MESH,
        )

    def grad_copy(w, i):
        own = grads[w]
        src, dst, dev = (
            (own.at[xo, c, first], fwd.at[w, 0], rp),
            (own.at[xo, c, second], fwd.at[w, 1], lp),
            (own.at[xr, c, second], fin.at[w, 0, second], rp),
            (own.at[xl, c, first], fin.at[w, 1, first], lp),
            (own.at[xr, c, first], fin.at[w, 0, first], rp),
            (own.at[xl, c, second], fin.at[w, 1, second], lp),
            (own.at[:, 1 - c, first], sib.at[:, first], sp),
            (own.at[:, 1 - c, second], sib.at[:, second], sp),
        )[i]
        return pltpu.make_async_remote_copy(
            src, dst, g_send.at[w, i], g_recv.at[w, i], device_id=(dev, t), device_id_type=MESH
        )

    def part_copy(w, step, d):
        along_y = (w == 0) == (step == 0)
        peer_y, peer_z = ((y + d) % 4, z) if along_y else (y, (z + d) % 4)
        if step == 0:
            src = parts[w].at[peer_y] if along_y else parts[w].at[:, peer_z]
            dst = f_buf.at[w, d - 1]
        else:
            src = parts[w].at[peer_y, peer_z]
            dst = f_fin.at[w, d - 1]
        return pltpu.make_async_remote_copy(
            src,
            dst,
            f_send.at[w, step, d],
            f_recv.at[w, step, d],
            device_id=(p, peer_y * 4 + peer_z),
            device_id_type=MESH,
        )

    loads = [
        pltpu.make_async_copy(w2_ref, w2in, l_sem.at[0]),
        pltpu.make_async_copy(w1_ref, w1in, l_sem.at[1]),
    ]
    for w, ref in enumerate((tok_ref, cot_ref)):
        for b in range(3):
            loads.append(
                pltpu.make_async_copy(
                    ref.at[:, pl.ds(b * 128, 128)],
                    feats[w].at[3 * t + b],
                    l_sem.at[2 + 3 * w + b],
                )
            )
    for cp in loads:
        cp.start()
    loads[0].wait()

    def lanes_out(i, _):
        s = own_slot_ref[i]
        lanes[i // 16, (i // 4) % 4, i % 4] = w2in[s]
        return 0

    lax.fori_loop(0, 32, lanes_out, 0)
    pl.semaphore_wait(barrier, 9)
    lanes_go(0)
    loads[1].wait()

    def scale_one(g, _):
        for k in range(NK):
            w1all[p, g, k] = (w1in[g, k].astype(F32) * s1_ref[g, k]).astype(BF)
        return 0

    lax.fori_loop(0, NB, scale_one, 0)
    for i in range(5):
        weight_copy(0, i).start()
    w1all[:, :, NK] = jnp.zeros((8, NB, 16, 128), BF)
    w2all[:, :, NK] = jnp.zeros((8, NB, 16, 128), BF)
    for cp in loads[2:]:
        cp.wait()

    def weights_on(w):
        weight_copy(w, 0).wait_recv()
        weight_copy(w, 5).start()
        weight_copy(w, 2).wait_recv()
        weight_copy(w, 6).start()
        weight_copy(w, 1).wait_recv()
        weight_copy(w, 7).start()
        weight_copy(w, 3).wait_recv()
        weight_copy(w, 8).start()

    def weights_last(w):
        weight_copy(w, 5).wait_recv()
        weight_copy(w, 6).wait_recv()
        weight_copy(w, 9).start()

    lanes_turn(0)
    for group in (0, 1):
        for w in range(2):
            for i in range(2):
                feature_copy(w, group, i).start()
    weights_on(0)
    lanes_end(0)

    def scale_two(g, _):
        i = home_lane_ref[g]
        for k in range(NK):
            w2all[p, g, k] = (rbuf[i // 16, (i // 4) % 4, i % 4, k].astype(F32) * s2_ref[g, k]).astype(BF)
        return 0

    lax.fori_loop(0, NB, scale_two, 0)
    for i in range(5):
        weight_copy(1, i).start()

    def feature_on(w, group):
        for i in range(2):
            feature_copy(w, group, i).wait_recv()
            feature_copy(w, group, i + 2).start()
            if group == 0:
                for k in range(2):
                    feature_copy(w, (2, 4)[i], k).start()

    for w in range(2):
        feature_on(w, 0)
    for w in range(2):
        feature_on(w, 1)
    weights_last(0)
    for w in range(2):
        for i in (2, 3):
            feature_copy(w, 0, i).wait_recv()
        for k in range(2):
            feature_copy(w, 3, k).start()
    for group in (2, 4):
        for w in range(2):
            feature_on(w, group)
    weights_on(1)
    for w in range(2):
        feature_on(w, 3)
    for group in range(1, 5):
        for w in range(2):
            for i in (2, 3):
                feature_copy(w, group, i).wait_recv()
    for i in (4, 7, 8, 9):
        weight_copy(0, i).wait_recv()

    def project(g, _):
        w1c = jnp.concatenate([w1all[:, g, k].reshape(128, 128) for k in range(NK)], axis=0)
        xs = jnp.concatenate([xall[rows[g, k]] for k in range(NK)], axis=1)
        pre = jnp.dot(xs, w1c, preferred_element_type=F32)
        th = jnp.tanh(GELU_C * (pre + GELU_A * pre * pre * pre))
        act = (0.5 * pre * (1.0 + th)).astype(BF)
        slope[g] = 0.5 * (1.0 + th) + 0.5 * pre * (1.0 - th * th) * GELU_C * (
            1.0 + 3.0 * GELU_A * pre * pre
        )
        act_all[:, pl.ds(pl.multiple_of(g * 128, 128), 128)] = act
        dys = jnp.concatenate([dyall[cols[g, k]] for k in range(NK)], axis=1)
        gw2 = jnp.dot(act.T, dys, preferred_element_type=F32).astype(BF)
        for k in range(NK):
            g2s[:, :, g, k] = gw2[:, k * 128 : (k + 1) * 128].reshape(4, 2, 16, 128)
        return 0

    def flip(j, _):
        xt[j] = xall[j].T
        return 0

    lax.fori_loop(0, HALF, project, 0)
    grad_copy(0, 6).start()
    weights_last(1)
    lax.fori_loop(HALF, NB, project, 0)
    grad_copy(0, 7).start()
    lax.fori_loop(0, 48, flip, 0)

    def pair_sum(w, chunk, h):
        own = grads[w]

        def body(g, _):
            own[chunk, c, g] = (own[chunk, c, g].astype(F32) + sib[chunk, g].astype(F32)).astype(BF)
            return 0

        lax.fori_loop(h * HALF, (h + 1) * HALF, body, 0)

    def pair_stage(w):
        grad_copy(w, 6).wait_recv()
        pair_sum(w, xo, 0)
        grad_copy(w, 0).start()
        pair_sum(w, xl, 0)
        grad_copy(w, 3).start()
        grad_copy(w, 7).wait_recv()
        pair_sum(w, xo, 1)
        grad_copy(w, 1).start()
        pair_sum(w, xr, 1)
        grad_copy(w, 2).start()
        pair_sum(w, xr, 0)
        pair_sum(w, xl, 1)
        pair_sum(w, x, 0)
        pair_sum(w, x, 1)

    def pass_stage(w):
        own = grads[w]
        grad_copy(w, 0).wait_recv()

        def right(g, _):
            own[xr, c, g] = (own[xr, c, g].astype(F32) + fwd[w, 0, g].astype(F32)).astype(BF)
            return 0

        lax.fori_loop(0, HALF, right, 0)
        grad_copy(w, 4).start()
        grad_copy(w, 1).wait_recv()

        def left(g, _):
            own[xl, c, g + HALF] = (
                own[xl, c, g + HALF].astype(F32) + fwd[w, 1, g].astype(F32)
            ).astype(BF)
            return 0

        lax.fori_loop(0, HALF, left, 0)
        grad_copy(w, 5).start()

    def last_stage(w, out, scale):
        own = grads[w]
        for i in (2, 3, 4, 5):
            grad_copy(w, i).wait_recv()

        def body(g, _):
            for k in range(NK):
                total = own[x, c, g, k].astype(F32) + fin[w, 0, g, k].astype(F32)
                total = total + fin[w, 1, g, k].astype(F32)
                out(g, k, (total * scale[g, k]).astype(BF))
            return 0

        lax.fori_loop(0, NB, body, 0)

    def mix(row):
        def body(i, _):
            j = 12 * row + 2 * i
            panel = jnp.concatenate(
                [
                    jnp.concatenate(
                        [w2all[:, g, kv2[j + b, g]].reshape(128, 128) for g in range(NB)], axis=0
                    )
                    for b in range(2)
                ],
                axis=1,
            )
            res = jnp.dot(act_all[...], panel, preferred_element_type=F32).astype(BF)
            for b in range(2):
                at = 2 * i + b
                m_part[row, at // 3, at % 3] = res[:, b * 128 : (b + 1) * 128]
            return 0

        lax.fori_loop(0, 6, body, 0)

    def back(col):
        def body(i, _):
            at = (2 * i, 2 * i + 1)
            panel = jnp.concatenate(
                [
                    jnp.concatenate(
                        [
                            w1all[:, g, kv1[12 * (a // 3) + 3 * col + a % 3, g]].reshape(128, 128)
                            for g in range(NB)
                        ],
                        axis=1,
                    )
                    for a in at
                ],
                axis=0,
            )
            res = lax.dot_general(dpre_all[...], panel, nt, preferred_element_type=F32).astype(BF)
            for b, a in enumerate(at):
                d_part[a // 3, col, a % 3] = res[:, b * 128 : (b + 1) * 128]
            return 0

        lax.fori_loop(0, 6, body, 0)

    for i in (4, 7, 8, 9):
        weight_copy(1, i).wait_recv()
    mix((y + 2) % 4)
    part_copy(0, 0, 2).start()
    pair_stage(0)
    pl.semaphore_signal(free_sem, inc=1, device_id=(sp, t), device_id_type=MESH)
    for d in (1, 3):
        mix((y + d) % 4)
        part_copy(0, 0, d).start()

    def hidden(g, _):
        w2c = jnp.concatenate([w2all[:, g, k].reshape(128, 128) for k in range(NK)], axis=1)
        dys = jnp.concatenate([dyall[cols[g, k]] for k in range(NK)], axis=1)
        dact = lax.dot_general(dys, w2c, nt, preferred_element_type=F32).astype(BF)
        dpre = (dact.astype(F32) * slope[g]).astype(BF)
        dpre_all[:, pl.ds(pl.multiple_of(g * 128, 128), 128)] = dpre
        return 0

    def grad_one(g, _):
        dpre = dpre_all[:, pl.ds(pl.multiple_of(g * 128, 128), 128)]
        for k in range(NK):
            gw1 = jnp.dot(xt[rows[g, k]], dpre, preferred_element_type=F32).astype(BF)
            g1s[:, :, g, k] = gw1.reshape(4, 2, 16, 128)
        return 0

    def keep_two(g, k, value):
        g2s[x, c, g, k] = value

    def lanes_back(i, _):
        s = home_local_ref[i]
        lanes[i // 16, (i // 4) % 4, i % 4] = g2s[x, c, s]
        return 0

    lax.fori_loop(0, NB, hidden, 0)
    back((z + 2) % 4)
    part_copy(1, 0, 2).start()
    pass_stage(0)
    for d in (1, 3):
        back((z + d) % 4)
        part_copy(1, 0, d).start()
    lax.fori_loop(0, HALF, grad_one, 0)
    pl.semaphore_wait(free_sem, 1)
    grad_copy(1, 6).start()
    last_stage(0, keep_two, s2_ref)
    lanes_sent(0)
    lax.fori_loop(0, 32, lanes_back, 0)
    lanes_go(1)
    lax.fori_loop(HALF, NB, grad_one, 0)
    grad_copy(1, 7).start()
    mix(y)
    pair_stage(1)
    back(z)
    lanes_turn(1)
    for w in range(2):
        for d in range(1, 4):
            part_copy(w, 0, d).wait_recv()
        part = parts[w]

        def add_four(i, _):
            a, b = i // 3, i % 3
            here = (y, a) if w == 0 else (a, z)
            total = part[here[0], here[1], b].astype(F32)
            for d in range(3):
                total = total + f_buf[w, d, a, b].astype(F32)
            part[here[0], here[1], b] = total.astype(BF)
            return 0

        lax.fori_loop(0, 12, add_four, 0)
        for d in range(1, 4):
            part_copy(w, 1, d).start()
    pass_stage(1)
    for w, out in ((0, mixed), (1, dxo)):
        for d in range(1, 4):
            part_copy(w, 1, d).wait_recv()
        for b in range(3):
            total = parts[w][y, z, b].astype(F32)
            for d in range(3):
                total = total + f_fin[w, d, b].astype(F32)
            out[:, b * 128 : (b + 1) * 128] = total.astype(BF)
    lanes_end(1)

    def slot_out(s, _):
        i = slot_lane_ref[s]
        got = rback[i // 16, (i // 4) % 4, i % 4]
        o2[s] = jnp.where(slot_live_ref[s] > 0, got, jnp.zeros_like(got))
        return 0

    lax.fori_loop(0, CAP, slot_out, 0)

    def keep_one(g, k, value):
        o1[g, k] = value

    last_stage(1, keep_one, s1_ref)
    lanes_sent(1)
    for w in range(2):
        for i in range(10):
            weight_copy(w, i).wait_send()
        for group in range(5):
            for i in range(4):
                feature_copy(w, group, i).wait_send()
        for i in range(8):
            grad_copy(w, i).wait_send()
        for step in range(2):
            for d in range(1, 4):
                part_copy(w, step, d).wait_send()


def route_tables(owner, rank):
    index = jnp.arange(192, dtype=jnp.int32)
    source = index // NB
    earlier = index[None, :] < index[:, None]
    same_dest = owner[None, :] == owner[:, None]
    same_src = source[None, :] == source[:, None]
    slot = jnp.sum((earlier & same_dest).astype(jnp.int32), axis=1)
    pair = jnp.sum((earlier & same_dest & same_src).astype(jnp.int32), axis=1)
    mine_first = rank * NB
    mine_owner = lax.dynamic_slice(owner, (mine_first,), (NB,))
    mine_pair = lax.dynamic_slice(pair, (mine_first,), (NB,))
    mine_slot = lax.dynamic_slice(slot, (mine_first,), (NB,))
    home_lane = mine_pair * 16 + mine_owner
    home_q = mine_owner * CAP + mine_slot
    lane = jnp.arange(32, dtype=jnp.int32)
    mine_lane = jnp.where(owner == rank, pair * 16 + source, -1)
    own_slot = jnp.sum(jnp.where(lane[:, None] == mine_lane[None, :], slot[None, :], 0), axis=1)
    home_local = jnp.sum(
        jnp.where(
            lane[:, None] == home_lane[None, :], jnp.arange(NB, dtype=jnp.int32)[None, :], 0
        ),
        axis=1,
    )
    mine_at = jnp.where(owner == rank, slot, -1)
    hit = jnp.arange(CAP, dtype=jnp.int32)[:, None] == mine_at[None, :]
    slot_lane = jnp.sum(jnp.where(hit, (pair * 16 + source)[None, :], 0), axis=1)
    slot_live = jnp.any(hit, axis=1).astype(jnp.int32)
    return home_lane, home_q, own_slot, home_local, slot_lane, slot_live


def hand_over(*refs):
    sem = refs[8]
    copies = [pltpu.make_async_copy(refs[i], refs[4 + i], sem.at[i]) for i in range(4)]
    for cp in copies:
        cp.start()
    for cp in copies:
        cp.wait()


VM = pl.BlockSpec(memory_space=pltpu.VMEM)
SM = pl.BlockSpec(memory_space=pltpu.SMEM)
ANY = pl.BlockSpec(memory_space=pl.ANY)
SHARD = (NB, NK, 16, 128)
LANES = (2, 4, 4, NK, 16, 128)


def inverse(index):
    k = jnp.arange(NK, dtype=jnp.int32)
    hit = index[None, :, :] == jnp.arange(48, dtype=jnp.int32)[:, None, None]
    return NK + jnp.sum(jnp.where(hit, k[None, None, :] - NK, 0), axis=2)


def local(tokens, cotangent, w1_blocks, w1_rows, w1_scale, w2_blocks, w2_cols, w2_scale, owner):
    rank = lax.axis_index("tensor")
    home_lane, home_q, own_slot, home_local, slot_lane, slot_live = route_tables(owner, rank)
    rows = lax.dynamic_slice(w1_rows, (rank * NB, 0), (NB, NK))
    scale_one = lax.dynamic_slice(w1_scale, (rank * NB, 0), (NB, NK))
    cols = w2_cols[home_q]
    scale_two = w2_scale[home_q]
    dma = pltpu.SemaphoreType.DMA
    part = (4, 4, 3, 192, 128)
    outs = [
        jax.ShapeDtypeStruct((192, 384), BF),
        jax.ShapeDtypeStruct((192, 384), BF),
        jax.ShapeDtypeStruct(SHARD, BF),
        jax.ShapeDtypeStruct((CAP, NK, 16, 128), BF),
    ]
    results = pl.pallas_call(
        layer_kernel,
        out_shape=outs,
        in_specs=[ANY] * 4 + [SM] * 11,
        out_specs=[VM] * 4,
        scratch_shapes=[
            pltpu.VMEM(SHARD, BF),
            pltpu.VMEM((CAP, NK, 16, 128), BF),
            pltpu.VMEM((48, 192, 128), BF),
            pltpu.VMEM((48, 192, 128), BF),
            pltpu.VMEM((8, NB, NK + 1, 16, 128), BF),
            pltpu.VMEM((8, NB, NK + 1, 16, 128), BF),
            pltpu.VMEM(LANES, BF),
            pltpu.VMEM(LANES, BF),
            pltpu.VMEM(LANES, BF),
            pltpu.VMEM((2,) + LANES, BF),
            pltpu.VMEM((48, 128, 192), BF),
            pltpu.VMEM((NB, 192, 128), F32),
            pltpu.VMEM((192, NB * 128), BF),
            pltpu.VMEM((192, NB * 128), BF),
            pltpu.VMEM((4, 2) + SHARD, BF),
            pltpu.VMEM((4, 2) + SHARD, BF),
            pltpu.VMEM((4,) + SHARD, BF),
            pltpu.VMEM((2, 2, HALF, NK, 16, 128), BF),
            pltpu.VMEM((2, 2) + SHARD, BF),
            pltpu.VMEM(part, BF),
            pltpu.VMEM(part, BF),
            pltpu.VMEM((2, 3, 4, 3, 192, 128), BF),
            pltpu.VMEM((2, 3, 3, 192, 128), BF),
            dma((2, 2, 2, 4)),
            dma((2, 2, 2, 4)),
            dma((2, 10)),
            dma((2, 10)),
            dma((2, 5, 4)),
            dma((2, 5, 4)),
            dma((2, 8)),
            dma((2, 8)),
            dma((2, 2, 4)),
            dma((2, 2, 4)),
            dma((8,)),
            pltpu.SemaphoreType.REGULAR,
        ],
        compiler_params=pltpu.CompilerParams(
            collective_id=0, has_side_effects=True, vmem_limit_bytes=(64 << 20) - (64 << 10)
        ),
    )(
        tokens,
        cotangent,
        w1_blocks,
        w2_blocks,
        scale_one,
        scale_two,
        rows,
        cols,
        inverse(rows),
        inverse(cols),
        own_slot,
        home_lane,
        home_local,
        slot_lane,
        slot_live,
    )
    return pl.pallas_call(
        hand_over,
        out_shape=outs,
        in_specs=[ANY] * 4,
        out_specs=[ANY] * 4,
        scratch_shapes=[dma((4,))],
    )(*results)


def solution(mesh):
    in_specs = (
        P("dp", "tensor"),
        P("dp", "tensor"),
        P("tensor", None, "dp", None),
        P(),
        P(),
        P("tensor", None, "dp", None),
        P(),
        P(),
        P(),
    )
    out_specs = (
        P("dp", "tensor"),
        P("dp", "tensor"),
        P("tensor", None, "dp", None),
        P("tensor", None, "dp", None),
    )
    return jax.shard_map(local, mesh=mesh, in_specs=in_specs, out_specs=out_specs, check_vma=False)
```

```python
import jax
import jax.numpy as jnp
from jax import lax
from jax.experimental import pallas as pl
from jax.experimental.pallas import tpu as pltpu
from jax.sharding import PartitionSpec as P

GELU_C = 0.7978845608028654
GELU_A = 0.044715
MESH = pl.DeviceIdType.MESH
BF = jnp.bfloat16
F32 = jnp.float32
NB = 12
NK = 15
CAP = 18
HALF = NB // 2


def where_am_i():
    p = lax.axis_index("dp")
    t = lax.axis_index("tensor")
    return p, t, p // 2, p % 2, t // 4, t % 4


def enter(p, t, x, c, y, z):
    barrier = pltpu.get_barrier_semaphore()
    for d in range(1, 4):
        for peer in (((y + d) % 4) * 4 + z, y * 4 + (z + d) % 4):
            pl.semaphore_signal(barrier, inc=1, device_id=(p, peer), device_id_type=MESH)
    for q in (2 * ((x + 1) % 4) + c, 2 * ((x + 3) % 4) + c, 2 * x + 1 - c):
        pl.semaphore_signal(barrier, inc=1, device_id=(q, t), device_id_type=MESH)
    return barrier


def layer_kernel(
    tok_ref,
    cot_ref,
    w1_ref,
    w2_ref,
    s1_ref,
    s2_ref,
    rows_ref,
    cols_ref,
    tab,
    kv_ref,
    mixed,
    dxo,
    o1,
    o2,
    w1in,
    w2in,
    xall,
    dyall,
    w1all,
    w2all,
    lanes,
    rbuf,
    rback,
    middle,
    xt,
    slope,
    act_all,
    dpre_all,
    g1s,
    g2s,
    sib,
    fwd,
    fin,
    m_part,
    d_part,
    f_buf,
    f_fin,
    a_send,
    a_recv,
    w_send,
    w_recv,
    x_send,
    x_recv,
    g_send,
    g_recv,
    f_send,
    f_recv,
    l_sem,
    free_sem,
):
    p, t, x, c, y, z = where_am_i()
    barrier = enter(p, t, x, c, y, z)
    xr, xl, xo = (x + 1) % 4, (x + 3) % 4, (x + 2) % 4
    rp, lp, op, sp = 2 * xr + c, 2 * xl + c, 2 * xo + c, 2 * x + 1 - c
    halves = (pl.ds(0, HALF), pl.ds(HALF, HALF))
    first, second = halves
    whole = pl.ds(0, NB)
    feats = (xall, dyall)
    weights = (w1all, w2all)
    grads = (g2s, g1s)
    parts = (m_part, d_part)
    landed = (rbuf, rback)
    nt = (((1,), (1,)), ((), ()))

    def row(g, k):
        return rows_ref[k, t * NB + g]

    def col(g, k):
        return cols_ref[k, tab[HOME_Q + g]]

    def scale1(g, k):
        return s1_ref[k, t * NB + g]

    def scale2(g, k):
        return s2_ref[k, tab[HOME_Q + g]]

    def lane_copy(trip, j, step, d):
        along_y = (j == 0) == (step == 0)
        peer_y, peer_z = ((y + d) % 4, z) if along_y else (y, (z + d) % 4)
        src = lanes.at[j] if step == 0 else middle.at[trip, j]
        dst = middle.at[trip, j] if step == 0 else landed[trip].at[j]
        return pltpu.make_async_remote_copy(
            src.at[peer_y] if along_y else src.at[:, peer_z],
            dst.at[y] if along_y else dst.at[:, z],
            a_send.at[trip, j, step, d],
            a_recv.at[trip, j, step, d],
            device_id=(p, peer_y * 4 + peer_z),
            device_id_type=MESH,
        )

    def lanes_go(trip):
        for d in (2, 1, 3):
            for j in range(2):
                lane_copy(trip, j, 0, d).start()
        middle[trip, 0, y] = lanes[0, y]
        middle[trip, 1, :, z] = lanes[1, :, z]

    def lanes_turn(trip):
        for j in range(2):
            for d in range(1, 4):
                lane_copy(trip, j, 0, d).wait_recv()
            for d in (2, 1, 3):
                lane_copy(trip, j, 1, d).start()
        landed[trip][0, :, z] = middle[trip, 0, :, z]
        landed[trip][1, y] = middle[trip, 1, y]

    def lanes_end(trip):
        for j in range(2):
            for d in range(1, 4):
                lane_copy(trip, j, 1, d).wait_recv()

    def lanes_sent(trip):
        for j in range(2):
            for step in range(2):
                for d in range(1, 4):
                    lane_copy(trip, j, step, d).wait_send()

    def weight_copy(w, i):
        who, part, dev = (
            (p, first, rp),
            (p, second, rp),
            (p, second, lp),
            (p, first, lp),
            (p, whole, sp),
            (lp, first, rp),
            (rp, second, lp),
            (lp, whole, sp),
            (rp, whole, sp),
            (op, whole, sp),
        )[i]
        ref = weights[w].at[who, part, pl.ds(0, NK)]
        return pltpu.make_async_remote_copy(
            ref, ref, w_send.at[w, i], w_recv.at[w, i], device_id=(dev, t), device_id_type=MESH
        )

    def feature_copy(w, group, i):
        along_y = (w == 0) == (group == 0)
        came = 0 if group == 0 else group - 1
        on = (0, 0, 1, 3)[i]
        if along_y:
            holder = ((y + 4 - on) % 4) * 4 + (z + 4 - came) % 4
        else:
            holder = ((y + 4 - came) % 4) * 4 + (z + 4 - on) % 4
        d = (1, 3, 1, 3)[i]
        peer = ((y + d) % 4) * 4 + z if along_y else y * 4 + (z + d) % 4
        ref = feats[w].at[pl.ds(3 * holder, 3)]
        if i >= 2:
            ref = ref.at[:, pl.ds(96 * (i - 2), 96)]
        return pltpu.make_async_remote_copy(
            ref,
            ref,
            x_send.at[w, group, i],
            x_recv.at[w, group, i],
            device_id=(p, peer),
            device_id_type=MESH,
        )

    def grad_copy(w, i):
        own = grads[w]
        src, dst, dev = (
            (own.at[xo, c, first], fwd.at[w, 0], rp),
            (own.at[xo, c, second], fwd.at[w, 1], lp),
            (own.at[xr, c, second], fin.at[w, 0, second], rp),
            (own.at[xl, c, first], fin.at[w, 1, first], lp),
            (own.at[xr, c, first], fin.at[w, 0, first], rp),
            (own.at[xl, c, second], fin.at[w, 1, second], lp),
            (own.at[:, 1 - c, first], sib.at[:, first], sp),
            (own.at[:, 1 - c, second], sib.at[:, second], sp),
        )[i]
        return pltpu.make_async_remote_copy(
            src, dst, g_send.at[w, i], g_recv.at[w, i], device_id=(dev, t), device_id_type=MESH
        )

    def part_copy(w, step, d):
        along_y = (w == 0) == (step == 0)
        peer_y, peer_z = ((y + d) % 4, z) if along_y else (y, (z + d) % 4)
        if step == 0:
            src = parts[w].at[peer_y] if along_y else parts[w].at[:, peer_z]
            dst = f_buf.at[w, d - 1]
        else:
            src = parts[w].at[peer_y, peer_z]
            dst = f_fin.at[w, d - 1]
        return pltpu.make_async_remote_copy(
            src,
            dst,
            f_send.at[w, step, d],
            f_recv.at[w, step, d],
            device_id=(p, peer_y * 4 + peer_z),
            device_id_type=MESH,
        )

    loads = [
        pltpu.make_async_copy(w2_ref, w2in, l_sem.at[0]),
        pltpu.make_async_copy(w1_ref, w1in, l_sem.at[1]),
    ]
    for w, ref in enumerate((tok_ref, cot_ref)):
        for b in range(3):
            loads.append(
                pltpu.make_async_copy(
                    ref.at[:, pl.ds(b * 128, 128)],
                    feats[w].at[3 * t + b],
                    l_sem.at[2 + 3 * w + b],
                )
            )
    for cp in loads:
        cp.start()
    loads[0].wait()

    def lanes_out(i, _):
        s = tab[OWN_SLOT + i]
        lanes[i // 16, (i // 4) % 4, i % 4] = w2in[s]
        return 0

    lax.fori_loop(0, 32, lanes_out, 0)
    pl.semaphore_wait(barrier, 9)
    lanes_go(0)
    loads[1].wait()

    def scale_one(g, _):
        for k in range(NK):
            w1all[p, g, k] = (w1in[g, k].astype(F32) * scale1(g, k)).astype(BF)
        return 0

    lax.fori_loop(0, NB, scale_one, 0)
    for i in range(5):
        weight_copy(0, i).start()
    w1all[:, :, NK] = jnp.zeros((8, NB, 16, 128), BF)
    w2all[:, :, NK] = jnp.zeros((8, NB, 16, 128), BF)
    for cp in loads[2:]:
        cp.wait()

    def weights_on(w):
        weight_copy(w, 0).wait_recv()
        weight_copy(w, 5).start()
        weight_copy(w, 2).wait_recv()
        weight_copy(w, 6).start()
        weight_copy(w, 1).wait_recv()
        weight_copy(w, 7).start()
        weight_copy(w, 3).wait_recv()
        weight_copy(w, 8).start()

    def weights_last(w):
        weight_copy(w, 5).wait_recv()
        weight_copy(w, 6).wait_recv()
        weight_copy(w, 9).start()

    lanes_turn(0)
    for group in (0, 1):
        for w in range(2):
            for i in range(2):
                feature_copy(w, group, i).start()
    weights_on(0)
    lanes_end(0)

    def scale_two(g, _):
        i = tab[HOME_LANE + g]
        for k in range(NK):
            w2all[p, g, k] = (rbuf[i // 16, (i // 4) % 4, i % 4, k].astype(F32) * scale2(g, k)).astype(BF)
        return 0

    lax.fori_loop(0, NB, scale_two, 0)
    for i in range(5):
        weight_copy(1, i).start()

    def feature_on(w, group):
        for i in range(2):
            feature_copy(w, group, i).wait_recv()
            feature_copy(w, group, i + 2).start()
            if group == 0:
                for k in range(2):
                    feature_copy(w, (2, 4)[i], k).start()

    for w in range(2):
        feature_on(w, 0)
    for w in range(2):
        feature_on(w, 1)
    weights_last(0)
    for w in range(2):
        for i in (2, 3):
            feature_copy(w, 0, i).wait_recv()
        for k in range(2):
            feature_copy(w, 3, k).start()
    for group in (2, 4):
        for w in range(2):
            feature_on(w, group)
    weights_on(1)
    for w in range(2):
        feature_on(w, 3)
    for group in range(1, 5):
        for w in range(2):
            for i in (2, 3):
                feature_copy(w, group, i).wait_recv()
    for i in (4, 7, 8, 9):
        weight_copy(0, i).wait_recv()

    def project(g, _):
        w1c = jnp.concatenate([w1all[:, g, k].reshape(128, 128) for k in range(NK)], axis=0)
        xs = jnp.concatenate([xall[row(g, k)] for k in range(NK)], axis=1)
        pre = jnp.dot(xs, w1c, preferred_element_type=F32)
        th = jnp.tanh(GELU_C * (pre + GELU_A * pre * pre * pre))
        act = (0.5 * pre * (1.0 + th)).astype(BF)
        slope[g] = 0.5 * (1.0 + th) + 0.5 * pre * (1.0 - th * th) * GELU_C * (
            1.0 + 3.0 * GELU_A * pre * pre
        )
        act_all[:, pl.ds(pl.multiple_of(g * 128, 128), 128)] = act
        dys = jnp.concatenate([dyall[col(g, k)] for k in range(NK)], axis=1)
        gw2 = jnp.dot(act.T, dys, preferred_element_type=F32).astype(BF)
        for k in range(NK):
            g2s[:, :, g, k] = gw2[:, k * 128 : (k + 1) * 128].reshape(4, 2, 16, 128)
        return 0

    def flip(j, _):
        xt[j] = xall[j].T
        return 0

    lax.fori_loop(0, HALF, project, 0)
    grad_copy(0, 6).start()
    weights_last(1)
    lax.fori_loop(HALF, NB, project, 0)
    grad_copy(0, 7).start()
    lax.fori_loop(0, 48, flip, 0)

    def pair_sum(w, chunk, h):
        own = grads[w]

        def body(g, _):
            own[chunk, c, g] = (own[chunk, c, g].astype(F32) + sib[chunk, g].astype(F32)).astype(BF)
            return 0

        lax.fori_loop(h * HALF, (h + 1) * HALF, body, 0)

    def pair_stage(w):
        grad_copy(w, 6).wait_recv()
        pair_sum(w, xo, 0)
        grad_copy(w, 0).start()
        pair_sum(w, xl, 0)
        grad_copy(w, 3).start()
        grad_copy(w, 7).wait_recv()
        pair_sum(w, xo, 1)
        grad_copy(w, 1).start()
        pair_sum(w, xr, 1)
        grad_copy(w, 2).start()
        pair_sum(w, xr, 0)
        pair_sum(w, xl, 1)
        pair_sum(w, x, 0)
        pair_sum(w, x, 1)

    def pass_stage(w):
        own = grads[w]
        grad_copy(w, 0).wait_recv()

        def right(g, _):
            own[xr, c, g] = (own[xr, c, g].astype(F32) + fwd[w, 0, g].astype(F32)).astype(BF)
            return 0

        lax.fori_loop(0, HALF, right, 0)
        grad_copy(w, 4).start()
        grad_copy(w, 1).wait_recv()

        def left(g, _):
            own[xl, c, g + HALF] = (
                own[xl, c, g + HALF].astype(F32) + fwd[w, 1, g].astype(F32)
            ).astype(BF)
            return 0

        lax.fori_loop(0, HALF, left, 0)
        grad_copy(w, 5).start()

    def last_stage(w, out, scale):
        own = grads[w]
        for i in (2, 3, 4, 5):
            grad_copy(w, i).wait_recv()

        def body(g, _):
            for k in range(NK):
                total = own[x, c, g, k].astype(F32) + fin[w, 0, g, k].astype(F32)
                total = total + fin[w, 1, g, k].astype(F32)
                out(g, k, (total * scale(g, k)).astype(BF))
            return 0

        lax.fori_loop(0, NB, body, 0)

    def mix(to_y):
        def body(i, _):
            j = 12 * to_y + 2 * i
            panel = jnp.concatenate(
                [
                    jnp.concatenate(
                        [w2all[:, g, kv_ref[NB + g, j + b]].reshape(128, 128) for g in range(NB)], axis=0
                    )
                    for b in range(2)
                ],
                axis=1,
            )
            res = jnp.dot(act_all[...], panel, preferred_element_type=F32).astype(BF)
            for b in range(2):
                at = 2 * i + b
                m_part[to_y, at // 3, at % 3] = res[:, b * 128 : (b + 1) * 128]
            return 0

        lax.fori_loop(0, 6, body, 0)

    def back(to_z):
        def body(i, _):
            at = (2 * i, 2 * i + 1)
            panel = jnp.concatenate(
                [
                    jnp.concatenate(
                        [
                            w1all[:, g, kv_ref[g, 12 * (a // 3) + 3 * to_z + a % 3]].reshape(128, 128)
                            for g in range(NB)
                        ],
                        axis=1,
                    )
                    for a in at
                ],
                axis=0,
            )
            res = lax.dot_general(dpre_all[...], panel, nt, preferred_element_type=F32).astype(BF)
            for b, a in enumerate(at):
                d_part[a // 3, to_z, a % 3] = res[:, b * 128 : (b + 1) * 128]
            return 0

        lax.fori_loop(0, 6, body, 0)

    for i in (4, 7, 8, 9):
        weight_copy(1, i).wait_recv()
    mix((y + 2) % 4)
    part_copy(0, 0, 2).start()
    pair_stage(0)
    pl.semaphore_signal(free_sem, inc=1, device_id=(sp, t), device_id_type=MESH)
    for d in (1, 3):
        mix((y + d) % 4)
        part_copy(0, 0, d).start()

    def hidden(g, _):
        w2c = jnp.concatenate([w2all[:, g, k].reshape(128, 128) for k in range(NK)], axis=1)
        dys = jnp.concatenate([dyall[col(g, k)] for k in range(NK)], axis=1)
        dact = lax.dot_general(dys, w2c, nt, preferred_element_type=F32).astype(BF)
        dpre = (dact.astype(F32) * slope[g]).astype(BF)
        dpre_all[:, pl.ds(pl.multiple_of(g * 128, 128), 128)] = dpre
        return 0

    def grad_one(g, _):
        dpre = dpre_all[:, pl.ds(pl.multiple_of(g * 128, 128), 128)]
        for k in range(NK):
            gw1 = jnp.dot(xt[row(g, k)], dpre, preferred_element_type=F32).astype(BF)
            g1s[:, :, g, k] = gw1.reshape(4, 2, 16, 128)
        return 0

    def keep_two(g, k, value):
        g2s[x, c, g, k] = value

    def lanes_back(i, _):
        s = tab[HOME_LOCAL + i]
        lanes[i // 16, (i // 4) % 4, i % 4] = g2s[x, c, s]
        return 0

    lax.fori_loop(0, NB, hidden, 0)
    back((z + 2) % 4)
    part_copy(1, 0, 2).start()
    pass_stage(0)
    for d in (1, 3):
        back((z + d) % 4)
        part_copy(1, 0, d).start()
    lax.fori_loop(0, HALF, grad_one, 0)
    pl.semaphore_wait(free_sem, 1)
    grad_copy(1, 6).start()
    last_stage(0, keep_two, scale2)
    lanes_sent(0)
    lax.fori_loop(0, 32, lanes_back, 0)
    lanes_go(1)
    lax.fori_loop(HALF, NB, grad_one, 0)
    grad_copy(1, 7).start()
    mix(y)
    pair_stage(1)
    back(z)
    lanes_turn(1)
    for w in range(2):
        for d in range(1, 4):
            part_copy(w, 0, d).wait_recv()
        part = parts[w]

        def add_four(i, _):
            a, b = i // 3, i % 3
            here = (y, a) if w == 0 else (a, z)
            total = part[here[0], here[1], b].astype(F32)
            for d in range(3):
                total = total + f_buf[w, d, a, b].astype(F32)
            part[here[0], here[1], b] = total.astype(BF)
            return 0

        lax.fori_loop(0, 12, add_four, 0)
        for d in range(1, 4):
            part_copy(w, 1, d).start()
    pass_stage(1)
    for w, out in ((0, mixed), (1, dxo)):
        for d in range(1, 4):
            part_copy(w, 1, d).wait_recv()
        for b in range(3):
            total = parts[w][y, z, b].astype(F32)
            for d in range(3):
                total = total + f_fin[w, d, b].astype(F32)
            out[:, b * 128 : (b + 1) * 128] = total.astype(BF)
    lanes_end(1)

    def slot_out(s, _):
        i = tab[SLOT_LANE + s]
        got = rback[i // 16, (i // 4) % 4, i % 4]
        o2[s] = jnp.where(s < tab[SLOTS_HERE], got, jnp.zeros_like(got))
        return 0

    lax.fori_loop(0, CAP, slot_out, 0)

    def keep_one(g, k, value):
        o1[g, k] = value

    last_stage(1, keep_one, scale1)
    lanes_sent(1)
    for w in range(2):
        for i in range(10):
            weight_copy(w, i).wait_send()
        for group in range(5):
            for i in range(4):
                feature_copy(w, group, i).wait_send()
        for i in range(8):
            grad_copy(w, i).wait_send()
        for step in range(2):
            for d in range(1, 4):
                part_copy(w, step, d).wait_send()


OWN_SLOT, HOME_LOCAL, HOME_LANE, HOME_Q, SLOT_LANE, SLOTS_HERE, SPARE = 0, 32, 64, 80, 96, 120, 128


def table_kernel(owner, rows, cols, tab, kv, count, pairs):
    t = lax.axis_index("tensor")
    for i in range(16):
        count[i] = 0
    for i in range(32):
        tab[OWN_SLOT + i] = 0
        tab[HOME_LOCAL + i] = 0
    for s in range(CAP):
        tab[SLOT_LANE + s] = 0

    def source(src, _):
        for i in range(16):
            pairs[i] = 0
        for i in range(NB):
            o = owner[src * NB + i]
            slot, pair = count[o], pairs[o]
            count[o] = slot + 1
            pairs[o] = pair + 1
            here = o == t
            tab[jnp.where(here, OWN_SLOT + pair * 16 + src, SPARE)] = slot
            tab[jnp.where(here, SLOT_LANE + slot, SPARE + 1)] = pair * 16 + src

            @pl.when(src == t)
            def _():
                tab[HOME_LANE + i] = pair * 16 + o
                tab[HOME_Q + i] = o * CAP + slot
                tab[HOME_LOCAL + pair * 16 + o] = i

        return 0

    lax.fori_loop(0, 16, source, 0)
    tab[SLOTS_HERE] = count[t]

    def inverse(g, _):
        for j in range(48):
            kv[g, j] = NK
            kv[NB + g, j] = NK
        q = tab[HOME_Q + g]
        for k in range(NK):
            kv[g, rows[k, t * NB + g]] = k
            kv[NB + g, cols[k, q]] = k
        return 0

    lax.fori_loop(0, NB, inverse, 0)


def hand_over(*refs):
    src, dst, kept, sem = refs[:4], refs[4:8], refs[8:12], refs[12]
    loads = [pltpu.make_async_copy(src[i], kept[i], sem.at[0, i]) for i in range(4)]
    stores = [pltpu.make_async_copy(kept[i], dst[i], sem.at[1, i]) for i in range(4)]
    for i in (3, 2, 0, 1):
        loads[i].start()
    for i in (3, 2, 0, 1):
        loads[i].wait()
        stores[i].start()
    for cp in stores:
        cp.wait()


VM = pl.BlockSpec(memory_space=pltpu.VMEM)
SM = pl.BlockSpec(memory_space=pltpu.SMEM)
ANY = pl.BlockSpec(memory_space=pl.ANY)
SHARD = (NB, NK, 16, 128)
LANES = (2, 4, 4, NK, 16, 128)


def local(tokens, cotangent, w1_blocks, w1_rows, w1_scale, w2_blocks, w2_cols, w2_scale, owner):
    dma = pltpu.SemaphoreType.DMA
    part = (4, 4, 3, 192, 128)
    outs = [
        jax.ShapeDtypeStruct((192, 384), BF),
        jax.ShapeDtypeStruct((192, 384), BF),
        jax.ShapeDtypeStruct(SHARD, BF),
        jax.ShapeDtypeStruct((CAP, NK, 16, 128), BF),
    ]
    tab, kv = pl.pallas_call(
        table_kernel,
        out_shape=[
            jax.ShapeDtypeStruct((256,), jnp.int32),
            jax.ShapeDtypeStruct((2 * NB, 48), jnp.int32),
        ],
        in_specs=[SM] * 3,
        out_specs=[SM] * 2,
        scratch_shapes=[pltpu.SMEM((16,), jnp.int32), pltpu.SMEM((16,), jnp.int32)],
    )(owner, w1_rows.T, w2_cols.T)
    results = pl.pallas_call(
        layer_kernel,
        out_shape=outs,
        in_specs=[ANY] * 4 + [SM] * 6,
        out_specs=[VM] * 4,
        scratch_shapes=[
            pltpu.VMEM(SHARD, BF),
            pltpu.VMEM((CAP, NK, 16, 128), BF),
            pltpu.VMEM((48, 192, 128), BF),
            pltpu.VMEM((48, 192, 128), BF),
            pltpu.VMEM((8, NB, NK + 1, 16, 128), BF),
            pltpu.VMEM((8, NB, NK + 1, 16, 128), BF),
            pltpu.VMEM(LANES, BF),
            pltpu.VMEM(LANES, BF),
            pltpu.VMEM(LANES, BF),
            pltpu.VMEM((2,) + LANES, BF),
            pltpu.VMEM((48, 128, 192), BF),
            pltpu.VMEM((NB, 192, 128), F32),
            pltpu.VMEM((192, NB * 128), BF),
            pltpu.VMEM((192, NB * 128), BF),
            pltpu.VMEM((4, 2) + SHARD, BF),
            pltpu.VMEM((4, 2) + SHARD, BF),
            pltpu.VMEM((4,) + SHARD, BF),
            pltpu.VMEM((2, 2, HALF, NK, 16, 128), BF),
            pltpu.VMEM((2, 2) + SHARD, BF),
            pltpu.VMEM(part, BF),
            pltpu.VMEM(part, BF),
            pltpu.VMEM((2, 3, 4, 3, 192, 128), BF),
            pltpu.VMEM((2, 3, 3, 192, 128), BF),
            dma((2, 2, 2, 4)),
            dma((2, 2, 2, 4)),
            dma((2, 10)),
            dma((2, 10)),
            dma((2, 5, 4)),
            dma((2, 5, 4)),
            dma((2, 8)),
            dma((2, 8)),
            dma((2, 2, 4)),
            dma((2, 2, 4)),
            dma((8,)),
            pltpu.SemaphoreType.REGULAR,
        ],
        compiler_params=pltpu.CompilerParams(
            collective_id=0, has_side_effects=True, vmem_limit_bytes=(64 << 20) - (64 << 10)
        ),
    )(
        tokens,
        cotangent,
        w1_blocks,
        w2_blocks,
        w1_scale.T,
        w2_scale.T,
        w1_rows.T,
        w2_cols.T,
        tab,
        kv,
    )
    return pl.pallas_call(
        hand_over,
        out_shape=outs,
        in_specs=[ANY] * 4,
        out_specs=[ANY] * 4,
        scratch_shapes=[pltpu.VMEM(o.shape, BF) for o in outs] + [dma((2, 4))],
    )(*results)


def solution(mesh):
    in_specs = (
        P("dp", "tensor"),
        P("dp", "tensor"),
        P("tensor", None, "dp", None),
        P(),
        P(),
        P("tensor", None, "dp", None),
        P(),
        P(),
        P(),
    )
    out_specs = (
        P("dp", "tensor"),
        P("dp", "tensor"),
        P("tensor", None, "dp", None),
        P("tensor", None, "dp", None),
    )
    return jax.shard_map(local, mesh=mesh, in_specs=in_specs, out_specs=out_specs, check_vma=False)
```

```python
import jax
import jax.numpy as jnp
from jax import lax
from jax.experimental import pallas as pl
from jax.experimental.pallas import tpu as pltpu
from jax.sharding import PartitionSpec as P

GELU_C = 0.7978845608028654
GELU_A = 0.044715
MESH = pl.DeviceIdType.MESH
BF = jnp.bfloat16
F32 = jnp.float32
NB = 12
NK = 15
CAP = 18
HALF = NB // 2


def where_am_i():
    p = lax.axis_index("dp")
    t = lax.axis_index("tensor")
    return p, t, p // 2, p % 2, t // 4, t % 4


def enter(p, t, x, c, y, z):
    barrier = pltpu.get_barrier_semaphore()
    for d in range(1, 4):
        for peer in (((y + d) % 4) * 4 + z, y * 4 + (z + d) % 4):
            pl.semaphore_signal(barrier, inc=1, device_id=(p, peer), device_id_type=MESH)
    for q in (2 * ((x + 1) % 4) + c, 2 * ((x + 3) % 4) + c, 2 * x + 1 - c):
        pl.semaphore_signal(barrier, inc=1, device_id=(q, t), device_id_type=MESH)
    return barrier


def layer_kernel(
    tok_ref,
    cot_ref,
    w1_ref,
    w2_ref,
    s1_ref,
    s2_ref,
    rows_ref,
    cols_ref,
    tab,
    kv_ref,
    mixed,
    dxo,
    o1,
    o2,
    w1in,
    w2in,
    xall,
    dyall,
    w1all,
    w2all,
    lanes,
    rbuf,
    rback,
    middle,
    xt,
    slope,
    act_all,
    dpre_all,
    g1s,
    g2s,
    sib,
    fwd,
    fin,
    m_part,
    d_part,
    f_buf,
    f_hop,
    f_fin,
    a_send,
    a_recv,
    w_send,
    w_recv,
    x_send,
    x_recv,
    g_send,
    g_recv,
    f_send,
    f_recv,
    l_sem,
    free_sem,
):
    p, t, x, c, y, z = where_am_i()
    barrier = enter(p, t, x, c, y, z)
    xr, xl, xo = (x + 1) % 4, (x + 3) % 4, (x + 2) % 4
    rp, lp, op, sp = 2 * xr + c, 2 * xl + c, 2 * xo + c, 2 * x + 1 - c
    halves = (pl.ds(0, HALF), pl.ds(HALF, HALF))
    first, second = halves
    whole = pl.ds(0, NB)
    feats = (xall, dyall)
    weights = (w1all, w2all)
    grads = (g2s, g1s)
    parts = (m_part, d_part)
    landed = (rbuf, rback)
    nt = (((1,), (1,)), ((), ()))

    def row(g, k):
        return rows_ref[k, t * NB + g]

    def col(g, k):
        return cols_ref[k, tab[HOME_Q + g]]

    def scale1(g, k):
        return s1_ref[k, t * NB + g]

    def scale2(g, k):
        return s2_ref[k, tab[HOME_Q + g]]

    def lane_copy(trip, j, step, d, piece):
        along_y = (j == 0) == (step == 0)
        peer_y, peer_z = ((y + d) % 4, z) if along_y else (y, (z + d) % 4)
        ks = (pl.ds(0, 8), pl.ds(8, NK - 8))[piece]
        src = lanes.at[j] if step == 0 else middle.at[trip, j]
        dst = middle.at[trip, j] if step == 0 else landed[trip].at[j]
        return pltpu.make_async_remote_copy(
            src.at[peer_y, :, ks] if along_y else src.at[:, peer_z, ks],
            dst.at[y, :, ks] if along_y else dst.at[:, z, ks],
            a_send.at[trip, j, step, d, piece],
            a_recv.at[trip, j, step, d, piece],
            device_id=(p, peer_y * 4 + peer_z),
            device_id_type=MESH,
        )

    def lanes_go(trip):
        for piece in range(2):
            for d in (2, 1, 3):
                for j in range(2):
                    lane_copy(trip, j, 0, d, piece).start()
        middle[trip, 0, y] = lanes[0, y]
        middle[trip, 1, :, z] = lanes[1, :, z]

    def lanes_turn(trip, piece):
        for j in range(2):
            for d in range(1, 4):
                lane_copy(trip, j, 0, d, piece).wait_recv()
            for d in (2, 1, 3):
                lane_copy(trip, j, 1, d, piece).start()

    def lanes_end(trip):
        landed[trip][0, :, z] = middle[trip, 0, :, z]
        landed[trip][1, y] = middle[trip, 1, y]
        for piece in range(2):
            for j in range(2):
                for d in range(1, 4):
                    lane_copy(trip, j, 1, d, piece).wait_recv()

    def lanes_sent(trip):
        for j in range(2):
            for step in range(2):
                for d in range(1, 4):
                    for piece in range(2):
                        lane_copy(trip, j, step, d, piece).wait_send()

    def weight_copy(w, i):
        who, part, dev = (
            (p, first, rp),
            (p, second, rp),
            (p, second, lp),
            (p, first, lp),
            (p, whole, sp),
            (lp, first, rp),
            (rp, second, lp),
            (lp, whole, sp),
            (rp, whole, sp),
            (op, whole, sp),
        )[i]
        ref = weights[w].at[who, part, pl.ds(0, NK)]
        return pltpu.make_async_remote_copy(
            ref, ref, w_send.at[w, i], w_recv.at[w, i], device_id=(dev, t), device_id_type=MESH
        )

    def feature_copy(w, group, i):
        along_y = (w == 0) == (group == 0)
        came = 0 if group == 0 else group - 1
        on = (0, 0, 1, 3)[i]
        if along_y:
            holder = ((y + 4 - on) % 4) * 4 + (z + 4 - came) % 4
        else:
            holder = ((y + 4 - came) % 4) * 4 + (z + 4 - on) % 4
        d = (1, 3, 1, 3)[i]
        peer = ((y + d) % 4) * 4 + z if along_y else y * 4 + (z + d) % 4
        ref = feats[w].at[pl.ds(3 * holder, 3)]
        if i >= 2:
            ref = ref.at[:, pl.ds(96 * (i - 2), 96)]
        return pltpu.make_async_remote_copy(
            ref,
            ref,
            x_send.at[w, group, i],
            x_recv.at[w, group, i],
            device_id=(p, peer),
            device_id_type=MESH,
        )

    def grad_copy(w, i):
        own = grads[w]
        src, dst, dev = (
            (own.at[xo, c, first], fwd.at[w, 0], rp),
            (own.at[xo, c, second], fwd.at[w, 1], lp),
            (own.at[xr, c, second], fin.at[w, 0, second], rp),
            (own.at[xl, c, first], fin.at[w, 1, first], lp),
            (own.at[xr, c, first], fin.at[w, 0, first], rp),
            (own.at[xl, c, second], fin.at[w, 1, second], lp),
            (own.at[:, 1 - c, first], sib.at[:, first], sp),
            (own.at[:, 1 - c, second], sib.at[:, second], sp),
        )[i]
        return pltpu.make_async_remote_copy(
            src, dst, g_send.at[w, i], g_recv.at[w, i], device_id=(dev, t), device_id_type=MESH
        )

    def shards_of(w, place, lo, n):
        return (place, pl.ds(lo, n)) if w == 0 else (pl.ds(lo, n), place)

    def part_copy(w, step, d):
        along_y = (w == 0) == (step == 0)
        if step == 0:
            here = y if w == 0 else z
            up, down, far = (here + 1) % 4, (here + 3) % 4, (here + 2) % 4
            place, lo, dst, to = (
                (far, 0, f_hop.at[w, 0], 1),
                (far, 2, f_hop.at[w, 1], 3),
                (up, 2, f_buf.at[w, 0, pl.ds(2, 2)], 1),
                (down, 0, f_buf.at[w, 1, pl.ds(0, 2)], 3),
                (up, 0, f_buf.at[w, 0, pl.ds(0, 2)], 1),
                (down, 2, f_buf.at[w, 1, pl.ds(2, 2)], 3),
            )[d]
            src = parts[w].at[shards_of(w, place, lo, 2)]
            peer_y, peer_z = ((y + to) % 4, z) if along_y else (y, (z + to) % 4)
        else:
            peer_y, peer_z = ((y + d) % 4, z) if along_y else (y, (z + d) % 4)
            src = parts[w].at[peer_y, peer_z]
            dst = f_fin.at[w, d - 1]
        return pltpu.make_async_remote_copy(
            src,
            dst,
            f_send.at[w, step, d],
            f_recv.at[w, step, d],
            device_id=(p, peer_y * 4 + peer_z),
            device_id_type=MESH,
        )

    def part_on(w, way):
        here = y if w == 0 else z
        place = (here + (1, 3)[way]) % 4
        part = parts[w]
        part_copy(w, 0, way).wait_recv()

        def add(i, _):
            a, b = i // 3 + 2 * way, i % 3
            at = (place, a) if w == 0 else (a, place)
            total = part[at[0], at[1], b].astype(F32) + f_hop[w, way, i // 3, b].astype(F32)
            part[at[0], at[1], b] = total.astype(BF)
            return 0

        lax.fori_loop(0, 6, add, 0)
        part_copy(w, 0, 4 + way).start()

    loads = [
        pltpu.make_async_copy(w2_ref, w2in, l_sem.at[0]),
        pltpu.make_async_copy(w1_ref, w1in, l_sem.at[1]),
    ]
    for w, ref in enumerate((tok_ref, cot_ref)):
        for b in range(3):
            loads.append(
                pltpu.make_async_copy(
                    ref.at[:, pl.ds(b * 128, 128)],
                    feats[w].at[3 * t + b],
                    l_sem.at[2 + 3 * w + b],
                )
            )
    for cp in loads:
        cp.start()
    loads[0].wait()

    def lanes_out(i, _):
        s = tab[OWN_SLOT + i]
        lanes[i // 16, (i // 4) % 4, i % 4] = w2in[s]
        return 0

    lax.fori_loop(0, 32, lanes_out, 0)
    pl.semaphore_wait(barrier, 9)
    lanes_go(0)
    loads[1].wait()

    def scale_one(g, _):
        for k in range(NK):
            w1all[p, g, k] = (w1in[g, k].astype(F32) * scale1(g, k)).astype(BF)
        return 0

    lax.fori_loop(0, NB, scale_one, 0)
    for i in range(5):
        weight_copy(0, i).start()
    w1all[:, :, NK] = jnp.zeros((8, NB, 16, 128), BF)
    w2all[:, :, NK] = jnp.zeros((8, NB, 16, 128), BF)
    for cp in loads[2:]:
        cp.wait()

    def weights_on(w):
        weight_copy(w, 0).wait_recv()
        weight_copy(w, 5).start()
        weight_copy(w, 2).wait_recv()
        weight_copy(w, 6).start()
        weight_copy(w, 1).wait_recv()
        weight_copy(w, 7).start()
        weight_copy(w, 3).wait_recv()
        weight_copy(w, 8).start()

    def weights_last(w):
        weight_copy(w, 5).wait_recv()
        weight_copy(w, 6).wait_recv()
        weight_copy(w, 9).start()

    lanes_turn(0, 0)
    lanes_turn(0, 1)
    for group in (0, 1):
        for w in range(2):
            for i in range(2):
                feature_copy(w, group, i).start()
    weights_on(0)
    lanes_end(0)

    def scale_two(g, _):
        i = tab[HOME_LANE + g]
        for k in range(NK):
            w2all[p, g, k] = (rbuf[i // 16, (i // 4) % 4, i % 4, k].astype(F32) * scale2(g, k)).astype(BF)
        return 0

    lax.fori_loop(0, NB, scale_two, 0)
    for i in range(5):
        weight_copy(1, i).start()

    def feature_on(w, group):
        for i in range(2):
            feature_copy(w, group, i).wait_recv()
            feature_copy(w, group, i + 2).start()
            if group == 0:
                for k in range(2):
                    feature_copy(w, (2, 4)[i], k).start()

    for w in range(2):
        feature_on(w, 0)
    for w in range(2):
        feature_on(w, 1)
    weights_last(0)
    for w in range(2):
        for i in (2, 3):
            feature_copy(w, 0, i).wait_recv()
        for k in range(2):
            feature_copy(w, 3, k).start()
    for group in (2, 4):
        for w in range(2):
            feature_on(w, group)
    weights_on(1)
    for w in range(2):
        feature_on(w, 3)
    for group in range(1, 5):
        for w in range(2):
            for i in (2, 3):
                feature_copy(w, group, i).wait_recv()
    for i in (4, 7, 8, 9):
        weight_copy(0, i).wait_recv()

    def project(g, _):
        w1c = jnp.concatenate([w1all[:, g, k].reshape(128, 128) for k in range(NK)], axis=0)
        xs = jnp.concatenate([xall[row(g, k)] for k in range(NK)], axis=1)
        pre = jnp.dot(xs, w1c, preferred_element_type=F32)
        th = jnp.tanh(GELU_C * (pre + GELU_A * pre * pre * pre))
        act = (0.5 * pre * (1.0 + th)).astype(BF)
        slope[g] = 0.5 * (1.0 + th) + 0.5 * pre * (1.0 - th * th) * GELU_C * (
            1.0 + 3.0 * GELU_A * pre * pre
        )
        act_all[:, pl.ds(pl.multiple_of(g * 128, 128), 128)] = act
        dys = jnp.concatenate([dyall[col(g, k)] for k in range(NK)], axis=1)
        gw2 = jnp.dot(act.T, dys, preferred_element_type=F32).astype(BF)
        for k in range(NK):
            g2s[:, :, g, k] = gw2[:, k * 128 : (k + 1) * 128].reshape(4, 2, 16, 128)
        return 0

    def flip(j, _):
        xt[j] = xall[j].T
        return 0

    lax.fori_loop(0, HALF, project, 0)
    grad_copy(0, 6).start()
    weights_last(1)
    lax.fori_loop(HALF, NB, project, 0)
    grad_copy(0, 7).start()
    lax.fori_loop(0, 48, flip, 0)

    def pair_sum(w, chunk, h):
        own = grads[w]

        def body(g, _):
            own[chunk, c, g] = (own[chunk, c, g].astype(F32) + sib[chunk, g].astype(F32)).astype(BF)
            return 0

        lax.fori_loop(h * HALF, (h + 1) * HALF, body, 0)

    def pair_stage(w):
        grad_copy(w, 6).wait_recv()
        pair_sum(w, xo, 0)
        grad_copy(w, 0).start()
        pair_sum(w, xl, 0)
        grad_copy(w, 3).start()
        grad_copy(w, 7).wait_recv()
        pair_sum(w, xo, 1)
        grad_copy(w, 1).start()
        pair_sum(w, xr, 1)
        grad_copy(w, 2).start()
        pair_sum(w, xr, 0)
        pair_sum(w, xl, 1)
        pair_sum(w, x, 0)
        pair_sum(w, x, 1)

    def pass_stage(w):
        own = grads[w]
        grad_copy(w, 0).wait_recv()

        def right(g, _):
            own[xr, c, g] = (own[xr, c, g].astype(F32) + fwd[w, 0, g].astype(F32)).astype(BF)
            return 0

        lax.fori_loop(0, HALF, right, 0)
        grad_copy(w, 4).start()
        grad_copy(w, 1).wait_recv()

        def left(g, _):
            own[xl, c, g + HALF] = (
                own[xl, c, g + HALF].astype(F32) + fwd[w, 1, g].astype(F32)
            ).astype(BF)
            return 0

        lax.fori_loop(0, HALF, left, 0)
        grad_copy(w, 5).start()

    def last_stage(w, out, scale):
        own = grads[w]
        for i in (2, 3, 4, 5):
            grad_copy(w, i).wait_recv()

        def body(g, _):
            for k in range(NK):
                total = own[x, c, g, k].astype(F32) + fin[w, 0, g, k].astype(F32)
                total = total + fin[w, 1, g, k].astype(F32)
                out(g, k, (total * scale(g, k)).astype(BF))
            return 0

        lax.fori_loop(0, NB, body, 0)

    def mix(to_y):
        def body(i, _):
            j = 12 * to_y + 2 * i
            panel = jnp.concatenate(
                [
                    jnp.concatenate(
                        [w2all[:, g, kv_ref[NB + g, j + b]].reshape(128, 128) for g in range(NB)], axis=0
                    )
                    for b in range(2)
                ],
                axis=1,
            )
            res = jnp.dot(act_all[...], panel, preferred_element_type=F32).astype(BF)
            for b in range(2):
                at = 2 * i + b
                m_part[to_y, at // 3, at % 3] = res[:, b * 128 : (b + 1) * 128]
            return 0

        lax.fori_loop(0, 6, body, 0)

    def back(to_z):
        def body(i, _):
            at = (2 * i, 2 * i + 1)
            panel = jnp.concatenate(
                [
                    jnp.concatenate(
                        [
                            w1all[:, g, kv_ref[g, 12 * (a // 3) + 3 * to_z + a % 3]].reshape(128, 128)
                            for g in range(NB)
                        ],
                        axis=1,
                    )
                    for a in at
                ],
                axis=0,
            )
            res = lax.dot_general(dpre_all[...], panel, nt, preferred_element_type=F32).astype(BF)
            for b, a in enumerate(at):
                d_part[a // 3, to_z, a % 3] = res[:, b * 128 : (b + 1) * 128]
            return 0

        lax.fori_loop(0, 6, body, 0)

    for i in (4, 7, 8, 9):
        weight_copy(1, i).wait_recv()
    mix((y + 2) % 4)
    part_copy(0, 0, 0).start()
    part_copy(0, 0, 1).start()
    pair_stage(0)
    pl.semaphore_signal(free_sem, inc=1, device_id=(sp, t), device_id_type=MESH)
    def hidden(g, _):
        w2c = jnp.concatenate([w2all[:, g, k].reshape(128, 128) for k in range(NK)], axis=1)
        dys = jnp.concatenate([dyall[col(g, k)] for k in range(NK)], axis=1)
        dact = lax.dot_general(dys, w2c, nt, preferred_element_type=F32).astype(BF)
        dpre = (dact.astype(F32) * slope[g]).astype(BF)
        dpre_all[:, pl.ds(pl.multiple_of(g * 128, 128), 128)] = dpre
        return 0

    def grad_one(g, _):
        dpre = dpre_all[:, pl.ds(pl.multiple_of(g * 128, 128), 128)]
        for k in range(NK):
            gw1 = jnp.dot(xt[row(g, k)], dpre, preferred_element_type=F32).astype(BF)
            g1s[:, :, g, k] = gw1.reshape(4, 2, 16, 128)
        return 0

    def keep_two(g, k, value):
        g2s[x, c, g, k] = value

    def lanes_back(i, _):
        s = tab[HOME_LOCAL + i]
        lanes[i // 16, (i // 4) % 4, i % 4] = g2s[x, c, s]
        return 0

    def mix_go(way):
        mix((y + (1, 3)[way]) % 4)
        part_copy(0, 0, 2 + way).start()
        part_on(0, way)

    def back_go(way):
        back((z + (1, 3)[way]) % 4)
        part_copy(1, 0, 2 + way).start()
        part_on(1, way)

    lax.fori_loop(0, NB, hidden, 0)
    back((z + 2) % 4)
    part_copy(1, 0, 0).start()
    part_copy(1, 0, 1).start()
    mix_go(0)
    lax.fori_loop(0, HALF, grad_one, 0)
    pl.semaphore_wait(free_sem, 1)
    grad_copy(1, 6).start()
    pass_stage(0)
    mix_go(1)
    back_go(0)
    lax.fori_loop(HALF, NB, grad_one, 0)
    grad_copy(1, 7).start()
    back_go(1)
    mix(y)
    pair_stage(1)
    last_stage(0, keep_two, scale2)
    lanes_sent(0)
    lax.fori_loop(0, 32, lanes_back, 0)
    lanes_go(1)
    back(z)
    lanes_turn(1, 0)
    lanes_turn(1, 1)
    pass_stage(1)
    for w in range(2):
        for d in range(2, 6):
            part_copy(w, 0, d).wait_recv()
        part = parts[w]

        def add_four(i, _):
            a, b = i // 3, i % 3
            here = (y, a) if w == 0 else (a, z)
            total = part[here[0], here[1], b].astype(F32)
            for d in range(2):
                total = total + f_buf[w, d, a, b].astype(F32)
            part[here[0], here[1], b] = total.astype(BF)
            return 0

        lax.fori_loop(0, 12, add_four, 0)
        for d in range(1, 4):
            part_copy(w, 1, d).start()
    for w, out in ((0, mixed), (1, dxo)):
        for d in range(1, 4):
            part_copy(w, 1, d).wait_recv()
        for b in range(3):
            total = parts[w][y, z, b].astype(F32)
            for d in range(3):
                total = total + f_fin[w, d, b].astype(F32)
            out[:, b * 128 : (b + 1) * 128] = total.astype(BF)
    lanes_end(1)

    def slot_out(s, _):
        i = tab[SLOT_LANE + s]
        got = rback[i // 16, (i // 4) % 4, i % 4]
        o2[s] = jnp.where(s < tab[SLOTS_HERE], got, jnp.zeros_like(got))
        return 0

    lax.fori_loop(0, CAP, slot_out, 0)

    def keep_one(g, k, value):
        o1[g, k] = value

    last_stage(1, keep_one, scale1)
    lanes_sent(1)
    for w in range(2):
        for i in range(10):
            weight_copy(w, i).wait_send()
        for group in range(5):
            for i in range(4):
                feature_copy(w, group, i).wait_send()
        for i in range(8):
            grad_copy(w, i).wait_send()
        for d in range(6):
            part_copy(w, 0, d).wait_send()
        for d in range(1, 4):
            part_copy(w, 1, d).wait_send()


OWN_SLOT, HOME_LOCAL, HOME_LANE, HOME_Q, SLOT_LANE, SLOTS_HERE, SPARE = 0, 32, 64, 80, 96, 120, 128


def table_kernel(owner, rows, cols, tab, kv, count, pairs):
    t = lax.axis_index("tensor")
    for i in range(16):
        count[i] = 0
    for i in range(32):
        tab[OWN_SLOT + i] = 0
        tab[HOME_LOCAL + i] = 0
    for s in range(CAP):
        tab[SLOT_LANE + s] = 0

    def source(src, _):
        seen = []
        for i in range(16):
            pairs[i] = 0
        for i in range(NB):
            o = owner[src * NB + i]
            slot, pair = count[o], pairs[o]
            count[o] = slot + 1
            pairs[o] = pair + 1
            here = o == t
            tab[jnp.where(here, OWN_SLOT + pair * 16 + src, SPARE)] = slot
            tab[jnp.where(here, SLOT_LANE + slot, SPARE + 1)] = pair * 16 + src

            seen.append((o, slot, pair))

        @pl.when(src == t)
        def _():
            for i, (o, slot, pair) in enumerate(seen):
                tab[HOME_LANE + i] = pair * 16 + o
                tab[HOME_Q + i] = o * CAP + slot
                tab[HOME_LOCAL + pair * 16 + o] = i

        return 0

    lax.fori_loop(0, 16, source, 0)
    tab[SLOTS_HERE] = count[t]

    def inverse(g, _):
        for j in range(48):
            kv[g, j] = NK
            kv[NB + g, j] = NK
        q = tab[HOME_Q + g]
        for k in range(NK):
            kv[g, rows[k, t * NB + g]] = k
            kv[NB + g, cols[k, q]] = k
        return 0

    lax.fori_loop(0, NB, inverse, 0)


def hand_over(*refs):
    src, dst, kept, sem = refs[:4], refs[4:8], refs[8:12], refs[12]
    loads = [pltpu.make_async_copy(src[i], kept[i], sem.at[0, i]) for i in range(4)]
    stores = [pltpu.make_async_copy(kept[i], dst[i], sem.at[1, i]) for i in range(4)]
    for i in (3, 2, 0, 1):
        loads[i].start()
    for i in (3, 2, 0, 1):
        loads[i].wait()
        stores[i].start()
    for cp in stores:
        cp.wait()


VM = pl.BlockSpec(memory_space=pltpu.VMEM)
SM = pl.BlockSpec(memory_space=pltpu.SMEM)
ANY = pl.BlockSpec(memory_space=pl.ANY)
SHARD = (NB, NK, 16, 128)
LANES = (2, 4, 4, NK, 16, 128)


def local(tokens, cotangent, w1_blocks, w1_rows, w1_scale, w2_blocks, w2_cols, w2_scale, owner):
    dma = pltpu.SemaphoreType.DMA
    part = (4, 4, 3, 192, 128)
    outs = [
        jax.ShapeDtypeStruct((192, 384), BF),
        jax.ShapeDtypeStruct((192, 384), BF),
        jax.ShapeDtypeStruct(SHARD, BF),
        jax.ShapeDtypeStruct((CAP, NK, 16, 128), BF),
    ]
    tab, kv = pl.pallas_call(
        table_kernel,
        out_shape=[
            jax.ShapeDtypeStruct((256,), jnp.int32),
            jax.ShapeDtypeStruct((2 * NB, 48), jnp.int32),
        ],
        in_specs=[SM] * 3,
        out_specs=[SM] * 2,
        scratch_shapes=[pltpu.SMEM((16,), jnp.int32), pltpu.SMEM((16,), jnp.int32)],
    )(owner, w1_rows.T, w2_cols.T)
    results = pl.pallas_call(
        layer_kernel,
        out_shape=outs,
        in_specs=[ANY] * 4 + [SM] * 6,
        out_specs=[VM] * 4,
        scratch_shapes=[
            pltpu.VMEM(SHARD, BF),
            pltpu.VMEM((CAP, NK, 16, 128), BF),
            pltpu.VMEM((48, 192, 128), BF),
            pltpu.VMEM((48, 192, 128), BF),
            pltpu.VMEM((8, NB, NK + 1, 16, 128), BF),
            pltpu.VMEM((8, NB, NK + 1, 16, 128), BF),
            pltpu.VMEM(LANES, BF),
            pltpu.VMEM(LANES, BF),
            pltpu.VMEM(LANES, BF),
            pltpu.VMEM((2,) + LANES, BF),
            pltpu.VMEM((48, 128, 192), BF),
            pltpu.VMEM((NB, 192, 128), F32),
            pltpu.VMEM((192, NB * 128), BF),
            pltpu.VMEM((192, NB * 128), BF),
            pltpu.VMEM((4, 2) + SHARD, BF),
            pltpu.VMEM((4, 2) + SHARD, BF),
            pltpu.VMEM((4,) + SHARD, BF),
            pltpu.VMEM((2, 2, HALF, NK, 16, 128), BF),
            pltpu.VMEM((2, 2) + SHARD, BF),
            pltpu.VMEM(part, BF),
            pltpu.VMEM(part, BF),
            pltpu.VMEM((2, 2, 4, 3, 192, 128), BF),
            pltpu.VMEM((2, 2, 2, 3, 192, 128), BF),
            pltpu.VMEM((2, 3, 3, 192, 128), BF),
            dma((2, 2, 2, 4, 2)),
            dma((2, 2, 2, 4, 2)),
            dma((2, 10)),
            dma((2, 10)),
            dma((2, 5, 4)),
            dma((2, 5, 4)),
            dma((2, 8)),
            dma((2, 8)),
            dma((2, 2, 6)),
            dma((2, 2, 6)),
            dma((8,)),
            pltpu.SemaphoreType.REGULAR,
        ],
        compiler_params=pltpu.CompilerParams(
            collective_id=0, has_side_effects=True, vmem_limit_bytes=(64 << 20) - (64 << 10)
        ),
    )(
        tokens,
        cotangent,
        w1_blocks,
        w2_blocks,
        w1_scale.T,
        w2_scale.T,
        w1_rows.T,
        w2_cols.T,
        tab,
        kv,
    )
    return pl.pallas_call(
        hand_over,
        out_shape=outs,
        in_specs=[ANY] * 4,
        out_specs=[ANY] * 4,
        scratch_shapes=[pltpu.VMEM(o.shape, BF) for o in outs] + [dma((2, 4))],
    )(*results)


def solution(mesh):
    in_specs = (
        P("dp", "tensor"),
        P("dp", "tensor"),
        P("tensor", None, "dp", None),
        P(),
        P(),
        P("tensor", None, "dp", None),
        P(),
        P(),
        P(),
    )
    out_specs = (
        P("dp", "tensor"),
        P("dp", "tensor"),
        P("tensor", None, "dp", None),
        P("tensor", None, "dp", None),
    )
    return jax.shard_map(local, mesh=mesh, in_specs=in_specs, out_specs=out_specs, check_vma=False)
```

```python
import jax
import jax.numpy as jnp
from jax import lax
from jax.experimental import pallas as pl
from jax.experimental.pallas import tpu as pltpu
from jax.sharding import PartitionSpec as P

GELU_C = 0.7978845608028654
GELU_A = 0.044715
MESH = pl.DeviceIdType.MESH
BF = jnp.bfloat16
F32 = jnp.float32
NB = 12
NK = 15
CAP = 18
HALF = NB // 2


def where_am_i():
    p = lax.axis_index("dp")
    t = lax.axis_index("tensor")
    return p, t, p // 2, p % 2, t // 4, t % 4


def enter(p, t, x, c, y, z):
    barrier = pltpu.get_barrier_semaphore()
    for d in range(1, 4):
        for peer in (((y + d) % 4) * 4 + z, y * 4 + (z + d) % 4):
            pl.semaphore_signal(barrier, inc=1, device_id=(p, peer), device_id_type=MESH)
    for q in (2 * ((x + 1) % 4) + c, 2 * ((x + 3) % 4) + c, 2 * x + 1 - c):
        pl.semaphore_signal(barrier, inc=1, device_id=(q, t), device_id_type=MESH)
    return barrier


def layer_kernel(
    tok_ref,
    cot_ref,
    w1_ref,
    w2_ref,
    s1_ref,
    s2_ref,
    rows_ref,
    cols_ref,
    tab,
    kv_ref,
    mixed,
    dxo,
    o1,
    o2,
    w1in,
    w2in,
    xall,
    dyall,
    w1all,
    w2all,
    lanes,
    rbuf,
    rback,
    middle,
    xt,
    slope,
    act_all,
    dpre_all,
    g1s,
    g2s,
    sib,
    fwd,
    fin,
    m_part,
    d_part,
    f_buf,
    f_hop,
    f_fin,
    a_send,
    a_recv,
    w_send,
    w_recv,
    x_send,
    x_recv,
    g_send,
    g_recv,
    f_send,
    f_recv,
    l_sem,
    free_sem,
):
    p, t, x, c, y, z = where_am_i()
    barrier = enter(p, t, x, c, y, z)
    xr, xl, xo = (x + 1) % 4, (x + 3) % 4, (x + 2) % 4
    rp, lp, op, sp = 2 * xr + c, 2 * xl + c, 2 * xo + c, 2 * x + 1 - c
    halves = (pl.ds(0, HALF), pl.ds(HALF, HALF))
    first, second = halves
    whole = pl.ds(0, NB)
    feats = (xall, dyall)
    weights = (w1all, w2all)
    grads = (g2s, g1s)
    parts = (m_part, d_part)
    landed = (rbuf, rback)
    nt = (((1,), (1,)), ((), ()))

    def row(g, k):
        return rows_ref[k, t * NB + g]

    def col(g, k):
        return cols_ref[k, tab[HOME_Q + g]]

    def scale1(g, k):
        return s1_ref[k, t * NB + g]

    def scale2(g, k):
        return s2_ref[k, tab[HOME_Q + g]]

    def lane_copy(trip, j, step, d, piece):
        along_y = (j == 0) == (step == 0)
        peer_y, peer_z = ((y + d) % 4, z) if along_y else (y, (z + d) % 4)
        ks = (pl.ds(0, 8), pl.ds(8, NK - 8))[piece]
        src = lanes.at[j] if step == 0 else middle.at[trip, j]
        dst = middle.at[trip, j] if step == 0 else landed[trip].at[j]
        return pltpu.make_async_remote_copy(
            src.at[peer_y, :, ks] if along_y else src.at[:, peer_z, ks],
            dst.at[y, :, ks] if along_y else dst.at[:, z, ks],
            a_send.at[trip, j, step, d, piece],
            a_recv.at[trip, j, step, d, piece],
            device_id=(p, peer_y * 4 + peer_z),
            device_id_type=MESH,
        )

    def lanes_go(trip):
        for piece in range(2):
            for d in (2, 1, 3):
                for j in range(2):
                    lane_copy(trip, j, 0, d, piece).start()
        middle[trip, 0, y] = lanes[0, y]
        middle[trip, 1, :, z] = lanes[1, :, z]

    def lanes_turn(trip, piece):
        for j in range(2):
            for d in range(1, 4):
                lane_copy(trip, j, 0, d, piece).wait_recv()
            for d in (2, 1, 3):
                lane_copy(trip, j, 1, d, piece).start()

    def lanes_end(trip):
        landed[trip][0, :, z] = middle[trip, 0, :, z]
        landed[trip][1, y] = middle[trip, 1, y]
        for piece in range(2):
            for j in range(2):
                for d in range(1, 4):
                    lane_copy(trip, j, 1, d, piece).wait_recv()

    def lanes_sent(trip):
        for j in range(2):
            for step in range(2):
                for d in range(1, 4):
                    for piece in range(2):
                        lane_copy(trip, j, step, d, piece).wait_send()

    def weight_copy(w, i):
        who, part, dev = (
            (p, first, rp),
            (p, second, rp),
            (p, second, lp),
            (p, first, lp),
            (p, whole, sp),
            (lp, first, rp),
            (rp, second, lp),
            (lp, whole, sp),
            (rp, whole, sp),
            (op, whole, sp),
        )[i]
        ref = weights[w].at[who, part, pl.ds(0, NK)]
        return pltpu.make_async_remote_copy(
            ref, ref, w_send.at[w, i], w_recv.at[w, i], device_id=(dev, t), device_id_type=MESH
        )

    def feature_copy(w, group, i):
        along_y = (w == 0) == (group == 0)
        came = 0 if group == 0 else group - 1
        on = (0, 0, 1, 3)[i]
        if along_y:
            holder = ((y + 4 - on) % 4) * 4 + (z + 4 - came) % 4
        else:
            holder = ((y + 4 - came) % 4) * 4 + (z + 4 - on) % 4
        d = (1, 3, 1, 3)[i]
        peer = ((y + d) % 4) * 4 + z if along_y else y * 4 + (z + d) % 4
        ref = feats[w].at[pl.ds(3 * holder, 3)]
        if i >= 2:
            ref = ref.at[:, pl.ds(96 * (i - 2), 96)]
        return pltpu.make_async_remote_copy(
            ref,
            ref,
            x_send.at[w, group, i],
            x_recv.at[w, group, i],
            device_id=(p, peer),
            device_id_type=MESH,
        )

    def grad_copy(w, i):
        own = grads[w]
        src, dst, dev = (
            (own.at[xo, c, first], fwd.at[w, 0], rp),
            (own.at[xo, c, second], fwd.at[w, 1], lp),
            (own.at[xr, c, second], fin.at[w, 0, second], rp),
            (own.at[xl, c, first], fin.at[w, 1, first], lp),
            (own.at[xr, c, first], fin.at[w, 0, first], rp),
            (own.at[xl, c, second], fin.at[w, 1, second], lp),
            (own.at[:, 1 - c, first], sib.at[:, first], sp),
            (own.at[:, 1 - c, second], sib.at[:, second], sp),
        )[i]
        return pltpu.make_async_remote_copy(
            src, dst, g_send.at[w, i], g_recv.at[w, i], device_id=(dev, t), device_id_type=MESH
        )

    def shards_of(w, place, lo, n):
        return (place, pl.ds(lo, n)) if w == 0 else (pl.ds(lo, n), place)

    def part_copy(w, step, d):
        along_y = (w == 0) == (step == 0)
        if step == 0:
            here = y if w == 0 else z
            up, down, far = (here + 1) % 4, (here + 3) % 4, (here + 2) % 4
            place, lo, dst, to = (
                (far, 0, f_hop.at[w, 0], 1),
                (far, 2, f_hop.at[w, 1], 3),
                (up, 2, f_buf.at[w, 0, pl.ds(2, 2)], 1),
                (down, 0, f_buf.at[w, 1, pl.ds(0, 2)], 3),
                (up, 0, f_buf.at[w, 0, pl.ds(0, 2)], 1),
                (down, 2, f_buf.at[w, 1, pl.ds(2, 2)], 3),
            )[d]
            src = parts[w].at[shards_of(w, place, lo, 2)]
            peer_y, peer_z = ((y + to) % 4, z) if along_y else (y, (z + to) % 4)
        else:
            peer_y, peer_z = ((y + d) % 4, z) if along_y else (y, (z + d) % 4)
            src = parts[w].at[peer_y, peer_z]
            dst = f_fin.at[w, d - 1]
        return pltpu.make_async_remote_copy(
            src,
            dst,
            f_send.at[w, step, d],
            f_recv.at[w, step, d],
            device_id=(p, peer_y * 4 + peer_z),
            device_id_type=MESH,
        )

    def part_on(w, way):
        here = y if w == 0 else z
        place = (here + (1, 3)[way]) % 4
        part = parts[w]
        part_copy(w, 0, way).wait_recv()

        def add(i, _):
            a, b = i // 3 + 2 * way, i % 3
            at = (place, a) if w == 0 else (a, place)
            total = part[at[0], at[1], b].astype(F32) + f_hop[w, way, i // 3, b].astype(F32)
            part[at[0], at[1], b] = total.astype(BF)
            return 0

        lax.fori_loop(0, 6, add, 0)
        part_copy(w, 0, 4 + way).start()

    loads = [
        pltpu.make_async_copy(w2_ref, w2in, l_sem.at[0]),
        pltpu.make_async_copy(w1_ref, w1in, l_sem.at[1]),
    ]
    for w, ref in enumerate((tok_ref, cot_ref)):
        for b in range(3):
            loads.append(
                pltpu.make_async_copy(
                    ref.at[:, pl.ds(b * 128, 128)],
                    feats[w].at[3 * t + b],
                    l_sem.at[2 + 3 * w + b],
                )
            )
    for cp in loads:
        cp.start()
    loads[0].wait()

    def lanes_out(i, _):
        s = tab[OWN_SLOT + i]
        lanes[i // 16, (i // 4) % 4, i % 4] = w2in[s]
        return 0

    lax.fori_loop(0, 32, lanes_out, 0)
    pl.semaphore_wait(barrier, 9)
    lanes_go(0)
    loads[1].wait()

    def scale_one(g, _):
        for k in range(NK):
            w1all[p, g, k] = (w1in[g, k].astype(F32) * scale1(g, k)).astype(BF)
        return 0

    lax.fori_loop(0, NB, scale_one, 0)
    for i in range(5):
        weight_copy(0, i).start()
    w1all[:, :, NK] = jnp.zeros((8, NB, 16, 128), BF)
    w2all[:, :, NK] = jnp.zeros((8, NB, 16, 128), BF)
    for cp in loads[2:]:
        cp.wait()

    def weights_on(w):
        weight_copy(w, 0).wait_recv()
        weight_copy(w, 5).start()
        weight_copy(w, 2).wait_recv()
        weight_copy(w, 6).start()
        weight_copy(w, 1).wait_recv()
        weight_copy(w, 7).start()
        weight_copy(w, 3).wait_recv()
        weight_copy(w, 8).start()

    def weights_last(w):
        weight_copy(w, 5).wait_recv()
        weight_copy(w, 6).wait_recv()
        weight_copy(w, 9).start()

    lanes_turn(0, 0)
    lanes_turn(0, 1)
    for group in (0, 1):
        for w in range(2):
            for i in range(2):
                feature_copy(w, group, i).start()
    weights_on(0)
    lanes_end(0)

    def scale_two(g, _):
        i = tab[HOME_LANE + g]
        for k in range(NK):
            w2all[p, g, k] = (rbuf[i // 16, (i // 4) % 4, i % 4, k].astype(F32) * scale2(g, k)).astype(BF)
        return 0

    lax.fori_loop(0, NB, scale_two, 0)
    for i in range(5):
        weight_copy(1, i).start()

    def feature_on(w, group):
        for i in range(2):
            feature_copy(w, group, i).wait_recv()
            feature_copy(w, group, i + 2).start()
            if group == 0:
                for k in range(2):
                    feature_copy(w, (2, 4)[i], k).start()

    for w in range(2):
        feature_on(w, 0)
    for w in range(2):
        feature_on(w, 1)
    weights_last(0)
    for w in range(2):
        for i in (2, 3):
            feature_copy(w, 0, i).wait_recv()
        for k in range(2):
            feature_copy(w, 3, k).start()
    for group in (2, 4):
        for w in range(2):
            feature_on(w, group)
    weights_on(1)
    for w in range(2):
        feature_on(w, 3)
    for group in range(1, 5):
        for w in range(2):
            for i in (2, 3):
                feature_copy(w, group, i).wait_recv()
    for i in (4, 7, 8, 9):
        weight_copy(0, i).wait_recv()

    def project(g, _):
        w1c = jnp.concatenate([w1all[:, g, k].reshape(128, 128) for k in range(NK)], axis=0)
        xs = jnp.concatenate([xall[row(g, k)] for k in range(NK)], axis=1)
        pre = jnp.dot(xs, w1c, preferred_element_type=F32)
        th = jnp.tanh(GELU_C * (pre + GELU_A * pre * pre * pre))
        act = (0.5 * pre * (1.0 + th)).astype(BF)
        slope[g] = 0.5 * (1.0 + th) + 0.5 * pre * (1.0 - th * th) * GELU_C * (
            1.0 + 3.0 * GELU_A * pre * pre
        )
        act_all[:, pl.ds(pl.multiple_of(g * 128, 128), 128)] = act
        dys = jnp.concatenate([dyall[col(g, k)] for k in range(NK)], axis=1)
        gw2 = jnp.dot(act.T, dys, preferred_element_type=F32).astype(BF)
        for k in range(NK):
            g2s[:, :, g, k] = gw2[:, k * 128 : (k + 1) * 128].reshape(4, 2, 16, 128)
        return 0

    def flip(j, _):
        xt[j] = xall[j].T
        return 0

    lax.fori_loop(0, HALF, project, 0)
    grad_copy(0, 6).start()
    weights_last(1)
    lax.fori_loop(HALF, NB, project, 0)
    grad_copy(0, 7).start()
    lax.fori_loop(0, 48, flip, 0)

    def pair_sum(w, chunk, h):
        own = grads[w]

        def body(g, _):
            own[chunk, c, g] = (own[chunk, c, g].astype(F32) + sib[chunk, g].astype(F32)).astype(BF)
            return 0

        lax.fori_loop(h * HALF, (h + 1) * HALF, body, 0)

    def pair_stage(w):
        grad_copy(w, 6).wait_recv()
        pair_sum(w, xo, 0)
        grad_copy(w, 0).start()
        pair_sum(w, xl, 0)
        grad_copy(w, 3).start()
        grad_copy(w, 7).wait_recv()
        pair_sum(w, xo, 1)
        grad_copy(w, 1).start()
        pair_sum(w, xr, 1)
        grad_copy(w, 2).start()
        pair_sum(w, xr, 0)
        pair_sum(w, xl, 1)
        pair_sum(w, x, 0)
        pair_sum(w, x, 1)

    def pass_stage(w):
        own = grads[w]
        grad_copy(w, 0).wait_recv()

        def right(g, _):
            own[xr, c, g] = (own[xr, c, g].astype(F32) + fwd[w, 0, g].astype(F32)).astype(BF)
            return 0

        lax.fori_loop(0, HALF, right, 0)
        grad_copy(w, 4).start()
        grad_copy(w, 1).wait_recv()

        def left(g, _):
            own[xl, c, g + HALF] = (
                own[xl, c, g + HALF].astype(F32) + fwd[w, 1, g].astype(F32)
            ).astype(BF)
            return 0

        lax.fori_loop(0, HALF, left, 0)
        grad_copy(w, 5).start()

    def last_stage(w, out, scale):
        own = grads[w]
        for i in (2, 3, 4, 5):
            grad_copy(w, i).wait_recv()

        def body(g, _):
            for k in range(NK):
                total = own[x, c, g, k].astype(F32) + fin[w, 0, g, k].astype(F32)
                total = total + fin[w, 1, g, k].astype(F32)
                out(g, k, (total * scale(g, k)).astype(BF))
            return 0

        lax.fori_loop(0, NB, body, 0)

    def mix(to_y):
        def body(i, _):
            j = 12 * to_y + 2 * i
            panel = jnp.concatenate(
                [
                    jnp.concatenate(
                        [w2all[:, g, kv_ref[NB + g, j + b]].reshape(128, 128) for g in range(NB)], axis=0
                    )
                    for b in range(2)
                ],
                axis=1,
            )
            res = jnp.dot(act_all[...], panel, preferred_element_type=F32).astype(BF)
            for b in range(2):
                at = 2 * i + b
                m_part[to_y, at // 3, at % 3] = res[:, b * 128 : (b + 1) * 128]
            return 0

        lax.fori_loop(0, 6, body, 0)

    def back(to_z):
        def body(i, _):
            at = (2 * i, 2 * i + 1)
            panel = jnp.concatenate(
                [
                    jnp.concatenate(
                        [
                            w1all[:, g, kv_ref[g, 12 * (a // 3) + 3 * to_z + a % 3]].reshape(128, 128)
                            for g in range(NB)
                        ],
                        axis=1,
                    )
                    for a in at
                ],
                axis=0,
            )
            res = lax.dot_general(dpre_all[...], panel, nt, preferred_element_type=F32).astype(BF)
            for b, a in enumerate(at):
                d_part[a // 3, to_z, a % 3] = res[:, b * 128 : (b + 1) * 128]
            return 0

        lax.fori_loop(0, 6, body, 0)

    for i in (4, 7, 8, 9):
        weight_copy(1, i).wait_recv()
    mix((y + 2) % 4)
    part_copy(0, 0, 0).start()
    part_copy(0, 0, 1).start()
    pair_stage(0)
    pl.semaphore_signal(free_sem, inc=1, device_id=(sp, t), device_id_type=MESH)
    def hidden(g, _):
        w2c = jnp.concatenate([w2all[:, g, k].reshape(128, 128) for k in range(NK)], axis=1)
        dys = jnp.concatenate([dyall[col(g, k)] for k in range(NK)], axis=1)
        dact = lax.dot_general(dys, w2c, nt, preferred_element_type=F32).astype(BF)
        dpre = (dact.astype(F32) * slope[g]).astype(BF)
        dpre_all[:, pl.ds(pl.multiple_of(g * 128, 128), 128)] = dpre
        return 0

    def grad_one(g, _):
        dpre = dpre_all[:, pl.ds(pl.multiple_of(g * 128, 128), 128)]
        for k in range(NK):
            gw1 = jnp.dot(xt[row(g, k)], dpre, preferred_element_type=F32).astype(BF)
            g1s[:, :, g, k] = gw1.reshape(4, 2, 16, 128)
        return 0

    def keep_two(g, k, value):
        g2s[x, c, g, k] = value

    def lanes_back(i, _):
        s = tab[HOME_LOCAL + i]
        lanes[i // 16, (i // 4) % 4, i % 4] = g2s[x, c, s]
        return 0

    def mix_go(way):
        mix((y + (1, 3)[way]) % 4)
        part_copy(0, 0, 2 + way).start()
        part_on(0, way)

    def back_go(way):
        back((z + (1, 3)[way]) % 4)
        part_copy(1, 0, 2 + way).start()
        part_on(1, way)

    def part_turn(w):
        for d in range(2, 6):
            part_copy(w, 0, d).wait_recv()
        part = parts[w]

        def add_four(i, _):
            a, b = i // 3, i % 3
            here = (y, a) if w == 0 else (a, z)
            total = part[here[0], here[1], b].astype(F32)
            for d in range(2):
                total = total + f_buf[w, d, a, b].astype(F32)
            part[here[0], here[1], b] = total.astype(BF)
            return 0

        lax.fori_loop(0, 12, add_four, 0)
        for d in range(1, 4):
            part_copy(w, 1, d).start()
    lax.fori_loop(0, NB, hidden, 0)
    back((z + 2) % 4)
    part_copy(1, 0, 0).start()
    part_copy(1, 0, 1).start()
    mix_go(0)
    lax.fori_loop(0, HALF, grad_one, 0)
    pl.semaphore_wait(free_sem, 1)
    grad_copy(1, 6).start()
    pass_stage(0)
    mix_go(1)
    back_go(0)
    lax.fori_loop(HALF, NB, grad_one, 0)
    grad_copy(1, 7).start()
    last_stage(0, keep_two, scale2)
    lanes_sent(0)
    lax.fori_loop(0, 32, lanes_back, 0)
    lanes_go(1)
    back_go(1)
    pair_stage(1)
    mix(y)
    part_turn(0)
    back(z)
    lanes_turn(1, 0)
    part_turn(1)
    lanes_turn(1, 1)
    pass_stage(1)
    for w, out in ((0, mixed), (1, dxo)):
        for d in range(1, 4):
            part_copy(w, 1, d).wait_recv()
        for b in range(3):
            total = parts[w][y, z, b].astype(F32)
            for d in range(3):
                total = total + f_fin[w, d, b].astype(F32)
            out[:, b * 128 : (b + 1) * 128] = total.astype(BF)
    lanes_end(1)

    def slot_out(s, _):
        i = tab[SLOT_LANE + s]
        got = rback[i // 16, (i // 4) % 4, i % 4]
        o2[s] = jnp.where(s < tab[SLOTS_HERE], got, jnp.zeros_like(got))
        return 0

    lax.fori_loop(0, CAP, slot_out, 0)

    def keep_one(g, k, value):
        o1[g, k] = value

    last_stage(1, keep_one, scale1)
    lanes_sent(1)
    for w in range(2):
        for i in range(10):
            weight_copy(w, i).wait_send()
        for group in range(5):
            for i in range(4):
                feature_copy(w, group, i).wait_send()
        for i in range(8):
            grad_copy(w, i).wait_send()
        for d in range(6):
            part_copy(w, 0, d).wait_send()
        for d in range(1, 4):
            part_copy(w, 1, d).wait_send()


OWN_SLOT, HOME_LOCAL, HOME_LANE, HOME_Q, SLOT_LANE, SLOTS_HERE, SPARE = 0, 32, 64, 80, 96, 120, 128


def table_kernel(owner, rows, cols, tab, kv, count, pairs):
    t = lax.axis_index("tensor")
    for i in range(16):
        count[i] = 0
    for i in range(32):
        tab[OWN_SLOT + i] = 0
        tab[HOME_LOCAL + i] = 0
    for s in range(CAP):
        tab[SLOT_LANE + s] = 0

    def source(src, _):
        seen = []
        for i in range(16):
            pairs[i] = 0
        for i in range(NB):
            o = owner[src * NB + i]
            slot, pair = count[o], pairs[o]
            count[o] = slot + 1
            pairs[o] = pair + 1
            here = o == t
            tab[jnp.where(here, OWN_SLOT + pair * 16 + src, SPARE)] = slot
            tab[jnp.where(here, SLOT_LANE + slot, SPARE + 1)] = pair * 16 + src

            seen.append((o, slot, pair))

        @pl.when(src == t)
        def _():
            for i, (o, slot, pair) in enumerate(seen):
                tab[HOME_LANE + i] = pair * 16 + o
                tab[HOME_Q + i] = o * CAP + slot
                tab[HOME_LOCAL + pair * 16 + o] = i

        return 0

    lax.fori_loop(0, 16, source, 0)
    tab[SLOTS_HERE] = count[t]

    def inverse(g, _):
        for j in range(48):
            kv[g, j] = NK
            kv[NB + g, j] = NK
        q = tab[HOME_Q + g]
        for k in range(NK):
            kv[g, rows[k, t * NB + g]] = k
            kv[NB + g, cols[k, q]] = k
        return 0

    lax.fori_loop(0, NB, inverse, 0)


def hand_over(*refs):
    src, dst, kept, sem = refs[:4], refs[4:8], refs[8:12], refs[12]
    loads = [pltpu.make_async_copy(src[i], kept[i], sem.at[0, i]) for i in range(4)]
    stores = [pltpu.make_async_copy(kept[i], dst[i], sem.at[1, i]) for i in range(4)]
    for i in (3, 2, 0, 1):
        loads[i].start()
    for i in (3, 2, 0, 1):
        loads[i].wait()
        stores[i].start()
    for cp in stores:
        cp.wait()


VM = pl.BlockSpec(memory_space=pltpu.VMEM)
SM = pl.BlockSpec(memory_space=pltpu.SMEM)
ANY = pl.BlockSpec(memory_space=pl.ANY)
SHARD = (NB, NK, 16, 128)
LANES = (2, 4, 4, NK, 16, 128)


def local(tokens, cotangent, w1_blocks, w1_rows, w1_scale, w2_blocks, w2_cols, w2_scale, owner):
    dma = pltpu.SemaphoreType.DMA
    part = (4, 4, 3, 192, 128)
    outs = [
        jax.ShapeDtypeStruct((192, 384), BF),
        jax.ShapeDtypeStruct((192, 384), BF),
        jax.ShapeDtypeStruct(SHARD, BF),
        jax.ShapeDtypeStruct((CAP, NK, 16, 128), BF),
    ]
    tab, kv = pl.pallas_call(
        table_kernel,
        out_shape=[
            jax.ShapeDtypeStruct((256,), jnp.int32),
            jax.ShapeDtypeStruct((2 * NB, 48), jnp.int32),
        ],
        in_specs=[SM] * 3,
        out_specs=[SM] * 2,
        scratch_shapes=[pltpu.SMEM((16,), jnp.int32), pltpu.SMEM((16,), jnp.int32)],
    )(owner, w1_rows.T, w2_cols.T)
    results = pl.pallas_call(
        layer_kernel,
        out_shape=outs,
        in_specs=[ANY] * 4 + [SM] * 6,
        out_specs=[VM] * 4,
        scratch_shapes=[
            pltpu.VMEM(SHARD, BF),
            pltpu.VMEM((CAP, NK, 16, 128), BF),
            pltpu.VMEM((48, 192, 128), BF),
            pltpu.VMEM((48, 192, 128), BF),
            pltpu.VMEM((8, NB, NK + 1, 16, 128), BF),
            pltpu.VMEM((8, NB, NK + 1, 16, 128), BF),
            pltpu.VMEM(LANES, BF),
            pltpu.VMEM(LANES, BF),
            pltpu.VMEM(LANES, BF),
            pltpu.VMEM((2,) + LANES, BF),
            pltpu.VMEM((48, 128, 192), BF),
            pltpu.VMEM((NB, 192, 128), F32),
            pltpu.VMEM((192, NB * 128), BF),
            pltpu.VMEM((192, NB * 128), BF),
            pltpu.VMEM((4, 2) + SHARD, BF),
            pltpu.VMEM((4, 2) + SHARD, BF),
            pltpu.VMEM((4,) + SHARD, BF),
            pltpu.VMEM((2, 2, HALF, NK, 16, 128), BF),
            pltpu.VMEM((2, 2) + SHARD, BF),
            pltpu.VMEM(part, BF),
            pltpu.VMEM(part, BF),
            pltpu.VMEM((2, 2, 4, 3, 192, 128), BF),
            pltpu.VMEM((2, 2, 2, 3, 192, 128), BF),
            pltpu.VMEM((2, 3, 3, 192, 128), BF),
            dma((2, 2, 2, 4, 2)),
            dma((2, 2, 2, 4, 2)),
            dma((2, 10)),
            dma((2, 10)),
            dma((2, 5, 4)),
            dma((2, 5, 4)),
            dma((2, 8)),
            dma((2, 8)),
            dma((2, 2, 6)),
            dma((2, 2, 6)),
            dma((8,)),
            pltpu.SemaphoreType.REGULAR,
        ],
        compiler_params=pltpu.CompilerParams(
            collective_id=0, has_side_effects=True, vmem_limit_bytes=(64 << 20) - (64 << 10)
        ),
    )(
        tokens,
        cotangent,
        w1_blocks,
        w2_blocks,
        w1_scale.T,
        w2_scale.T,
        w1_rows.T,
        w2_cols.T,
        tab,
        kv,
    )
    return pl.pallas_call(
        hand_over,
        out_shape=outs,
        in_specs=[ANY] * 4,
        out_specs=[ANY] * 4,
        scratch_shapes=[pltpu.VMEM(o.shape, BF) for o in outs] + [dma((2, 4))],
    )(*results)


def solution(mesh):
    in_specs = (
        P("dp", "tensor"),
        P("dp", "tensor"),
        P("tensor", None, "dp", None),
        P(),
        P(),
        P("tensor", None, "dp", None),
        P(),
        P(),
        P(),
    )
    out_specs = (
        P("dp", "tensor"),
        P("dp", "tensor"),
        P("tensor", None, "dp", None),
        P("tensor", None, "dp", None),
    )
    return jax.shard_map(local, mesh=mesh, in_specs=in_specs, out_specs=out_specs, check_vma=False)
```

```python
import jax
import jax.numpy as jnp
from jax import lax
from jax.experimental import pallas as pl
from jax.experimental.pallas import tpu as pltpu
from jax.sharding import PartitionSpec as P

GELU_C = 0.7978845608028654
GELU_A = 0.044715
MESH = pl.DeviceIdType.MESH
BF = jnp.bfloat16
F32 = jnp.float32
NB = 12
NK = 15
CAP = 18
HALF = NB // 2


def where_am_i():
    p = lax.axis_index("dp")
    t = lax.axis_index("tensor")
    return p, t, p // 2, p % 2, t // 4, t % 4


def enter(p, t, x, c, y, z):
    barrier = pltpu.get_barrier_semaphore()
    for d in range(1, 4):
        for peer in (((y + d) % 4) * 4 + z, y * 4 + (z + d) % 4):
            pl.semaphore_signal(barrier, inc=1, device_id=(p, peer), device_id_type=MESH)
    for q in (2 * ((x + 1) % 4) + c, 2 * ((x + 3) % 4) + c, 2 * x + 1 - c):
        pl.semaphore_signal(barrier, inc=1, device_id=(q, t), device_id_type=MESH)
    return barrier


def layer_kernel(
    tok_ref,
    cot_ref,
    w1_ref,
    w2_ref,
    s1_ref,
    s2_ref,
    rows_ref,
    cols_ref,
    tab,
    kv_ref,
    mixed,
    dxo,
    o1,
    o2,
    w1in,
    w2in,
    xall,
    dyall,
    w1all,
    w2all,
    lanes,
    rbuf,
    rback,
    middle,
    xt,
    slope,
    act_all,
    dpre_all,
    g1s,
    g2s,
    sib,
    fwd,
    fin,
    m_part,
    d_part,
    f_buf,
    f_hop,
    f_fin,
    a_send,
    a_recv,
    w_send,
    w_recv,
    x_send,
    x_recv,
    g_send,
    g_recv,
    f_send,
    f_recv,
    l_sem,
    free_sem,
):
    p, t, x, c, y, z = where_am_i()
    barrier = enter(p, t, x, c, y, z)
    xr, xl, xo = (x + 1) % 4, (x + 3) % 4, (x + 2) % 4
    rp, lp, op, sp = 2 * xr + c, 2 * xl + c, 2 * xo + c, 2 * x + 1 - c
    halves = (pl.ds(0, HALF), pl.ds(HALF, HALF))
    first, second = halves
    whole = pl.ds(0, NB)
    feats = (xall, dyall)
    weights = (w1all, w2all)
    grads = (g2s, g1s)
    parts = (m_part, d_part)
    landed = (rbuf, rback)
    nt = (((1,), (1,)), ((), ()))

    def row(g, k):
        return rows_ref[k, t * NB + g]

    def col(g, k):
        return cols_ref[k, tab[HOME_Q + g]]

    def scale1(g, k):
        return s1_ref[k, t * NB + g]

    def scale2(g, k):
        return s2_ref[k, tab[HOME_Q + g]]

    def lane_copy(trip, j, step, d, piece):
        along_y = (j == 0) == (step == 0)
        peer_y, peer_z = ((y + d) % 4, z) if along_y else (y, (z + d) % 4)
        ks = (pl.ds(0, 8), pl.ds(8, NK - 8))[piece]
        src = lanes.at[j] if step == 0 else middle.at[trip, j]
        dst = middle.at[trip, j] if step == 0 else landed[trip].at[j]
        return pltpu.make_async_remote_copy(
            src.at[peer_y, :, ks] if along_y else src.at[:, peer_z, ks],
            dst.at[y, :, ks] if along_y else dst.at[:, z, ks],
            a_send.at[trip, j, step, d, piece],
            a_recv.at[trip, j, step, d, piece],
            device_id=(p, peer_y * 4 + peer_z),
            device_id_type=MESH,
        )

    def lanes_go(trip):
        for piece in range(2):
            for d in (2, 1, 3):
                for j in range(2):
                    lane_copy(trip, j, 0, d, piece).start()
        middle[trip, 0, y] = lanes[0, y]
        middle[trip, 1, :, z] = lanes[1, :, z]

    def lanes_turn(trip, piece):
        for j in range(2):
            for d in range(1, 4):
                lane_copy(trip, j, 0, d, piece).wait_recv()
            for d in (2, 1, 3):
                lane_copy(trip, j, 1, d, piece).start()

    def lanes_end(trip):
        landed[trip][0, :, z] = middle[trip, 0, :, z]
        landed[trip][1, y] = middle[trip, 1, y]
        for piece in range(2):
            for j in range(2):
                for d in range(1, 4):
                    lane_copy(trip, j, 1, d, piece).wait_recv()

    def lanes_sent(trip):
        for j in range(2):
            for step in range(2):
                for d in range(1, 4):
                    for piece in range(2):
                        lane_copy(trip, j, step, d, piece).wait_send()

    def weight_copy(w, i):
        who, part, dev = (
            (p, first, rp),
            (p, second, rp),
            (p, second, lp),
            (p, first, lp),
            (p, whole, sp),
            (lp, first, rp),
            (rp, second, lp),
            (lp, whole, sp),
            (rp, whole, sp),
            (op, whole, sp),
        )[i]
        ref = weights[w].at[who, part, pl.ds(0, NK)]
        return pltpu.make_async_remote_copy(
            ref, ref, w_send.at[w, i], w_recv.at[w, i], device_id=(dev, t), device_id_type=MESH
        )

    def feature_copy(w, group, i):
        along_y = (w == 0) == (group == 0)
        came = 0 if group == 0 else group - 1
        on = (0, 0, 1, 3)[i]
        if along_y:
            holder = ((y + 4 - on) % 4) * 4 + (z + 4 - came) % 4
        else:
            holder = ((y + 4 - came) % 4) * 4 + (z + 4 - on) % 4
        d = (1, 3, 1, 3)[i]
        peer = ((y + d) % 4) * 4 + z if along_y else y * 4 + (z + d) % 4
        ref = feats[w].at[pl.ds(3 * holder, 3)]
        if i >= 2:
            ref = ref.at[:, pl.ds(96 * (i - 2), 96)]
        return pltpu.make_async_remote_copy(
            ref,
            ref,
            x_send.at[w, group, i],
            x_recv.at[w, group, i],
            device_id=(p, peer),
            device_id_type=MESH,
        )

    def grad_copy(w, i):
        own = grads[w]
        src, dst, dev = (
            (own.at[xo, c, first], fwd.at[w, 0], rp),
            (own.at[xo, c, second], fwd.at[w, 1], lp),
            (own.at[xr, c, second], fin.at[w, 0, second], rp),
            (own.at[xl, c, first], fin.at[w, 1, first], lp),
            (own.at[xr, c, first], fin.at[w, 0, first], rp),
            (own.at[xl, c, second], fin.at[w, 1, second], lp),
            (own.at[:, 1 - c, first], sib.at[:, first], sp),
            (own.at[:, 1 - c, second], sib.at[:, second], sp),
        )[i]
        return pltpu.make_async_remote_copy(
            src, dst, g_send.at[w, i], g_recv.at[w, i], device_id=(dev, t), device_id_type=MESH
        )

    def shards_of(w, place, lo, n):
        return (place, pl.ds(lo, n)) if w == 0 else (pl.ds(lo, n), place)

    def part_copy(w, step, d):
        along_y = (w == 0) == (step == 0)
        if step == 0:
            here = y if w == 0 else z
            up, down, far = (here + 1) % 4, (here + 3) % 4, (here + 2) % 4
            place, lo, dst, to = (
                (far, 0, f_hop.at[w, 0], 1),
                (far, 2, f_hop.at[w, 1], 3),
                (up, 2, f_buf.at[w, 0, pl.ds(2, 2)], 1),
                (down, 0, f_buf.at[w, 1, pl.ds(0, 2)], 3),
                (up, 0, f_buf.at[w, 0, pl.ds(0, 2)], 1),
                (down, 2, f_buf.at[w, 1, pl.ds(2, 2)], 3),
            )[d]
            src = parts[w].at[shards_of(w, place, lo, 2)]
            peer_y, peer_z = ((y + to) % 4, z) if along_y else (y, (z + to) % 4)
        else:
            peer_y, peer_z = ((y + d) % 4, z) if along_y else (y, (z + d) % 4)
            src = parts[w].at[peer_y, peer_z]
            dst = f_fin.at[w, d - 1]
        return pltpu.make_async_remote_copy(
            src,
            dst,
            f_send.at[w, step, d],
            f_recv.at[w, step, d],
            device_id=(p, peer_y * 4 + peer_z),
            device_id_type=MESH,
        )

    def part_on(w, way):
        here = y if w == 0 else z
        place = (here + (1, 3)[way]) % 4
        part = parts[w]
        part_copy(w, 0, way).wait_recv()

        def add(i, _):
            a, b = i // 3 + 2 * way, i % 3
            at = (place, a) if w == 0 else (a, place)
            total = part[at[0], at[1], b].astype(F32) + f_hop[w, way, i // 3, b].astype(F32)
            part[at[0], at[1], b] = total.astype(BF)
            return 0

        lax.fori_loop(0, 6, add, 0)
        part_copy(w, 0, 4 + way).start()

    loads = [
        pltpu.make_async_copy(w2_ref, w2in, l_sem.at[0]),
        pltpu.make_async_copy(w1_ref, w1in, l_sem.at[1]),
    ]
    for w, ref in enumerate((tok_ref, cot_ref)):
        for b in range(3):
            loads.append(
                pltpu.make_async_copy(
                    ref.at[:, pl.ds(b * 128, 128)],
                    feats[w].at[3 * t + b],
                    l_sem.at[2 + 3 * w + b],
                )
            )
    for cp in loads:
        cp.start()
    loads[0].wait()

    def lanes_out(i, _):
        s = tab[OWN_SLOT + i]
        lanes[i // 16, (i // 4) % 4, i % 4] = w2in[s]
        return 0

    lax.fori_loop(0, 32, lanes_out, 0)
    pl.semaphore_wait(barrier, 9)
    lanes_go(0)
    loads[1].wait()

    def scale_one(g, _):
        for k in range(NK):
            w1all[p, g, k] = (w1in[g, k].astype(F32) * scale1(g, k)).astype(BF)
        return 0

    lax.fori_loop(0, NB, scale_one, 0)
    for i in range(5):
        weight_copy(0, i).start()
    w1all[:, :, NK] = jnp.zeros((8, NB, 16, 128), BF)
    w2all[:, :, NK] = jnp.zeros((8, NB, 16, 128), BF)
    for cp in loads[2:]:
        cp.wait()

    def weights_on(w):
        weight_copy(w, 0).wait_recv()
        weight_copy(w, 5).start()
        weight_copy(w, 2).wait_recv()
        weight_copy(w, 6).start()
        weight_copy(w, 1).wait_recv()
        weight_copy(w, 7).start()
        weight_copy(w, 3).wait_recv()
        weight_copy(w, 8).start()

    def weights_last(w):
        weight_copy(w, 5).wait_recv()
        weight_copy(w, 6).wait_recv()
        weight_copy(w, 9).start()

    lanes_turn(0, 0)
    lanes_turn(0, 1)
    for group in (0, 1):
        for w in range(2):
            for i in range(2):
                feature_copy(w, group, i).start()
    weights_on(0)
    lanes_end(0)

    def scale_two(g, _):
        i = tab[HOME_LANE + g]
        for k in range(NK):
            w2all[p, g, k] = (rbuf[i // 16, (i // 4) % 4, i % 4, k].astype(F32) * scale2(g, k)).astype(BF)
        return 0

    lax.fori_loop(0, NB, scale_two, 0)
    for i in range(5):
        weight_copy(1, i).start()

    def feature_on(w, group):
        for i in range(2):
            feature_copy(w, group, i).wait_recv()
            feature_copy(w, group, i + 2).start()
            if group == 0:
                for k in range(2):
                    feature_copy(w, (2, 4)[i], k).start()

    for w in range(2):
        feature_on(w, 0)
    for w in range(2):
        feature_on(w, 1)
    weights_last(0)
    for w in range(2):
        for i in (2, 3):
            feature_copy(w, 0, i).wait_recv()
        for k in range(2):
            feature_copy(w, 3, k).start()
    for group in (2, 4):
        for w in range(2):
            feature_on(w, group)
    weights_on(1)
    for w in range(2):
        feature_on(w, 3)
    for group in range(1, 5):
        for w in range(2):
            for i in (2, 3):
                feature_copy(w, group, i).wait_recv()
    for i in (4, 7, 8, 9):
        weight_copy(0, i).wait_recv()

    def project(g, _):
        w1c = jnp.concatenate([w1all[:, g, k].reshape(128, 128) for k in range(NK)], axis=0)
        xs = jnp.concatenate([xall[row(g, k)] for k in range(NK)], axis=1)
        pre = jnp.dot(xs, w1c, preferred_element_type=F32)
        th = jnp.tanh(GELU_C * (pre + GELU_A * pre * pre * pre))
        act = (0.5 * pre * (1.0 + th)).astype(BF)
        slope[g] = 0.5 * (1.0 + th) + 0.5 * pre * (1.0 - th * th) * GELU_C * (
            1.0 + 3.0 * GELU_A * pre * pre
        )
        act_all[:, pl.ds(pl.multiple_of(g * 128, 128), 128)] = act
        dys = jnp.concatenate([dyall[col(g, k)] for k in range(NK)], axis=1)
        gw2 = jnp.dot(act.T, dys, preferred_element_type=F32).astype(BF)
        for k in range(NK):
            g2s[:, :, g, k] = gw2[:, k * 128 : (k + 1) * 128].reshape(4, 2, 16, 128)
        return 0

    def flip(j, _):
        xt[j] = xall[j].T
        return 0

    lax.fori_loop(0, HALF, project, 0)
    grad_copy(0, 6).start()
    weights_last(1)
    lax.fori_loop(HALF, NB, project, 0)
    grad_copy(0, 7).start()
    lax.fori_loop(0, 48, flip, 0)

    def pair_sum(w, chunk, h):
        own = grads[w]

        def body(g, _):
            own[chunk, c, g] = (own[chunk, c, g].astype(F32) + sib[chunk, g].astype(F32)).astype(BF)
            return 0

        lax.fori_loop(h * HALF, (h + 1) * HALF, body, 0)

    def pair_stage(w):
        grad_copy(w, 6).wait_recv()
        pair_sum(w, xo, 0)
        grad_copy(w, 0).start()
        pair_sum(w, xl, 0)
        grad_copy(w, 3).start()
        grad_copy(w, 7).wait_recv()
        pair_sum(w, xo, 1)
        grad_copy(w, 1).start()
        pair_sum(w, xr, 1)
        grad_copy(w, 2).start()
        pair_sum(w, xr, 0)
        pair_sum(w, xl, 1)
        pair_sum(w, x, 0)
        pair_sum(w, x, 1)

    def pass_stage(w):
        own = grads[w]
        grad_copy(w, 0).wait_recv()

        def right(g, _):
            own[xr, c, g] = (own[xr, c, g].astype(F32) + fwd[w, 0, g].astype(F32)).astype(BF)
            return 0

        lax.fori_loop(0, HALF, right, 0)
        grad_copy(w, 4).start()
        grad_copy(w, 1).wait_recv()

        def left(g, _):
            own[xl, c, g + HALF] = (
                own[xl, c, g + HALF].astype(F32) + fwd[w, 1, g].astype(F32)
            ).astype(BF)
            return 0

        lax.fori_loop(0, HALF, left, 0)
        grad_copy(w, 5).start()

    def last_stage(w, out, scale):
        own = grads[w]
        for i in (2, 3, 4, 5):
            grad_copy(w, i).wait_recv()

        def body(g, _):
            for k in range(NK):
                total = own[x, c, g, k].astype(F32) + fin[w, 0, g, k].astype(F32)
                total = total + fin[w, 1, g, k].astype(F32)
                out(g, k, (total * scale(g, k)).astype(BF))
            return 0

        lax.fori_loop(0, NB, body, 0)

    def mix(to_y):
        def body(i, _):
            j = 12 * to_y + 2 * i
            panel = jnp.concatenate(
                [
                    jnp.concatenate(
                        [w2all[:, g, kv_ref[NB + g, j + b]].reshape(128, 128) for g in range(NB)], axis=0
                    )
                    for b in range(2)
                ],
                axis=1,
            )
            res = jnp.dot(act_all[...], panel, preferred_element_type=F32).astype(BF)
            for b in range(2):
                at = 2 * i + b
                m_part[to_y, at // 3, at % 3] = res[:, b * 128 : (b + 1) * 128]
            return 0

        lax.fori_loop(0, 6, body, 0)

    def back(to_z):
        def body(i, _):
            at = (2 * i, 2 * i + 1)
            panel = jnp.concatenate(
                [
                    jnp.concatenate(
                        [
                            w1all[:, g, kv_ref[g, 12 * (a // 3) + 3 * to_z + a % 3]].reshape(128, 128)
                            for g in range(NB)
                        ],
                        axis=1,
                    )
                    for a in at
                ],
                axis=0,
            )
            res = lax.dot_general(dpre_all[...], panel, nt, preferred_element_type=F32).astype(BF)
            for b, a in enumerate(at):
                d_part[a // 3, to_z, a % 3] = res[:, b * 128 : (b + 1) * 128]
            return 0

        lax.fori_loop(0, 6, body, 0)

    for i in (4, 7, 8, 9):
        weight_copy(1, i).wait_recv()
    pair_stage(0)
    pl.semaphore_signal(free_sem, inc=1, device_id=(sp, t), device_id_type=MESH)
    mix((y + 2) % 4)
    part_copy(0, 0, 0).start()
    part_copy(0, 0, 1).start()
    def hidden(g, _):
        w2c = jnp.concatenate([w2all[:, g, k].reshape(128, 128) for k in range(NK)], axis=1)
        dys = jnp.concatenate([dyall[col(g, k)] for k in range(NK)], axis=1)
        dact = lax.dot_general(dys, w2c, nt, preferred_element_type=F32).astype(BF)
        dpre = (dact.astype(F32) * slope[g]).astype(BF)
        dpre_all[:, pl.ds(pl.multiple_of(g * 128, 128), 128)] = dpre
        return 0

    def grad_one(g, _):
        dpre = dpre_all[:, pl.ds(pl.multiple_of(g * 128, 128), 128)]
        for k in range(NK):
            gw1 = jnp.dot(xt[row(g, k)], dpre, preferred_element_type=F32).astype(BF)
            g1s[:, :, g, k] = gw1.reshape(4, 2, 16, 128)
        return 0

    def keep_two(g, k, value):
        g2s[x, c, g, k] = value

    def lanes_back(i, _):
        s = tab[HOME_LOCAL + i]
        lanes[i // 16, (i // 4) % 4, i % 4] = g2s[x, c, s]
        return 0

    def mix_go(way):
        mix((y + (1, 3)[way]) % 4)
        part_copy(0, 0, 2 + way).start()
        part_on(0, way)

    def back_go(way):
        back((z + (1, 3)[way]) % 4)
        part_copy(1, 0, 2 + way).start()
        part_on(1, way)

    def part_turn(w):
        for d in range(2, 6):
            part_copy(w, 0, d).wait_recv()
        part = parts[w]

        def add_four(i, _):
            a, b = i // 3, i % 3
            here = (y, a) if w == 0 else (a, z)
            total = part[here[0], here[1], b].astype(F32)
            for d in range(2):
                total = total + f_buf[w, d, a, b].astype(F32)
            part[here[0], here[1], b] = total.astype(BF)
            return 0

        lax.fori_loop(0, 12, add_four, 0)
        for d in range(1, 4):
            part_copy(w, 1, d).start()
    lax.fori_loop(0, NB, hidden, 0)
    back((z + 2) % 4)
    part_copy(1, 0, 0).start()
    part_copy(1, 0, 1).start()
    mix_go(0)
    lax.fori_loop(0, HALF, grad_one, 0)
    pl.semaphore_wait(free_sem, 1)
    grad_copy(1, 6).start()
    pass_stage(0)
    mix_go(1)
    back_go(0)
    lax.fori_loop(HALF, NB, grad_one, 0)
    grad_copy(1, 7).start()
    last_stage(0, keep_two, scale2)
    lanes_sent(0)
    lax.fori_loop(0, 32, lanes_back, 0)
    lanes_go(1)
    back_go(1)
    pair_stage(1)
    mix(y)
    part_turn(0)
    back(z)
    lanes_turn(1, 0)
    part_turn(1)
    lanes_turn(1, 1)
    pass_stage(1)
    for w, out in ((0, mixed), (1, dxo)):
        for d in range(1, 4):
            part_copy(w, 1, d).wait_recv()
        for b in range(3):
            total = parts[w][y, z, b].astype(F32)
            for d in range(3):
                total = total + f_fin[w, d, b].astype(F32)
            out[:, b * 128 : (b + 1) * 128] = total.astype(BF)
    lanes_end(1)

    def slot_out(s, _):
        i = tab[SLOT_LANE + s]
        got = rback[i // 16, (i // 4) % 4, i % 4]
        o2[s] = jnp.where(s < tab[SLOTS_HERE], got, jnp.zeros_like(got))
        return 0

    lax.fori_loop(0, CAP, slot_out, 0)

    def keep_one(g, k, value):
        o1[g, k] = value

    last_stage(1, keep_one, scale1)
    lanes_sent(1)
    for w in range(2):
        for i in range(10):
            weight_copy(w, i).wait_send()
        for group in range(5):
            for i in range(4):
                feature_copy(w, group, i).wait_send()
        for i in range(8):
            grad_copy(w, i).wait_send()
        for d in range(6):
            part_copy(w, 0, d).wait_send()
        for d in range(1, 4):
            part_copy(w, 1, d).wait_send()


OWN_SLOT, HOME_LOCAL, HOME_LANE, HOME_Q, SLOT_LANE, SLOTS_HERE, SPARE = 0, 32, 64, 80, 96, 120, 128


def table_kernel(owner, rows, cols, tab, kv, count, pairs):
    t = lax.axis_index("tensor")
    for i in range(16):
        count[i] = 0
    for i in range(32):
        tab[OWN_SLOT + i] = 0
        tab[HOME_LOCAL + i] = 0
    for s in range(CAP):
        tab[SLOT_LANE + s] = 0

    def source(src, _):
        seen = []
        for i in range(16):
            pairs[i] = 0
        for i in range(NB):
            o = owner[src * NB + i]
            slot, pair = count[o], pairs[o]
            count[o] = slot + 1
            pairs[o] = pair + 1
            here = o == t
            tab[jnp.where(here, OWN_SLOT + pair * 16 + src, SPARE)] = slot
            tab[jnp.where(here, SLOT_LANE + slot, SPARE + 1)] = pair * 16 + src

            seen.append((o, slot, pair))

        @pl.when(src == t)
        def _():
            for i, (o, slot, pair) in enumerate(seen):
                tab[HOME_LANE + i] = pair * 16 + o
                tab[HOME_Q + i] = o * CAP + slot
                tab[HOME_LOCAL + pair * 16 + o] = i

        return 0

    lax.fori_loop(0, 16, source, 0)
    tab[SLOTS_HERE] = count[t]

    def inverse(g, _):
        for j in range(48):
            kv[g, j] = NK
            kv[NB + g, j] = NK
        q = tab[HOME_Q + g]
        for k in range(NK):
            kv[g, rows[k, t * NB + g]] = k
            kv[NB + g, cols[k, q]] = k
        return 0

    lax.fori_loop(0, NB, inverse, 0)


def hand_over(*refs):
    src, dst, kept, sem = refs[:4], refs[4:8], refs[8:12], refs[12]
    loads = [pltpu.make_async_copy(src[i], kept[i], sem.at[0, i]) for i in range(4)]
    stores = [pltpu.make_async_copy(kept[i], dst[i], sem.at[1, i]) for i in range(4)]
    for i in (3, 2, 0, 1):
        loads[i].start()
    for i in (3, 2, 0, 1):
        loads[i].wait()
        stores[i].start()
    for cp in stores:
        cp.wait()


VM = pl.BlockSpec(memory_space=pltpu.VMEM)
SM = pl.BlockSpec(memory_space=pltpu.SMEM)
ANY = pl.BlockSpec(memory_space=pl.ANY)
SHARD = (NB, NK, 16, 128)
LANES = (2, 4, 4, NK, 16, 128)


def local(tokens, cotangent, w1_blocks, w1_rows, w1_scale, w2_blocks, w2_cols, w2_scale, owner):
    dma = pltpu.SemaphoreType.DMA
    part = (4, 4, 3, 192, 128)
    outs = [
        jax.ShapeDtypeStruct((192, 384), BF),
        jax.ShapeDtypeStruct((192, 384), BF),
        jax.ShapeDtypeStruct(SHARD, BF),
        jax.ShapeDtypeStruct((CAP, NK, 16, 128), BF),
    ]
    tab, kv = pl.pallas_call(
        table_kernel,
        out_shape=[
            jax.ShapeDtypeStruct((256,), jnp.int32),
            jax.ShapeDtypeStruct((2 * NB, 48), jnp.int32),
        ],
        in_specs=[SM] * 3,
        out_specs=[SM] * 2,
        scratch_shapes=[pltpu.SMEM((16,), jnp.int32), pltpu.SMEM((16,), jnp.int32)],
    )(owner, w1_rows.T, w2_cols.T)
    results = pl.pallas_call(
        layer_kernel,
        out_shape=outs,
        in_specs=[ANY] * 4 + [SM] * 6,
        out_specs=[VM] * 4,
        scratch_shapes=[
            pltpu.VMEM(SHARD, BF),
            pltpu.VMEM((CAP, NK, 16, 128), BF),
            pltpu.VMEM((48, 192, 128), BF),
            pltpu.VMEM((48, 192, 128), BF),
            pltpu.VMEM((8, NB, NK + 1, 16, 128), BF),
            pltpu.VMEM((8, NB, NK + 1, 16, 128), BF),
            pltpu.VMEM(LANES, BF),
            pltpu.VMEM(LANES, BF),
            pltpu.VMEM(LANES, BF),
            pltpu.VMEM((2,) + LANES, BF),
            pltpu.VMEM((48, 128, 192), BF),
            pltpu.VMEM((NB, 192, 128), F32),
            pltpu.VMEM((192, NB * 128), BF),
            pltpu.VMEM((192, NB * 128), BF),
            pltpu.VMEM((4, 2) + SHARD, BF),
            pltpu.VMEM((4, 2) + SHARD, BF),
            pltpu.VMEM((4,) + SHARD, BF),
            pltpu.VMEM((2, 2, HALF, NK, 16, 128), BF),
            pltpu.VMEM((2, 2) + SHARD, BF),
            pltpu.VMEM(part, BF),
            pltpu.VMEM(part, BF),
            pltpu.VMEM((2, 2, 4, 3, 192, 128), BF),
            pltpu.VMEM((2, 2, 2, 3, 192, 128), BF),
            pltpu.VMEM((2, 3, 3, 192, 128), BF),
            dma((2, 2, 2, 4, 2)),
            dma((2, 2, 2, 4, 2)),
            dma((2, 10)),
            dma((2, 10)),
            dma((2, 5, 4)),
            dma((2, 5, 4)),
            dma((2, 8)),
            dma((2, 8)),
            dma((2, 2, 6)),
            dma((2, 2, 6)),
            dma((8,)),
            pltpu.SemaphoreType.REGULAR,
        ],
        compiler_params=pltpu.CompilerParams(
            collective_id=0, has_side_effects=True, vmem_limit_bytes=(64 << 20) - (64 << 10)
        ),
    )(
        tokens,
        cotangent,
        w1_blocks,
        w2_blocks,
        w1_scale.T,
        w2_scale.T,
        w1_rows.T,
        w2_cols.T,
        tab,
        kv,
    )
    return pl.pallas_call(
        hand_over,
        out_shape=outs,
        in_specs=[ANY] * 4,
        out_specs=[ANY] * 4,
        scratch_shapes=[pltpu.VMEM(o.shape, BF) for o in outs] + [dma((2, 4))],
    )(*results)


def solution(mesh):
    in_specs = (
        P("dp", "tensor"),
        P("dp", "tensor"),
        P("tensor", None, "dp", None),
        P(),
        P(),
        P("tensor", None, "dp", None),
        P(),
        P(),
        P(),
    )
    out_specs = (
        P("dp", "tensor"),
        P("dp", "tensor"),
        P("tensor", None, "dp", None),
        P("tensor", None, "dp", None),
    )
    return jax.shard_map(local, mesh=mesh, in_specs=in_specs, out_specs=out_specs, check_vma=False)
```

```python
import jax
import jax.numpy as jnp
from jax import lax
from jax.experimental import pallas as pl
from jax.experimental.pallas import tpu as pltpu
from jax.sharding import PartitionSpec as P

GELU_C = 0.7978845608028654
GELU_A = 0.044715
MESH = pl.DeviceIdType.MESH
BF = jnp.bfloat16
F32 = jnp.float32
NB = 12
NK = 15
CAP = 18
HALF = NB // 2


def where_am_i():
    p = lax.axis_index("dp")
    t = lax.axis_index("tensor")
    return p, t, p // 2, p % 2, t // 4, t % 4


def enter(p, t, x, c, y, z):
    barrier = pltpu.get_barrier_semaphore()
    for d in range(1, 4):
        for peer in (((y + d) % 4) * 4 + z, y * 4 + (z + d) % 4):
            pl.semaphore_signal(barrier, inc=1, device_id=(p, peer), device_id_type=MESH)
    for q in (2 * ((x + 1) % 4) + c, 2 * ((x + 3) % 4) + c, 2 * x + 1 - c):
        pl.semaphore_signal(barrier, inc=1, device_id=(q, t), device_id_type=MESH)
    return barrier


def layer_kernel(
    tok_ref,
    cot_ref,
    w1_ref,
    w2_ref,
    s1_ref,
    s2_ref,
    rows_ref,
    cols_ref,
    tab,
    kv_ref,
    mixed,
    dxo,
    o1,
    o2,
    w1in,
    w2in,
    xall,
    dyall,
    w1all,
    w2all,
    lanes,
    rbuf,
    rback,
    middle,
    xt,
    slope,
    act_all,
    dpre_all,
    g1s,
    g2s,
    sib,
    fwd,
    fin,
    m_part,
    d_part,
    f_buf,
    f_hop,
    f_fin,
    a_send,
    a_recv,
    w_send,
    w_recv,
    x_send,
    x_recv,
    g_send,
    g_recv,
    f_send,
    f_recv,
    l_sem,
    free_sem,
):
    p, t, x, c, y, z = where_am_i()
    barrier = enter(p, t, x, c, y, z)
    xr, xl, xo = (x + 1) % 4, (x + 3) % 4, (x + 2) % 4
    rp, lp, op, sp = 2 * xr + c, 2 * xl + c, 2 * xo + c, 2 * x + 1 - c
    halves = (pl.ds(0, HALF), pl.ds(HALF, HALF))
    first, second = halves
    whole = pl.ds(0, NB)
    feats = (xall, dyall)
    weights = (w1all, w2all)
    grads = (g2s, g1s)
    parts = (m_part, d_part)
    landed = (rbuf, rback)
    nt = (((1,), (1,)), ((), ()))

    def row(g, k):
        return rows_ref[k, t * NB + g]

    def col(g, k):
        return cols_ref[k, tab[HOME_Q + g]]

    def scale1(g, k):
        return s1_ref[k, t * NB + g]

    def scale2(g, k):
        return s2_ref[k, tab[HOME_Q + g]]

    def lane_copy(trip, j, step, d, piece):
        along_y = (j == 0) == (step == 0)
        peer_y, peer_z = ((y + d) % 4, z) if along_y else (y, (z + d) % 4)
        ks = (pl.ds(0, 8), pl.ds(8, NK - 8))[piece]
        src = lanes.at[j] if step == 0 else middle.at[trip, j]
        dst = middle.at[trip, j] if step == 0 else landed[trip].at[j]
        return pltpu.make_async_remote_copy(
            src.at[peer_y, :, ks] if along_y else src.at[:, peer_z, ks],
            dst.at[y, :, ks] if along_y else dst.at[:, z, ks],
            a_send.at[trip, j, step, d, piece],
            a_recv.at[trip, j, step, d, piece],
            device_id=(p, peer_y * 4 + peer_z),
            device_id_type=MESH,
        )

    def lanes_go(trip):
        for piece in range(2):
            for d in (2, 1, 3):
                for j in range(2):
                    lane_copy(trip, j, 0, d, piece).start()
        middle[trip, 0, y] = lanes[0, y]
        middle[trip, 1, :, z] = lanes[1, :, z]

    def lanes_turn(trip, piece):
        for j in range(2):
            for d in range(1, 4):
                lane_copy(trip, j, 0, d, piece).wait_recv()
            for d in (2, 1, 3):
                lane_copy(trip, j, 1, d, piece).start()

    def lanes_end(trip):
        landed[trip][0, :, z] = middle[trip, 0, :, z]
        landed[trip][1, y] = middle[trip, 1, y]
        for piece in range(2):
            for j in range(2):
                for d in range(1, 4):
                    lane_copy(trip, j, 1, d, piece).wait_recv()

    def lanes_sent(trip):
        for j in range(2):
            for step in range(2):
                for d in range(1, 4):
                    for piece in range(2):
                        lane_copy(trip, j, step, d, piece).wait_send()

    def weight_copy(w, i):
        who, part, dev = (
            (p, first, rp),
            (p, second, rp),
            (p, second, lp),
            (p, first, lp),
            (p, whole, sp),
            (lp, first, rp),
            (rp, second, lp),
            (lp, whole, sp),
            (rp, whole, sp),
            (op, whole, sp),
        )[i]
        ref = weights[w].at[who, part, pl.ds(0, NK)]
        return pltpu.make_async_remote_copy(
            ref, ref, w_send.at[w, i], w_recv.at[w, i], device_id=(dev, t), device_id_type=MESH
        )

    def feature_copy(w, group, i):
        along_y = (w == 0) == (group == 0)
        came = 0 if group == 0 else group - 1
        on = (0, 0, 1, 3)[i]
        if along_y:
            holder = ((y + 4 - on) % 4) * 4 + (z + 4 - came) % 4
        else:
            holder = ((y + 4 - came) % 4) * 4 + (z + 4 - on) % 4
        d = (1, 3, 1, 3)[i]
        peer = ((y + d) % 4) * 4 + z if along_y else y * 4 + (z + d) % 4
        ref = feats[w].at[pl.ds(3 * holder, 3)]
        if i >= 2:
            ref = ref.at[:, pl.ds(96 * (i - 2), 96)]
        return pltpu.make_async_remote_copy(
            ref,
            ref,
            x_send.at[w, group, i],
            x_recv.at[w, group, i],
            device_id=(p, peer),
            device_id_type=MESH,
        )

    def grad_copy(w, i):
        own = grads[w]
        src, dst, dev = (
            (own.at[xo, c, first], fwd.at[w, 0], rp),
            (own.at[xo, c, second], fwd.at[w, 1], lp),
            (own.at[xr, c, second], fin.at[w, 0, second], rp),
            (own.at[xl, c, first], fin.at[w, 1, first], lp),
            (own.at[xr, c, first], fin.at[w, 0, first], rp),
            (own.at[xl, c, second], fin.at[w, 1, second], lp),
            (own.at[:, 1 - c, first], sib.at[:, first], sp),
            (own.at[:, 1 - c, second], sib.at[:, second], sp),
        )[i]
        return pltpu.make_async_remote_copy(
            src, dst, g_send.at[w, i], g_recv.at[w, i], device_id=(dev, t), device_id_type=MESH
        )

    def shards_of(w, place, lo, n):
        return (place, pl.ds(lo, n)) if w == 0 else (pl.ds(lo, n), place)

    def part_copy(w, step, d):
        along_y = (w == 0) == (step == 0)
        if step == 0:
            here = y if w == 0 else z
            up, down, far = (here + 1) % 4, (here + 3) % 4, (here + 2) % 4
            place, lo, dst, to = (
                (far, 0, f_hop.at[w, 0], 1),
                (far, 2, f_hop.at[w, 1], 3),
                (up, 2, f_buf.at[w, 0, pl.ds(2, 2)], 1),
                (down, 0, f_buf.at[w, 1, pl.ds(0, 2)], 3),
                (up, 0, f_buf.at[w, 0, pl.ds(0, 2)], 1),
                (down, 2, f_buf.at[w, 1, pl.ds(2, 2)], 3),
            )[d]
            src = parts[w].at[shards_of(w, place, lo, 2)]
            peer_y, peer_z = ((y + to) % 4, z) if along_y else (y, (z + to) % 4)
        else:
            peer_y, peer_z = ((y + d) % 4, z) if along_y else (y, (z + d) % 4)
            src = parts[w].at[peer_y, peer_z]
            dst = f_fin.at[w, d - 1]
        return pltpu.make_async_remote_copy(
            src,
            dst,
            f_send.at[w, step, d],
            f_recv.at[w, step, d],
            device_id=(p, peer_y * 4 + peer_z),
            device_id_type=MESH,
        )

    def part_on(w, way):
        here = y if w == 0 else z
        place = (here + (1, 3)[way]) % 4
        part = parts[w]
        part_copy(w, 0, way).wait_recv()

        def add(i, _):
            a, b = i // 3 + 2 * way, i % 3
            at = (place, a) if w == 0 else (a, place)
            total = part[at[0], at[1], b].astype(F32) + f_hop[w, way, i // 3, b].astype(F32)
            part[at[0], at[1], b] = total.astype(BF)
            return 0

        lax.fori_loop(0, 6, add, 0)
        part_copy(w, 0, 4 + way).start()

    loads = [
        pltpu.make_async_copy(w2_ref, w2in, l_sem.at[0]),
        pltpu.make_async_copy(w1_ref, w1in, l_sem.at[1]),
    ]
    for w, ref in enumerate((tok_ref, cot_ref)):
        for b in range(3):
            loads.append(
                pltpu.make_async_copy(
                    ref.at[:, pl.ds(b * 128, 128)],
                    feats[w].at[3 * t + b],
                    l_sem.at[2 + 3 * w + b],
                )
            )
    for cp in loads:
        cp.start()
    loads[1].wait()

    def scale_one(g, _):
        for k in range(NK):
            w1all[p, g, k] = (w1in[g, k].astype(F32) * scale1(g, k)).astype(BF)
        return 0

    lax.fori_loop(0, NB, scale_one, 0)
    pl.semaphore_wait(barrier, 9)
    for i in range(5):
        weight_copy(0, i).start()
    loads[0].wait()

    def lanes_out(i, _):
        s = tab[OWN_SLOT + i]
        lanes[i // 16, (i // 4) % 4, i % 4] = w2in[s]
        return 0

    lax.fori_loop(0, 32, lanes_out, 0)
    lanes_go(0)
    w1all[:, :, NK] = jnp.zeros((8, NB, 16, 128), BF)
    w2all[:, :, NK] = jnp.zeros((8, NB, 16, 128), BF)
    for cp in loads[2:]:
        cp.wait()

    def weights_on(w):
        weight_copy(w, 0).wait_recv()
        weight_copy(w, 5).start()
        weight_copy(w, 2).wait_recv()
        weight_copy(w, 6).start()
        weight_copy(w, 1).wait_recv()
        weight_copy(w, 7).start()
        weight_copy(w, 3).wait_recv()
        weight_copy(w, 8).start()

    def weights_last(w):
        weight_copy(w, 5).wait_recv()
        weight_copy(w, 6).wait_recv()
        weight_copy(w, 9).start()

    lanes_turn(0, 0)
    lanes_turn(0, 1)
    for group in (0, 1):
        for w in range(2):
            for i in range(2):
                feature_copy(w, group, i).start()
    weights_on(0)
    lanes_end(0)

    def scale_two(g, _):
        i = tab[HOME_LANE + g]
        for k in range(NK):
            w2all[p, g, k] = (rbuf[i // 16, (i // 4) % 4, i % 4, k].astype(F32) * scale2(g, k)).astype(BF)
        return 0

    lax.fori_loop(0, NB, scale_two, 0)
    for i in range(5):
        weight_copy(1, i).start()

    def feature_on(w, group):
        for i in range(2):
            feature_copy(w, group, i).wait_recv()
            feature_copy(w, group, i + 2).start()
            if group == 0:
                for k in range(2):
                    feature_copy(w, (2, 4)[i], k).start()

    for w in range(2):
        feature_on(w, 0)
    for w in range(2):
        feature_on(w, 1)
    weights_last(0)
    for w in range(2):
        for i in (2, 3):
            feature_copy(w, 0, i).wait_recv()
        for k in range(2):
            feature_copy(w, 3, k).start()
    for group in (2, 4):
        for w in range(2):
            feature_on(w, group)
    weights_on(1)
    for w in range(2):
        feature_on(w, 3)
    for group in range(1, 5):
        for w in range(2):
            for i in (2, 3):
                feature_copy(w, group, i).wait_recv()
    for i in (4, 7, 8, 9):
        weight_copy(0, i).wait_recv()

    def project(g, _):
        w1c = jnp.concatenate([w1all[:, g, k].reshape(128, 128) for k in range(NK)], axis=0)
        xs = jnp.concatenate([xall[row(g, k)] for k in range(NK)], axis=1)
        pre = jnp.dot(xs, w1c, preferred_element_type=F32)
        th = jnp.tanh(GELU_C * (pre + GELU_A * pre * pre * pre))
        act = (0.5 * pre * (1.0 + th)).astype(BF)
        slope[g] = 0.5 * (1.0 + th) + 0.5 * pre * (1.0 - th * th) * GELU_C * (
            1.0 + 3.0 * GELU_A * pre * pre
        )
        act_all[:, pl.ds(pl.multiple_of(g * 128, 128), 128)] = act
        dys = jnp.concatenate([dyall[col(g, k)] for k in range(NK)], axis=1)
        gw2 = jnp.dot(act.T, dys, preferred_element_type=F32).astype(BF)
        for k in range(NK):
            g2s[:, :, g, k] = gw2[:, k * 128 : (k + 1) * 128].reshape(4, 2, 16, 128)
        return 0

    def flip(j, _):
        xt[j] = xall[j].T
        return 0

    lax.fori_loop(0, HALF, project, 0)
    grad_copy(0, 6).start()
    weights_last(1)
    lax.fori_loop(HALF, NB, project, 0)
    grad_copy(0, 7).start()
    lax.fori_loop(0, 48, flip, 0)

    def pair_sum(w, chunk, h):
        own = grads[w]

        def body(g, _):
            own[chunk, c, g] = (own[chunk, c, g].astype(F32) + sib[chunk, g].astype(F32)).astype(BF)
            return 0

        lax.fori_loop(h * HALF, (h + 1) * HALF, body, 0)

    def pair_stage(w):
        grad_copy(w, 6).wait_recv()
        pair_sum(w, xo, 0)
        grad_copy(w, 0).start()
        pair_sum(w, xl, 0)
        grad_copy(w, 3).start()
        grad_copy(w, 7).wait_recv()
        pair_sum(w, xo, 1)
        grad_copy(w, 1).start()
        pair_sum(w, xr, 1)
        grad_copy(w, 2).start()
        pair_sum(w, xr, 0)
        pair_sum(w, xl, 1)
        pair_sum(w, x, 0)
        pair_sum(w, x, 1)

    def pass_stage(w):
        own = grads[w]
        grad_copy(w, 0).wait_recv()

        def right(g, _):
            own[xr, c, g] = (own[xr, c, g].astype(F32) + fwd[w, 0, g].astype(F32)).astype(BF)
            return 0

        lax.fori_loop(0, HALF, right, 0)
        grad_copy(w, 4).start()
        grad_copy(w, 1).wait_recv()

        def left(g, _):
            own[xl, c, g + HALF] = (
                own[xl, c, g + HALF].astype(F32) + fwd[w, 1, g].astype(F32)
            ).astype(BF)
            return 0

        lax.fori_loop(0, HALF, left, 0)
        grad_copy(w, 5).start()

    def last_stage(w, out, scale):
        own = grads[w]
        for i in (2, 3, 4, 5):
            grad_copy(w, i).wait_recv()

        def body(g, _):
            for k in range(NK):
                total = own[x, c, g, k].astype(F32) + fin[w, 0, g, k].astype(F32)
                total = total + fin[w, 1, g, k].astype(F32)
                out(g, k, (total * scale(g, k)).astype(BF))
            return 0

        lax.fori_loop(0, NB, body, 0)

    def mix(to_y):
        def body(i, _):
            j = 12 * to_y + 2 * i
            panel = jnp.concatenate(
                [
                    jnp.concatenate(
                        [w2all[:, g, kv_ref[NB + g, j + b]].reshape(128, 128) for g in range(NB)], axis=0
                    )
                    for b in range(2)
                ],
                axis=1,
            )
            res = jnp.dot(act_all[...], panel, preferred_element_type=F32).astype(BF)
            for b in range(2):
                at = 2 * i + b
                m_part[to_y, at // 3, at % 3] = res[:, b * 128 : (b + 1) * 128]
            return 0

        lax.fori_loop(0, 6, body, 0)

    def back(to_z):
        def body(i, _):
            at = (2 * i, 2 * i + 1)
            panel = jnp.concatenate(
                [
                    jnp.concatenate(
                        [
                            w1all[:, g, kv_ref[g, 12 * (a // 3) + 3 * to_z + a % 3]].reshape(128, 128)
                            for g in range(NB)
                        ],
                        axis=1,
                    )
                    for a in at
                ],
                axis=0,
            )
            res = lax.dot_general(dpre_all[...], panel, nt, preferred_element_type=F32).astype(BF)
            for b, a in enumerate(at):
                d_part[a // 3, to_z, a % 3] = res[:, b * 128 : (b + 1) * 128]
            return 0

        lax.fori_loop(0, 6, body, 0)

    for i in (4, 7, 8, 9):
        weight_copy(1, i).wait_recv()
    pair_stage(0)
    pl.semaphore_signal(free_sem, inc=1, device_id=(sp, t), device_id_type=MESH)
    mix((y + 2) % 4)
    part_copy(0, 0, 0).start()
    part_copy(0, 0, 1).start()
    def hidden(g, _):
        w2c = jnp.concatenate([w2all[:, g, k].reshape(128, 128) for k in range(NK)], axis=1)
        dys = jnp.concatenate([dyall[col(g, k)] for k in range(NK)], axis=1)
        dact = lax.dot_general(dys, w2c, nt, preferred_element_type=F32).astype(BF)
        dpre = (dact.astype(F32) * slope[g]).astype(BF)
        dpre_all[:, pl.ds(pl.multiple_of(g * 128, 128), 128)] = dpre
        return 0

    def grad_one(g, _):
        dpre = dpre_all[:, pl.ds(pl.multiple_of(g * 128, 128), 128)]
        for k in range(NK):
            gw1 = jnp.dot(xt[row(g, k)], dpre, preferred_element_type=F32).astype(BF)
            g1s[:, :, g, k] = gw1.reshape(4, 2, 16, 128)
        return 0

    def keep_two(g, k, value):
        g2s[x, c, g, k] = value

    def lanes_back(i, _):
        s = tab[HOME_LOCAL + i]
        lanes[i // 16, (i // 4) % 4, i % 4] = g2s[x, c, s]
        return 0

    def mix_go(way):
        mix((y + (1, 3)[way]) % 4)
        part_copy(0, 0, 2 + way).start()
        part_on(0, way)

    def back_go(way):
        back((z + (1, 3)[way]) % 4)
        part_copy(1, 0, 2 + way).start()
        part_on(1, way)

    def part_turn(w):
        for d in range(2, 6):
            part_copy(w, 0, d).wait_recv()
        part = parts[w]

        def add_four(i, _):
            a, b = i // 3, i % 3
            here = (y, a) if w == 0 else (a, z)
            total = part[here[0], here[1], b].astype(F32)
            for d in range(2):
                total = total + f_buf[w, d, a, b].astype(F32)
            part[here[0], here[1], b] = total.astype(BF)
            return 0

        lax.fori_loop(0, 12, add_four, 0)
        for d in range(1, 4):
            part_copy(w, 1, d).start()
    lax.fori_loop(0, NB, hidden, 0)
    back((z + 2) % 4)
    part_copy(1, 0, 0).start()
    part_copy(1, 0, 1).start()
    mix_go(0)
    lax.fori_loop(0, HALF, grad_one, 0)
    pl.semaphore_wait(free_sem, 1)
    grad_copy(1, 6).start()
    pass_stage(0)
    mix_go(1)
    back_go(0)
    lax.fori_loop(HALF, NB, grad_one, 0)
    grad_copy(1, 7).start()
    last_stage(0, keep_two, scale2)
    lanes_sent(0)
    lax.fori_loop(0, 32, lanes_back, 0)
    lanes_go(1)
    back_go(1)
    pair_stage(1)
    mix(y)
    part_turn(0)
    back(z)
    lanes_turn(1, 0)
    part_turn(1)
    lanes_turn(1, 1)
    pass_stage(1)
    for w, out in ((0, mixed), (1, dxo)):
        for d in range(1, 4):
            part_copy(w, 1, d).wait_recv()
        for b in range(3):
            total = parts[w][y, z, b].astype(F32)
            for d in range(3):
                total = total + f_fin[w, d, b].astype(F32)
            out[:, b * 128 : (b + 1) * 128] = total.astype(BF)
    lanes_end(1)

    def slot_out(s, _):
        i = tab[SLOT_LANE + s]
        got = rback[i // 16, (i // 4) % 4, i % 4]
        o2[s] = jnp.where(s < tab[SLOTS_HERE], got, jnp.zeros_like(got))
        return 0

    lax.fori_loop(0, CAP, slot_out, 0)

    def keep_one(g, k, value):
        o1[g, k] = value

    last_stage(1, keep_one, scale1)
    lanes_sent(1)
    for w in range(2):
        for i in range(10):
            weight_copy(w, i).wait_send()
        for group in range(5):
            for i in range(4):
                feature_copy(w, group, i).wait_send()
        for i in range(8):
            grad_copy(w, i).wait_send()
        for d in range(6):
            part_copy(w, 0, d).wait_send()
        for d in range(1, 4):
            part_copy(w, 1, d).wait_send()


OWN_SLOT, HOME_LOCAL, HOME_LANE, HOME_Q, SLOT_LANE, SLOTS_HERE, SPARE = 0, 32, 64, 80, 96, 120, 128


def table_kernel(owner, rows, cols, tab, kv, count, pairs):
    t = lax.axis_index("tensor")
    for i in range(16):
        count[i] = 0
    for i in range(32):
        tab[OWN_SLOT + i] = 0
        tab[HOME_LOCAL + i] = 0
    for s in range(CAP):
        tab[SLOT_LANE + s] = 0

    def source(src, _):
        seen = []
        for i in range(16):
            pairs[i] = 0
        for i in range(NB):
            o = owner[src * NB + i]
            slot, pair = count[o], pairs[o]
            count[o] = slot + 1
            pairs[o] = pair + 1
            here = o == t
            tab[jnp.where(here, OWN_SLOT + pair * 16 + src, SPARE)] = slot
            tab[jnp.where(here, SLOT_LANE + slot, SPARE + 1)] = pair * 16 + src

            seen.append((o, slot, pair))

        @pl.when(src == t)
        def _():
            for i, (o, slot, pair) in enumerate(seen):
                tab[HOME_LANE + i] = pair * 16 + o
                tab[HOME_Q + i] = o * CAP + slot
                tab[HOME_LOCAL + pair * 16 + o] = i

        return 0

    lax.fori_loop(0, 16, source, 0)
    tab[SLOTS_HERE] = count[t]

    def inverse(g, _):
        for j in range(48):
            kv[g, j] = NK
            kv[NB + g, j] = NK
        q = tab[HOME_Q + g]
        for k in range(NK):
            kv[g, rows[k, t * NB + g]] = k
            kv[NB + g, cols[k, q]] = k
        return 0

    lax.fori_loop(0, NB, inverse, 0)


def hand_over(*refs):
    src, dst, kept, sem = refs[:4], refs[4:8], refs[8:12], refs[12]
    loads = [pltpu.make_async_copy(src[i], kept[i], sem.at[0, i]) for i in range(4)]
    stores = [pltpu.make_async_copy(kept[i], dst[i], sem.at[1, i]) for i in range(4)]
    for i in (3, 2, 0, 1):
        loads[i].start()
    for i in (3, 2, 0, 1):
        loads[i].wait()
        stores[i].start()
    for cp in stores:
        cp.wait()


VM = pl.BlockSpec(memory_space=pltpu.VMEM)
SM = pl.BlockSpec(memory_space=pltpu.SMEM)
ANY = pl.BlockSpec(memory_space=pl.ANY)
SHARD = (NB, NK, 16, 128)
LANES = (2, 4, 4, NK, 16, 128)


def local(tokens, cotangent, w1_blocks, w1_rows, w1_scale, w2_blocks, w2_cols, w2_scale, owner):
    dma = pltpu.SemaphoreType.DMA
    part = (4, 4, 3, 192, 128)
    outs = [
        jax.ShapeDtypeStruct((192, 384), BF),
        jax.ShapeDtypeStruct((192, 384), BF),
        jax.ShapeDtypeStruct(SHARD, BF),
        jax.ShapeDtypeStruct((CAP, NK, 16, 128), BF),
    ]
    tab, kv = pl.pallas_call(
        table_kernel,
        out_shape=[
            jax.ShapeDtypeStruct((256,), jnp.int32),
            jax.ShapeDtypeStruct((2 * NB, 48), jnp.int32),
        ],
        in_specs=[SM] * 3,
        out_specs=[SM] * 2,
        scratch_shapes=[pltpu.SMEM((16,), jnp.int32), pltpu.SMEM((16,), jnp.int32)],
    )(owner, w1_rows.T, w2_cols.T)
    results = pl.pallas_call(
        layer_kernel,
        out_shape=outs,
        in_specs=[ANY] * 4 + [SM] * 6,
        out_specs=[VM] * 4,
        scratch_shapes=[
            pltpu.VMEM(SHARD, BF),
            pltpu.VMEM((CAP, NK, 16, 128), BF),
            pltpu.VMEM((48, 192, 128), BF),
            pltpu.VMEM((48, 192, 128), BF),
            pltpu.VMEM((8, NB, NK + 1, 16, 128), BF),
            pltpu.VMEM((8, NB, NK + 1, 16, 128), BF),
            pltpu.VMEM(LANES, BF),
            pltpu.VMEM(LANES, BF),
            pltpu.VMEM(LANES, BF),
            pltpu.VMEM((2,) + LANES, BF),
            pltpu.VMEM((48, 128, 192), BF),
            pltpu.VMEM((NB, 192, 128), F32),
            pltpu.VMEM((192, NB * 128), BF),
            pltpu.VMEM((192, NB * 128), BF),
            pltpu.VMEM((4, 2) + SHARD, BF),
            pltpu.VMEM((4, 2) + SHARD, BF),
            pltpu.VMEM((4,) + SHARD, BF),
            pltpu.VMEM((2, 2, HALF, NK, 16, 128), BF),
            pltpu.VMEM((2, 2) + SHARD, BF),
            pltpu.VMEM(part, BF),
            pltpu.VMEM(part, BF),
            pltpu.VMEM((2, 2, 4, 3, 192, 128), BF),
            pltpu.VMEM((2, 2, 2, 3, 192, 128), BF),
            pltpu.VMEM((2, 3, 3, 192, 128), BF),
            dma((2, 2, 2, 4, 2)),
            dma((2, 2, 2, 4, 2)),
            dma((2, 10)),
            dma((2, 10)),
            dma((2, 5, 4)),
            dma((2, 5, 4)),
            dma((2, 8)),
            dma((2, 8)),
            dma((2, 2, 6)),
            dma((2, 2, 6)),
            dma((8,)),
            pltpu.SemaphoreType.REGULAR,
        ],
        compiler_params=pltpu.CompilerParams(
            collective_id=0, has_side_effects=True, vmem_limit_bytes=(64 << 20) - (64 << 10)
        ),
    )(
        tokens,
        cotangent,
        w1_blocks,
        w2_blocks,
        w1_scale.T,
        w2_scale.T,
        w1_rows.T,
        w2_cols.T,
        tab,
        kv,
    )
    return pl.pallas_call(
        hand_over,
        out_shape=outs,
        in_specs=[ANY] * 4,
        out_specs=[ANY] * 4,
        scratch_shapes=[pltpu.VMEM(o.shape, BF) for o in outs] + [dma((2, 4))],
    )(*results)


def solution(mesh):
    in_specs = (
        P("dp", "tensor"),
        P("dp", "tensor"),
        P("tensor", None, "dp", None),
        P(),
        P(),
        P("tensor", None, "dp", None),
        P(),
        P(),
        P(),
    )
    out_specs = (
        P("dp", "tensor"),
        P("dp", "tensor"),
        P("tensor", None, "dp", None),
        P("tensor", None, "dp", None),
    )
    return jax.shard_map(local, mesh=mesh, in_specs=in_specs, out_specs=out_specs, check_vma=False)
```
